32 devices in a mesh: row: 4 (over x, core), col: 2 (over y), basis: 4 (over z).
Axes of the slice: x: 2, y: 2, z: 4, core: 2. Of those that a mesh axis runs over, the one named last changes fastest.
Arguments:
- block_data: bfloat16 [256, 128, 128], P(('row', 'col', 'basis')), may hold values from -1.1953125 to 1.1953125
- item_pairs: int32 [256, 2], P(('row', 'col', 'basis')), may hold values from 0 to 1023
- dest_slot: int32 [256], P(('row', 'col', 'basis')), may hold values from 0 to 7, as said below
- brick_tag: int32 [256], P(('row', 'col', 'basis')), may hold values from 0 to 7
- centres: float32 [1024, 3, 128], replicated, may hold values from -1.5 to 1.5
- exponents: float32 [1024, 128], replicated, may hold values from 4 to 12
- levels: int32 [64], replicated, may hold values 0 or 1
- cell_pos: int32 [64, 256], P(('row', 'col', 'basis')), may hold values from 0 to 4095, as said below
- corner_refs: int32 [64, 256, 8], P(('row', 'col', 'basis')), may hold values from 0 to 511, as said below
Outputs:
- density: float32 [64, 4096], P(('row', 'col', 'basis'))
The draws below stay inside these ranges and needn't reach their ends.
Inputs may be any that keep to these rules, and one draw needn't show every extreme that they name: `dest_slot`: on the rows of one device the values are distinct; value v sends the row to brick group v. `cell_pos`: within one brick the cells are distinct, one in each run of 16 consecutive points. `corner_refs`: index v names corner v % 8 of brick v // 8; every index occurs 256 times.
All inputs are finite; a program needn't handle non-finite values.
Results may differ from the reference program's by a relative error of at most 0.0028.
Values sent between devices are 32-bit elements; how exact they have to be, the bound alone decides.
No kernel may reach another device: no remote copies, remote signals or barrier semaphores. Data moves between devices by JAX's collectives and lax.ppermute only.
A program may use at most 64 MiB of HBM per device.

```python
import math
import jax
import jax.numpy as jnp
from jax import lax

BS = 128
EDGE = 16
TC = 256
NBLK = 1024
ITEMS_DEV = 8
PTS = 4096
GROUPS = 8
CAP = 1
BRK_GRP = 8
BRICKS = 64
ITEMS = 256


def draw_dest_slot(key, part):
    device_total = ITEMS // ITEMS_DEV
    if ITEMS_DEV == GROUPS * CAP:

        def full_slots(index):
            return jax.random.permutation(jax.random.fold_in(key, index), GROUPS * CAP)
        slot_rows = jax.vmap(full_slots)(jnp.arange(device_total))
        return slot_rows.reshape(-1).astype(jnp.int32)
    popular_count = max(1, ITEMS_DEV // 2)
    band_width = max(1, device_total // 2)

    def pick_slots(index):
        band_index = index // band_width
        ranking = jax.random.permutation(jax.random.fold_in(key, 1000003 + band_index), GROUPS)
        popular = jnp.zeros((GROUPS,), jnp.int32).at[ranking[:popular_count]].set(1)
        jitter_draw = jax.random.randint(jax.random.fold_in(key, index), (GROUPS,), 0, 2 ** 14)
        own_group = (jnp.arange(GROUPS) == index % GROUPS).astype(jnp.int32)
        scores = own_group * 2 ** 26 + popular * 2 ** 22 + jitter_draw * GROUPS + jnp.arange(GROUPS)
        chosen = lax.top_k(scores, ITEMS_DEV)[1]
        shuffle = jax.random.permutation(jax.random.fold_in(key, 2000003 + index), ITEMS_DEV)
        return chosen[shuffle] * CAP
    slot_rows = jax.vmap(pick_slots)(jnp.arange(device_total))
    return slot_rows.reshape(-1).astype(jnp.int32)


def draw_cell_pos(key, part):
    stride_len = PTS // TC
    jitter_draw = jax.random.randint(key, (BRICKS, TC), 0, stride_len)
    jitter_draw = jitter_draw.at[0, 0].set(0).at[0, TC - 1].set(stride_len - 1)
    return (jnp.arange(TC)[None, :] * stride_len + jitter_draw).astype(jnp.int32)


def draw_corner_refs(key, part):
    mixed = jax.random.permutation(key, BRICKS * TC * 8)
    return (mixed % (BRICKS * 8)).reshape(BRICKS, TC, 8).astype(jnp.int32)


def plant(entries, key, low, top_value):
    place = [jax.random.randint(jax.random.fold_in(key, axis), (), 0, length) for axis, length in enumerate(entries.shape)]
    main_axis = entries.shape.index(max(entries.shape))
    beside = place[:main_axis] + [(place[main_axis] + 1) % entries.shape[main_axis]] + place[main_axis + 1:]
    return entries.at[tuple(place)].set(low).at[tuple(beside)].set(top_value)


def block_levels(own_key, dims, split, smallest, largest):
    def one(axis_at, blocks):
        heights = jax.random.uniform(jax.random.fold_in(jax.random.fold_in(own_key, 6), axis_at), (blocks,), jnp.float32, smallest / len(split), largest / len(split))
        return jnp.repeat(jnp.exp(heights), dims[axis_at] // blocks).reshape((-1,) + (1,) * (len(dims) - axis_at - 1))

    gain = one(*split[0])
    for cut in split[1:]:
        gain = gain * one(*cut)
    return gain


def scatter_about(key, shape, spread, limit, shards=(), kind=jnp.bfloat16):
    array = spread * jax.random.normal(key, shape, jnp.float32)
    if shards:
        array = array * block_levels(key, shape, shards, -0.22, 0.18)
    return jnp.clip(array, -limit, limit).astype(kind)


def setup_inputs(seed: int = 0) -> dict:
    arg_keys = jax.random.split(jax.random.key(seed), 10)
    block_data = scatter_about(arg_keys[0], (ITEMS, BS, BS), 0.2, 1.1953125, ((0, 32),))
    item_pairs = plant(jax.random.randint(arg_keys[1], (ITEMS, 2), 0, NBLK), jax.random.fold_in(arg_keys[1], 1), 0, NBLK - 1).astype(jnp.int32)
    dest_slot = draw_dest_slot(jax.random.fold_in(arg_keys[9], 71), 0)
    brick_tag = plant(jax.random.randint(arg_keys[3], (ITEMS,), 0, BRK_GRP), jax.random.fold_in(arg_keys[3], 1), 0, BRK_GRP - 1).astype(jnp.int32)
    centres = jnp.clip(jax.random.uniform(arg_keys[4], (NBLK, 3, BS), jnp.float32, -1.5, 1.5), -1.5, 1.5)
    exponents = jnp.clip(jnp.exp(jax.random.uniform(arg_keys[5], (NBLK, BS), jnp.float32, math.log(4.0), math.log(12.0))), 4.0, 12.0)
    levels = plant((jax.random.randint(arg_keys[6], (BRICKS,), 0, 4) < 3).astype(jnp.int32), jax.random.fold_in(arg_keys[6], 1), 0, 1)
    cell_pos = draw_cell_pos(jax.random.fold_in(arg_keys[9], 71), 0)
    corner_refs = draw_corner_refs(jax.random.fold_in(arg_keys[9], 71), 0)
    return {"block_data": block_data, "item_pairs": item_pairs, "dest_slot": dest_slot, "brick_tag": brick_tag, "centres": centres, "exponents": exponents, "levels": levels, "cell_pos": cell_pos, "corner_refs": corner_refs}


coarse_spacing = 0.2


def basis_values(centres, exponents, block_index, level_value, edge_points):
    spacing = coarse_spacing * jnp.exp2(-level_value.astype(jnp.float32))
    coords = (jnp.arange(edge_points, dtype=jnp.float32) - (edge_points - 1) / 2.0) * spacing
    middle = centres[block_index]
    decay_rates = exponents[block_index]
    factor = jnp.exp(-decay_rates[None, :, None] * (coords[None, None, :] - middle[:, :, None]) ** 2)
    values_grid = factor[0][:, :, None, None] * factor[1][:, None, :, None] * factor[2][:, None, None, :]
    return values_grid.reshape(decay_rates.shape[0], edge_points * edge_points * edge_points)


def pair_density(block_values, pair_index, level_value, centres, exponents, edge_points):
    row_values = basis_values(centres, exponents, pair_index[0], level_value, edge_points)
    col_values = basis_values(centres, exponents, pair_index[1], level_value, edge_points).astype(jnp.bfloat16)
    product = jnp.dot(block_values, col_values, preferred_element_type=jnp.float32)
    return jnp.sum(row_values * product, axis=0)


def corner_points(edge_points):
    corner_code = jnp.arange(8, dtype=jnp.int32)
    first = (corner_code // 4) * (edge_points - 1)
    second = ((corner_code // 2) % 2) * (edge_points - 1)
    third = (corner_code % 2) * (edge_points - 1)
    return ((first * edge_points + second) * edge_points + third).astype(jnp.int32)


def reference(block_data, item_pairs, dest_slot, brick_tag, centres, exponents, levels, cell_pos, corner_refs):
    target = ((dest_slot // CAP) * BRK_GRP + brick_tag).astype(jnp.int32)
    item_level = levels[target]

    def single(operands):
        return pair_density(operands[0], operands[1], operands[2], centres, exponents, EDGE)

    densities = lax.map(single, (block_data, item_pairs, item_level))
    brick_density = jax.ops.segment_sum(densities, target, num_segments=BRICKS)
    corner_values = brick_density[:, corner_points(EDGE)].reshape(-1)
    corner_mean = jnp.mean(corner_values[corner_refs], axis=-1)
    current = jnp.take_along_axis(brick_density, cell_pos, axis=1)
    brick_rows = jnp.arange(BRICKS, dtype=jnp.int32)[:, None]
    return brick_density.at[brick_rows, cell_pos].set(0.5 * current + 0.5 * corner_mean)
```

```python
import functools

import jax
import jax.numpy as jnp
from jax import lax
from jax.experimental import pallas as pl
from jax.experimental.pallas import tpu as pltpu
from jax.sharding import PartitionSpec as P

EDGE = 16
FACE = EDGE * EDGE
LANES = 128
ROWS = EDGE * FACE // LANES
COARSE = 0.2
META = 8
SLOT_ROWS = ROWS + META


def lane_pick(values, index):
    return jnp.take_along_axis(values, index, axis=1, mode="promise_in_bounds")


def iota(shape, axis):
    return lax.broadcasted_iota(jnp.int32, shape, axis)


def axis_factors(coords, middle, decay):
    return jnp.exp(-decay * (coords - middle) ** 2)


def pair_kernel(
    slot_depth,
    bricks_group,
    pairs_ref,
    dest_ref,
    tag_ref,
    levels_ref,
    blocks_ref,
    centres_ref,
    exponents_ref,
    out_ref,
    centre_buf,
    decay_buf,
    corner_buf,
    sems,
):
    items = blocks_ref.shape[0]
    slots = out_ref.shape[0]

    def copies(k, side):
        block = pairs_ref[side, k]
        at = 2 * k + side
        return (
            pltpu.make_async_copy(
                centres_ref.at[:, pl.ds(block, 1), :], centre_buf.at[at], sems.at[0, at]
            ),
            pltpu.make_async_copy(
                exponents_ref.at[pl.ds(block, 1), :], decay_buf.at[at], sems.at[1, at]
            ),
        )

    for k in range(items):
        for side in range(2):
            for copy in copies(k, side):
                copy.start()
    if slots != items:
        out_ref[...] = jnp.zeros_like(out_ref)
    steps = iota((EDGE, LANES), 0).astype(jnp.float32) - (EDGE - 1) / 2.0

    @pl.loop(0, items)
    def _(k):
        for side in range(2):
            for copy in copies(k, side):
                copy.wait()
        slot = dest_ref[k]
        target = slot // slot_depth * bricks_group + tag_ref[k]
        spacing = jnp.where(levels_ref[target] == 1, COARSE * 0.5, COARSE)
        coords = steps * spacing

        def factors(side):
            at = 2 * k + side
            decay = decay_buf[at]
            found = [axis_factors(coords, centre_buf[at, d], decay) for d in range(3)]
            face = jnp.concatenate(
                [found[1][y : y + 1, :] * found[2] for y in range(EDGE)], axis=0
            )
            return found[0], face

        row_x, row_face = factors(0)
        col_x, col_face = factors(1)
        row_x = row_x.T
        row_face = row_face.T
        block = blocks_ref[k]
        for x in range(EDGE):
            col = (col_x[x : x + 1, :] * col_face).astype(jnp.bfloat16)
            product = lax.dot_general(
                block, col, (((1,), (1,)), ((), ())), preferred_element_type=jnp.float32
            )
            dens = jnp.sum(row_x[:, x : x + 1] * row_face * product, axis=0, keepdims=True)
            for half in range(FACE // LANES):
                piece = dens[:, half * LANES : (half + 1) * LANES]
                out_ref[slot, pl.ds(2 * x + half, 1), :] = piece
                if x in (0, EDGE - 1):
                    corner_buf[2 * (x // (EDGE - 1)) + half, pl.ds(k, 1), :] = piece

    shape = (items, LANES)
    lane = iota(shape, 1)
    place = lane % 4
    low = jnp.where(place % 2 == 1, EDGE - 1, 0)
    high = (FACE - EDGE) % LANES + low
    source = jnp.where(place >= 2, high, low)
    found = [lane_pick(corner_buf[n], source) for n in range(4)]
    corner = lane % 8
    first = jnp.where(corner % 4 >= 2, found[1], found[0])
    last = jnp.where(corner % 4 >= 2, found[3], found[2])
    values = jnp.where(corner >= 4, last, first)
    row = iota(shape, 0)
    brick = jnp.zeros(shape, jnp.int32)
    for k in range(items):
        target = dest_ref[k] // slot_depth * bricks_group + tag_ref[k]
        brick = jnp.where(row == k, target, brick)
    meta = jnp.where(lane < 8, values, brick.astype(jnp.float32))
    if slots != items:

        @pl.loop(0, slots)
        def _(s):
            out_ref[s, ROWS:, :] = jnp.where(lane >= LANES - 8, -1.0, meta)

    for k in range(items):
        tag = tag_ref[k].astype(jnp.float32)
        out_ref[dest_ref[k], ROWS:, :] = jnp.where(lane >= LANES - 8, tag, meta)


def group_kernel(bricks_dev, in_ref, out_ref):
    slots = in_ref.shape[0]
    owners = out_ref.shape[0]
    table_rows = out_ref.shape[1] - bricks_dev * ROWS

    out_ref[...] = jnp.zeros_like(out_ref)
    shape = (META, LANES)
    lane = iota(shape, 1)
    index_tag = jnp.full(shape, LANES - 1, jnp.int32)

    def one(s):
        meta = in_ref[s, ROWS:, :]
        tag = jnp.tile(lane_pick(meta, index_tag), (ROWS // META, 1))
        dens = in_ref[s, :ROWS, :]
        for owner in range(owners):
            for b in range(bricks_dev):
                hit = tag == float(owner * bricks_dev + b)
                out_ref[owner, b * ROWS : (b + 1) * ROWS, :] += jnp.where(hit, dens, 0.0)
        values = lane_pick(meta, lane % 8)
        brick = lane_pick(meta, jnp.full(shape, 8, jnp.int32)).astype(jnp.int32)
        values = jnp.where(brick % 16 == lane // 8, values, 0.0)
        line = brick // 16
        for r in range(table_rows):
            part = jnp.sum(jnp.where(line == r, values, 0.0), axis=0, keepdims=True)
            out_ref[0, bricks_dev * ROWS + r : bricks_dev * ROWS + r + 1, :] += part

    if slots <= 8:
        for s in range(slots):
            one(s)
    else:
        pl.loop(0, slots)(one)
    for owner in range(1, owners):
        out_ref[owner, bricks_dev * ROWS :, :] = out_ref[0, bricks_dev * ROWS :, :]


def cell_kernel(in_ref, cells_ref, refs_ref, out_ref):
    owners = in_ref.shape[0]
    bricks_dev, cells = cells_ref.shape
    table_rows = in_ref.shape[1] - bricks_dev * ROWS

    total = in_ref[0]
    for z in range(1, owners):
        total = total + in_ref[z]
    table = total[bricks_dev * ROWS :]
    chunk = (8, LANES)
    refs = [
        [refs_ref[b, :, c * LANES : (c + 1) * LANES] for c in range(cells // LANES)]
        for b in range(bricks_dev)
    ]
    picked = [[jnp.zeros(chunk, jnp.float32) for _ in row] for row in refs]
    for r in range(table_rows):
        line = jnp.broadcast_to(table[r : r + 1, :], chunk)
        for b in range(bricks_dev):
            for c, index in enumerate(refs[b]):
                found = lane_pick(line, index % LANES)
                picked[b][c] = jnp.where(index // LANES == r, found, picked[b][c])
    for b in range(bricks_dev):
        mean = jnp.concatenate(
            [jnp.sum(p, axis=0, keepdims=True) for p in picked[b]], axis=1
        ) * (0.5 / 8.0)
        position = cells_ref[b : b + 1, :]
        high = (position // LANES == iota((ROWS, cells), 0)).astype(jnp.float32)
        here = position % LANES == iota((LANES, cells), 0)

        def spread(values):
            return lax.dot_general(
                high,
                values,
                (((1,), (1,)), ((), ())),
                precision=lax.Precision.HIGHEST,
                preferred_element_type=jnp.float32,
            )

        hit = spread(here.astype(jnp.float32))
        new = spread(jnp.where(here, mean, 0.0))
        own = total[b * ROWS : (b + 1) * ROWS]
        result = jnp.where(hit > 0.5, 0.5 * own + new, own)
        for row in range(ROWS):
            out_ref[b : b + 1, row * LANES : (row + 1) * LANES] = result[row : row + 1, :]


def vmem():
    return pl.BlockSpec(memory_space=pltpu.VMEM)


def smem():
    return pl.BlockSpec(memory_space=pltpu.SMEM)


def body(
    block_data, item_pairs, dest_slot, brick_tag, centres, exponents, levels, cell_pos, corner_refs
):
    groups = lax.axis_size("row") * lax.axis_size("col")
    owners = lax.axis_size("basis")
    items = block_data.shape[0]
    slot_depth = max(1, items // groups)
    slots = groups * slot_depth
    bricks = levels.shape[0]
    bricks_group = bricks // groups
    bricks_dev = bricks_group // owners
    table_rows = -(-bricks * 8 // (8 * LANES)) * 8
    basis = block_data.shape[1]
    params = pltpu.CompilerParams(vmem_limit_bytes=32 * 1024 * 1024)

    outgoing = pl.pallas_call(
        functools.partial(pair_kernel, slot_depth, bricks_group),
        out_shape=jax.ShapeDtypeStruct((slots, SLOT_ROWS, LANES), jnp.float32),
        in_specs=[smem()] * 4 + [vmem()] + [pl.BlockSpec(memory_space=pl.ANY)] * 2,
        out_specs=vmem(),
        scratch_shapes=[
            pltpu.VMEM((2 * items, 3, 1, basis), jnp.float32),
            pltpu.VMEM((2 * items, 1, basis), jnp.float32),
            pltpu.VMEM((4, items, LANES), jnp.float32),
            pltpu.SemaphoreType.DMA((2, 2 * items)),
        ],
        compiler_params=params,
        name="pair_density",
    )(
        item_pairs.T,
        dest_slot,
        brick_tag,
        levels,
        block_data,
        jnp.transpose(centres, (1, 0, 2)),
        exponents,
    )
    arrived = lax.all_to_all(outgoing, ("row", "col"), split_axis=0, concat_axis=0, tiled=True)
    partial = pl.pallas_call(
        functools.partial(group_kernel, bricks_dev),
        out_shape=jax.ShapeDtypeStruct((owners, bricks_dev * ROWS + table_rows, LANES), jnp.float32),
        in_specs=[vmem()],
        out_specs=vmem(),
        compiler_params=params,
        name="group_sum",
    )(arrived)
    parts = lax.all_to_all(partial, "basis", split_axis=0, concat_axis=0, tiled=True)
    return pl.pallas_call(
        cell_kernel,
        out_shape=jax.ShapeDtypeStruct((bricks_dev, EDGE * FACE), jnp.float32),
        in_specs=[vmem()] * 3,
        out_specs=vmem(),
        compiler_params=params,
        name="cells",
    )(parts, cell_pos, jnp.transpose(corner_refs, (0, 2, 1)))


def solution(mesh):
    split = ("row", "col", "basis")
    return jax.shard_map(
        body,
        mesh=mesh,
        in_specs=(
            P(split, None, None),
            P(split, None),
            P(split),
            P(split),
            P(),
            P(),
            P(),
            P(split, None),
            P(split, None, None),
        ),
        out_specs=P(split, None),
        check_vma=False,
    )
```

```python
import functools

import jax
import jax.numpy as jnp
from jax import lax
from jax.experimental import pallas as pl
from jax.experimental.pallas import tpu as pltpu
from jax.sharding import PartitionSpec as P

EDGE = 16
FACE = EDGE * EDGE
LANES = 128
ROWS = EDGE * FACE // LANES
COARSE = 0.2
META = 8
SLOT_ROWS = ROWS + META


def lane_pick(values, index):
    return jnp.take_along_axis(values, index, axis=1, mode="promise_in_bounds")


def iota(shape, axis):
    return lax.broadcasted_iota(jnp.int32, shape, axis)


def axis_factors(coords, middle, decay):
    return jnp.exp(-decay * (coords - middle) ** 2)


def pair_kernel(
    slot_depth,
    bricks_group,
    pairs_hbm,
    dest_hbm,
    tag_hbm,
    levels_hbm,
    blocks_hbm,
    centres_ref,
    exponents_ref,
    out_ref,
    pairs_ref,
    dest_ref,
    tag_ref,
    levels_ref,
    blocks_ref,
    centre_buf,
    decay_buf,
    corner_buf,
    sems,
    list_sems,
    block_sems,
):
    items = blocks_ref.shape[0]
    slots = out_ref.shape[0]
    lists = [
        pltpu.make_async_copy(source, target, list_sems.at[n])
        for n, (source, target) in enumerate(
            (
                (pairs_hbm, pairs_ref),
                (dest_hbm, dest_ref),
                (tag_hbm, tag_ref),
                (levels_hbm, levels_ref),
            )
        )
    ]
    for copy in lists:
        copy.start()

    def block_copy(k):
        return pltpu.make_async_copy(blocks_hbm.at[k], blocks_ref.at[k], block_sems.at[k])

    for k in range(items):
        block_copy(k).start()
    lists[0].wait()

    def copies(k, side):
        block = pairs_ref[side, k]
        at = 2 * k + side
        return (
            pltpu.make_async_copy(
                centres_ref.at[:, pl.ds(block, 1), :], centre_buf.at[at], sems.at[0, at]
            ),
            pltpu.make_async_copy(
                exponents_ref.at[pl.ds(block, 1), :], decay_buf.at[at], sems.at[1, at]
            ),
        )

    for k in range(items):
        for side in range(2):
            for copy in copies(k, side):
                copy.start()
    for copy in lists[1:]:
        copy.wait()
    if slots != items:
        out_ref[...] = jnp.zeros_like(out_ref)
    steps = iota((EDGE, LANES), 0).astype(jnp.float32) - (EDGE - 1) / 2.0

    @pl.loop(0, items)
    def _(k):
        for side in range(2):
            for copy in copies(k, side):
                copy.wait()
        slot = dest_ref[k]
        target = slot // slot_depth * bricks_group + tag_ref[k]
        spacing = jnp.where(levels_ref[target] == 1, COARSE * 0.5, COARSE)
        coords = steps * spacing

        def factors(side):
            at = 2 * k + side
            decay = decay_buf[at]
            found = [axis_factors(coords, centre_buf[at, d], decay) for d in range(3)]
            face = jnp.concatenate(
                [found[1][y : y + 1, :] * found[2] for y in range(EDGE)], axis=0
            )
            return found[0], face

        row_x, row_face = factors(0)
        col_x, col_face = factors(1)
        row_x = row_x.T
        row_face = row_face.T
        block_copy(k).wait()
        block = blocks_ref[k]
        for x in range(EDGE):
            col = (col_x[x : x + 1, :] * col_face).astype(jnp.bfloat16)
            product = lax.dot_general(
                block, col, (((1,), (1,)), ((), ())), preferred_element_type=jnp.float32
            )
            dens = jnp.sum(row_x[:, x : x + 1] * row_face * product, axis=0, keepdims=True)
            for half in range(FACE // LANES):
                piece = dens[:, half * LANES : (half + 1) * LANES]
                out_ref[slot, pl.ds(2 * x + half, 1), :] = piece
                if x in (0, EDGE - 1):
                    corner_buf[2 * (x // (EDGE - 1)) + half, pl.ds(k, 1), :] = piece

    shape = (items, LANES)
    lane = iota(shape, 1)
    place = lane % 4
    low = jnp.where(place % 2 == 1, EDGE - 1, 0)
    high = (FACE - EDGE) % LANES + low
    source = jnp.where(place >= 2, high, low)
    found = [lane_pick(corner_buf[n], source) for n in range(4)]
    corner = lane % 8
    first = jnp.where(corner % 4 >= 2, found[1], found[0])
    last = jnp.where(corner % 4 >= 2, found[3], found[2])
    values = jnp.where(corner >= 4, last, first)
    row = iota(shape, 0)
    brick = jnp.zeros(shape, jnp.int32)
    for k in range(items):
        target = dest_ref[k] // slot_depth * bricks_group + tag_ref[k]
        brick = jnp.where(row == k, target, brick)
    meta = jnp.where(lane < 8, values, brick.astype(jnp.float32))
    if slots != items:

        @pl.loop(0, slots)
        def _(s):
            out_ref[s, ROWS:, :] = jnp.where(lane >= LANES - 8, -1.0, meta)

    for k in range(items):
        tag = tag_ref[k].astype(jnp.float32)
        out_ref[dest_ref[k], ROWS:, :] = jnp.where(lane >= LANES - 8, tag, meta)


def group_kernel(bricks_dev, in_ref, out_ref):
    slots = in_ref.shape[0]
    owners = out_ref.shape[0]
    table_rows = out_ref.shape[1] - bricks_dev * ROWS

    out_ref[...] = jnp.zeros_like(out_ref)
    shape = (META, LANES)
    lane = iota(shape, 1)
    index_tag = jnp.full(shape, LANES - 1, jnp.int32)

    def one(s):
        meta = in_ref[s, ROWS:, :]
        tag = jnp.tile(lane_pick(meta, index_tag), (ROWS // META, 1))
        dens = in_ref[s, :ROWS, :]
        for owner in range(owners):
            for b in range(bricks_dev):
                hit = tag == float(owner * bricks_dev + b)
                out_ref[owner, b * ROWS : (b + 1) * ROWS, :] += jnp.where(hit, dens, 0.0)
        values = lane_pick(meta, lane % 8)
        brick = lane_pick(meta, jnp.full(shape, 8, jnp.int32)).astype(jnp.int32)
        values = jnp.where(brick % 16 == lane // 8, values, 0.0)
        line = brick // 16
        for r in range(table_rows):
            part = jnp.sum(jnp.where(line == r, values, 0.0), axis=0, keepdims=True)
            out_ref[0, bricks_dev * ROWS + r : bricks_dev * ROWS + r + 1, :] += part

    if slots <= 8:
        for s in range(slots):
            one(s)
    else:
        pl.loop(0, slots)(one)
    for owner in range(1, owners):
        out_ref[owner, bricks_dev * ROWS :, :] = out_ref[0, bricks_dev * ROWS :, :]


def cell_kernel(in_ref, cells_ref, refs_ref, out_ref):
    owners = in_ref.shape[0]
    bricks_dev, cells = cells_ref.shape
    table_rows = in_ref.shape[1] - bricks_dev * ROWS

    total = in_ref[0]
    for z in range(1, owners):
        total = total + in_ref[z]
    table = total[bricks_dev * ROWS :]
    chunk = (8, LANES)
    refs = [
        [refs_ref[b, :, c * LANES : (c + 1) * LANES] for c in range(cells // LANES)]
        for b in range(bricks_dev)
    ]
    picked = [[jnp.zeros(chunk, jnp.float32) for _ in row] for row in refs]
    for r in range(table_rows):
        line = jnp.broadcast_to(table[r : r + 1, :], chunk)
        for b in range(bricks_dev):
            for c, index in enumerate(refs[b]):
                found = lane_pick(line, index % LANES)
                picked[b][c] = jnp.where(index // LANES == r, found, picked[b][c])
    for b in range(bricks_dev):
        mean = jnp.concatenate(
            [jnp.sum(p, axis=0, keepdims=True) for p in picked[b]], axis=1
        ) * (0.5 / 8.0)
        position = cells_ref[b : b + 1, :]
        high = (position // LANES == iota((ROWS, cells), 0)).astype(jnp.float32)
        here = position % LANES == iota((LANES, cells), 0)

        def spread(values):
            return lax.dot_general(
                high,
                values,
                (((1,), (1,)), ((), ())),
                precision=lax.Precision.HIGHEST,
                preferred_element_type=jnp.float32,
            )

        hit = spread(here.astype(jnp.float32))
        new = spread(jnp.where(here, mean, 0.0))
        own = total[b * ROWS : (b + 1) * ROWS]
        result = jnp.where(hit > 0.5, 0.5 * own + new, own)
        for row in range(ROWS):
            out_ref[b : b + 1, row * LANES : (row + 1) * LANES] = result[row : row + 1, :]


def vmem():
    return pl.BlockSpec(memory_space=pltpu.VMEM)


def body(
    block_data, item_pairs, dest_slot, brick_tag, centres, exponents, levels, cell_pos, corner_refs
):
    groups = lax.axis_size("row") * lax.axis_size("col")
    owners = lax.axis_size("basis")
    items = block_data.shape[0]
    slot_depth = max(1, items // groups)
    slots = groups * slot_depth
    bricks = levels.shape[0]
    bricks_group = bricks // groups
    bricks_dev = bricks_group // owners
    table_rows = -(-bricks * 8 // (8 * LANES)) * 8
    basis = block_data.shape[1]
    params = pltpu.CompilerParams(vmem_limit_bytes=32 * 1024 * 1024)

    outgoing = pl.pallas_call(
        functools.partial(pair_kernel, slot_depth, bricks_group),
        out_shape=jax.ShapeDtypeStruct((slots, SLOT_ROWS, LANES), jnp.float32),
        in_specs=[pl.BlockSpec(memory_space=pltpu.HBM)] * 7,
        out_specs=vmem(),
        scratch_shapes=[
            pltpu.SMEM((2, items), jnp.int32),
            pltpu.SMEM((items,), jnp.int32),
            pltpu.SMEM((items,), jnp.int32),
            pltpu.SMEM((bricks,), jnp.int32),
            pltpu.VMEM(block_data.shape, block_data.dtype),
            pltpu.VMEM((2 * items, 3, 1, basis), jnp.float32),
            pltpu.VMEM((2 * items, 1, basis), jnp.float32),
            pltpu.VMEM((4, items, LANES), jnp.float32),
            pltpu.SemaphoreType.DMA((2, 2 * items)),
            pltpu.SemaphoreType.DMA((4,)),
            pltpu.SemaphoreType.DMA((items,)),
        ],
        compiler_params=params,
        name="pair_density",
    )(
        *(
            pltpu.with_memory_space_constraint(operand, pltpu.HBM)
            for operand in (
                item_pairs.T,
                dest_slot,
                brick_tag,
                levels,
                block_data,
                jnp.transpose(centres, (1, 0, 2)),
                exponents,
            )
        )
    )
    arrived = lax.all_to_all(outgoing, ("row", "col"), split_axis=0, concat_axis=0, tiled=True)
    partial = pl.pallas_call(
        functools.partial(group_kernel, bricks_dev),
        out_shape=jax.ShapeDtypeStruct((owners, bricks_dev * ROWS + table_rows, LANES), jnp.float32),
        in_specs=[vmem()],
        out_specs=vmem(),
        compiler_params=params,
        name="group_sum",
    )(arrived)
    parts = lax.all_to_all(partial, "basis", split_axis=0, concat_axis=0, tiled=True)
    return pl.pallas_call(
        cell_kernel,
        out_shape=jax.ShapeDtypeStruct((bricks_dev, EDGE * FACE), jnp.float32),
        in_specs=[vmem()] * 3,
        out_specs=vmem(),
        compiler_params=params,
        name="cells",
    )(parts, cell_pos, jnp.transpose(corner_refs, (0, 2, 1)))


def solution(mesh):
    split = ("row", "col", "basis")
    return jax.shard_map(
        body,
        mesh=mesh,
        in_specs=(
            P(split, None, None),
            P(split, None),
            P(split),
            P(split),
            P(),
            P(),
            P(),
            P(split, None),
            P(split, None, None),
        ),
        out_specs=P(split, None),
        check_vma=False,
    )
```

```python
import functools

import jax
import jax.numpy as jnp
from jax import lax
from jax.experimental import pallas as pl
from jax.experimental.pallas import tpu as pltpu
from jax.sharding import PartitionSpec as P

EDGE = 16
FACE = EDGE * EDGE
LANES = 128
ROWS = EDGE * FACE // LANES
COARSE = 0.2
META = 8
SLOT_ROWS = ROWS + META


def lane_pick(values, index):
    return jnp.take_along_axis(values, index, axis=1, mode="promise_in_bounds")


def iota(shape, axis):
    return lax.broadcasted_iota(jnp.int32, shape, axis)


def axis_factors(coords, middle, decay):
    return jnp.exp(-decay * (coords - middle) ** 2)


def pair_kernel(
    slot_depth,
    bricks_group,
    pairs_hbm,
    dest_hbm,
    tag_hbm,
    levels_hbm,
    blocks_hbm,
    centres_ref,
    exponents_ref,
    *refs,
):
    count = len(refs) - 12
    outs = refs[:count]
    (
        out_ref,
        pairs_ref,
        dest_ref,
        tag_ref,
        levels_ref,
        blocks_ref,
        centre_buf,
        decay_buf,
        corner_buf,
        sems,
        list_sems,
        block_sems,
    ) = refs[count:]
    me = lax.axis_index("row") * lax.axis_size("col") + lax.axis_index("col")
    items = blocks_ref.shape[0]
    slots = out_ref.shape[0]
    lists = [
        pltpu.make_async_copy(source, target, list_sems.at[n])
        for n, (source, target) in enumerate(
            (
                (pairs_hbm, pairs_ref),
                (dest_hbm, dest_ref),
                (tag_hbm, tag_ref),
                (levels_hbm, levels_ref),
            )
        )
    ]
    for copy in lists:
        copy.start()

    def block_copy(k):
        return pltpu.make_async_copy(blocks_hbm.at[k], blocks_ref.at[k], block_sems.at[k])

    for k in range(items):
        block_copy(k).start()
    lists[0].wait()

    def copies(k, side):
        block = pairs_ref[side, k]
        at = 2 * k + side
        return (
            pltpu.make_async_copy(
                centres_ref.at[:, pl.ds(block, 1), :], centre_buf.at[at], sems.at[0, at]
            ),
            pltpu.make_async_copy(
                exponents_ref.at[pl.ds(block, 1), :], decay_buf.at[at], sems.at[1, at]
            ),
        )

    for k in range(items):
        for side in range(2):
            for copy in copies(k, side):
                copy.start()
    for copy in lists[1:]:
        copy.wait()
    if slots != items:
        out_ref[...] = jnp.zeros_like(out_ref)

    def slot_of(k):
        slot = dest_ref[k]
        shift = lax.rem(slot // slot_depth - me + count, count)
        return shift * slot_depth + lax.rem(slot, slot_depth)

    steps = iota((EDGE, LANES), 0).astype(jnp.float32) - (EDGE - 1) / 2.0

    @pl.loop(0, items)
    def _(k):
        for side in range(2):
            for copy in copies(k, side):
                copy.wait()
        slot = slot_of(k)
        target = dest_ref[k] // slot_depth * bricks_group + tag_ref[k]
        spacing = jnp.where(levels_ref[target] == 1, COARSE * 0.5, COARSE)
        coords = steps * spacing

        def factors(side):
            at = 2 * k + side
            decay = decay_buf[at]
            found = [axis_factors(coords, centre_buf[at, d], decay) for d in range(3)]
            face = jnp.concatenate(
                [found[1][y : y + 1, :] * found[2] for y in range(EDGE)], axis=0
            )
            return found[0], face

        row_x, row_face = factors(0)
        col_x, col_face = factors(1)
        row_x = row_x.T
        row_face = row_face.T
        block_copy(k).wait()
        block = blocks_ref[k]
        for x in range(EDGE):
            col = (col_x[x : x + 1, :] * col_face).astype(jnp.bfloat16)
            product = lax.dot_general(
                block, col, (((1,), (1,)), ((), ())), preferred_element_type=jnp.float32
            )
            dens = jnp.sum(row_x[:, x : x + 1] * row_face * product, axis=0, keepdims=True)
            for half in range(FACE // LANES):
                piece = dens[:, half * LANES : (half + 1) * LANES]
                out_ref[slot, pl.ds(2 * x + half, 1), :] = piece
                if x in (0, EDGE - 1):
                    corner_buf[2 * (x // (EDGE - 1)) + half, pl.ds(k, 1), :] = piece

    shape = (items, LANES)
    lane = iota(shape, 1)
    place = lane % 4
    low = jnp.where(place % 2 == 1, EDGE - 1, 0)
    high = (FACE - EDGE) % LANES + low
    source = jnp.where(place >= 2, high, low)
    found = [lane_pick(corner_buf[n], source) for n in range(4)]
    corner = lane % 8
    first = jnp.where(corner % 4 >= 2, found[1], found[0])
    last = jnp.where(corner % 4 >= 2, found[3], found[2])
    values = jnp.where(corner >= 4, last, first)
    row = iota(shape, 0)
    brick = jnp.zeros(shape, jnp.int32)
    for k in range(items):
        target = dest_ref[k] // slot_depth * bricks_group + tag_ref[k]
        brick = jnp.where(row == k, target, brick)
    meta = jnp.where(lane < 8, values, brick.astype(jnp.float32))
    if slots != items:

        @pl.loop(0, slots)
        def _(s):
            out_ref[s, ROWS:, :] = jnp.where(lane >= LANES - 8, -1.0, meta)

    for k in range(items):
        tag = tag_ref[k].astype(jnp.float32)
        out_ref[slot_of(k), ROWS:, :] = jnp.where(lane >= LANES - 8, tag, meta)
    for d, out in enumerate(outs):
        out[...] = out_ref[d * slot_depth : (d + 1) * slot_depth]


def group_kernel(bricks_dev, count, *refs):
    ins, outs = refs[:count], refs[count:]
    owners = len(outs)
    me = lax.axis_index("basis")
    table_rows = outs[0].shape[0] - bricks_dev * ROWS
    shape = (META, LANES)
    lane = iota(shape, 1)
    index_tag = jnp.full(shape, LANES - 1, jnp.int32)
    sums = [jnp.zeros((bricks_dev * ROWS, LANES), jnp.float32) for _ in outs]
    slots = [(ref, s) for ref in ins for s in range(ref.shape[0])]
    for b in range(bricks_dev):
        for d in range(owners):
            brick = (lax.rem(me + d, owners) * bricks_dev + b).astype(jnp.float32)
            total = jnp.zeros((ROWS, LANES), jnp.float32)
            for ref, s in slots:
                tag = lane_pick(ref[s, ROWS:, :], index_tag)
                hit = jnp.tile(tag, (ROWS // META, 1)) == brick
                total = total + jnp.where(hit, ref[s, :ROWS, :], 0.0)
            outs[d][b * ROWS : (b + 1) * ROWS, :] = total
    lines = [jnp.zeros((1, LANES), jnp.float32) for _ in range(table_rows)]
    for ref, s in slots:
        meta = ref[s, ROWS:, :]
        values = lane_pick(meta, lane % 8)
        brick = lane_pick(meta, jnp.full(shape, 8, jnp.int32)).astype(jnp.int32)
        values = jnp.where(brick % 16 == lane // 8, values, 0.0)
        line = brick // 16
        for r in range(table_rows):
            part = jnp.sum(jnp.where(line == r, values, 0.0), axis=0, keepdims=True)
            lines[r] = lines[r] + part
    table = jnp.concatenate(lines, axis=0)
    for out in outs:
        out[bricks_dev * ROWS :, :] = table


def cell_kernel(*refs):
    *ins, cells_ref, refs_ref, out_ref = refs
    bricks_dev, cells = cells_ref.shape
    table_rows = ins[0].shape[0] - bricks_dev * ROWS

    total = ins[0][...]
    for part in ins[1:]:
        total = total + part[...]
    table = total[bricks_dev * ROWS :]
    chunk = (8, LANES)
    refs = [
        [refs_ref[b, :, c * LANES : (c + 1) * LANES] for c in range(cells // LANES)]
        for b in range(bricks_dev)
    ]
    picked = [[jnp.zeros(chunk, jnp.float32) for _ in row] for row in refs]
    for r in range(table_rows):
        line = jnp.broadcast_to(table[r : r + 1, :], chunk)
        for b in range(bricks_dev):
            for c, index in enumerate(refs[b]):
                found = lane_pick(line, index % LANES)
                picked[b][c] = jnp.where(index // LANES == r, found, picked[b][c])
    for b in range(bricks_dev):
        mean = jnp.concatenate(
            [jnp.sum(p, axis=0, keepdims=True) for p in picked[b]], axis=1
        ) * (0.5 / 8.0)
        position = cells_ref[b : b + 1, :]
        high = (position // LANES == iota((ROWS, cells), 0)).astype(jnp.float32)
        here = position % LANES == iota((LANES, cells), 0)

        def spread(values):
            return lax.dot_general(
                high,
                values,
                (((1,), (1,)), ((), ())),
                precision=lax.Precision.HIGHEST,
                preferred_element_type=jnp.float32,
            )

        hit = spread(here.astype(jnp.float32))
        new = spread(jnp.where(here, mean, 0.0))
        own = total[b * ROWS : (b + 1) * ROWS]
        result = jnp.where(hit > 0.5, 0.5 * own + new, own)
        for row in range(ROWS):
            out_ref[b : b + 1, row * LANES : (row + 1) * LANES] = result[row : row + 1, :]


def shifted(pieces, axes):
    count = len(pieces)
    return [
        lax.ppermute(piece, axes, [(i, (i + d) % count) for i in range(count)]) if d else piece
        for d, piece in enumerate(pieces)
    ]


def vmem():
    return pl.BlockSpec(memory_space=pltpu.VMEM)


def body(
    block_data, item_pairs, dest_slot, brick_tag, centres, exponents, levels, cell_pos, corner_refs
):
    groups = lax.axis_size("row") * lax.axis_size("col")
    owners = lax.axis_size("basis")
    items = block_data.shape[0]
    slot_depth = max(1, items // groups)
    slots = groups * slot_depth
    bricks = levels.shape[0]
    bricks_group = bricks // groups
    bricks_dev = bricks_group // owners
    table_rows = -(-bricks * 8 // (8 * LANES)) * 8
    basis = block_data.shape[1]
    params = pltpu.CompilerParams(vmem_limit_bytes=32 * 1024 * 1024)

    outgoing = pl.pallas_call(
        functools.partial(pair_kernel, slot_depth, bricks_group),
        out_shape=[jax.ShapeDtypeStruct((slot_depth, SLOT_ROWS, LANES), jnp.float32)] * groups,
        in_specs=[pl.BlockSpec(memory_space=pltpu.HBM)] * 7,
        out_specs=[vmem()] * groups,
        scratch_shapes=[
            pltpu.VMEM((slots, SLOT_ROWS, LANES), jnp.float32),
            pltpu.SMEM((2, items), jnp.int32),
            pltpu.SMEM((items,), jnp.int32),
            pltpu.SMEM((items,), jnp.int32),
            pltpu.SMEM((bricks,), jnp.int32),
            pltpu.VMEM(block_data.shape, block_data.dtype),
            pltpu.VMEM((2 * items, 3, 1, basis), jnp.float32),
            pltpu.VMEM((2 * items, 1, basis), jnp.float32),
            pltpu.VMEM((4, items, LANES), jnp.float32),
            pltpu.SemaphoreType.DMA((2, 2 * items)),
            pltpu.SemaphoreType.DMA((4,)),
            pltpu.SemaphoreType.DMA((items,)),
        ],
        compiler_params=params,
        name="pair_density",
    )(
        *(
            pltpu.with_memory_space_constraint(operand, pltpu.HBM)
            for operand in (
                item_pairs.T,
                dest_slot,
                brick_tag,
                levels,
                block_data,
                jnp.transpose(centres, (1, 0, 2)),
                exponents,
            )
        )
    )
    arrived = shifted(outgoing, ("row", "col"))
    partial = pl.pallas_call(
        functools.partial(group_kernel, bricks_dev, groups),
        out_shape=[jax.ShapeDtypeStruct((bricks_dev * ROWS + table_rows, LANES), jnp.float32)]
        * owners,
        in_specs=[vmem()] * groups,
        out_specs=[vmem()] * owners,
        compiler_params=params,
        name="group_sum",
    )(*arrived)
    parts = shifted(partial, "basis")
    return pl.pallas_call(
        cell_kernel,
        out_shape=jax.ShapeDtypeStruct((bricks_dev, EDGE * FACE), jnp.float32),
        in_specs=[vmem()] * (owners + 2),
        out_specs=vmem(),
        compiler_params=params,
        name="cells",
    )(*parts, cell_pos, jnp.transpose(corner_refs, (0, 2, 1)))


def solution(mesh):
    split = ("row", "col", "basis")
    return jax.shard_map(
        body,
        mesh=mesh,
        in_specs=(
            P(split, None, None),
            P(split, None),
            P(split),
            P(split),
            P(),
            P(),
            P(),
            P(split, None),
            P(split, None, None),
        ),
        out_specs=P(split, None),
        check_vma=False,
    )
```

```python
import functools

import jax
import jax.numpy as jnp
from jax import lax
from jax.experimental import pallas as pl
from jax.experimental.pallas import tpu as pltpu
from jax.sharding import PartitionSpec as P

EDGE = 16
FACE = EDGE * EDGE
LANES = 128
ROWS = EDGE * FACE // LANES
COARSE = 0.2
META = 8
SLOT_ROWS = ROWS + META


def lane_pick(values, index):
    return jnp.take_along_axis(values, index, axis=1, mode="promise_in_bounds")


def iota(shape, axis):
    return lax.broadcasted_iota(jnp.int32, shape, axis)


def axis_factors(coords, middle, decay):
    return jnp.exp(-decay * (coords - middle) ** 2)


def pair_kernel(
    slot_depth,
    bricks_group,
    pairs_hbm,
    dest_hbm,
    tag_hbm,
    levels_hbm,
    blocks_hbm,
    centres_ref,
    exponents_ref,
    out_ref,
    pairs_ref,
    dest_ref,
    tag_ref,
    levels_ref,
    blocks_ref,
    centre_buf,
    decay_buf,
    corner_buf,
    sems,
    list_sems,
    block_sems,
):
    items = blocks_ref.shape[0]
    slots = out_ref.shape[0]
    lists = [
        pltpu.make_async_copy(source, target, list_sems.at[n])
        for n, (source, target) in enumerate(
            (
                (pairs_hbm, pairs_ref),
                (dest_hbm, dest_ref),
                (tag_hbm, tag_ref),
                (levels_hbm, levels_ref),
            )
        )
    ]
    for copy in lists:
        copy.start()

    def block_copy(k):
        return pltpu.make_async_copy(blocks_hbm.at[k], blocks_ref.at[k], block_sems.at[k])

    for k in range(items):
        block_copy(k).start()
    lists[0].wait()

    def copies(k, side):
        block = pairs_ref[side, k]
        at = 2 * k + side
        return (
            pltpu.make_async_copy(
                centres_ref.at[:, pl.ds(block, 1), :], centre_buf.at[at], sems.at[0, at]
            ),
            pltpu.make_async_copy(
                exponents_ref.at[pl.ds(block, 1), :], decay_buf.at[at], sems.at[1, at]
            ),
        )

    for k in range(items):
        for side in range(2):
            for copy in copies(k, side):
                copy.start()
    for copy in lists[1:]:
        copy.wait()
    if slots != items:
        out_ref[...] = jnp.zeros_like(out_ref)
    steps = iota((EDGE, LANES), 0).astype(jnp.float32) - (EDGE - 1) / 2.0

    @pl.loop(0, items)
    def _(k):
        for side in range(2):
            for copy in copies(k, side):
                copy.wait()
        slot = dest_ref[k]
        target = slot // slot_depth * bricks_group + tag_ref[k]
        spacing = jnp.where(levels_ref[target] == 1, COARSE * 0.5, COARSE)
        coords = steps * spacing

        def factors(side):
            at = 2 * k + side
            decay = decay_buf[at]
            found = [axis_factors(coords, centre_buf[at, d], decay) for d in range(3)]
            face = jnp.concatenate(
                [found[1][y : y + 1, :] * found[2] for y in range(EDGE)], axis=0
            )
            return found[0], face

        row_x, row_face = factors(0)
        col_x, col_face = factors(1)
        row_x = row_x.T
        row_face = row_face.T
        block_copy(k).wait()
        block = blocks_ref[k]
        for x in range(EDGE):
            col = (col_x[x : x + 1, :] * col_face).astype(jnp.bfloat16)
            product = lax.dot_general(
                block, col, (((1,), (1,)), ((), ())), preferred_element_type=jnp.float32
            )
            dens = jnp.sum(row_x[:, x : x + 1] * row_face * product, axis=0, keepdims=True)
            for half in range(FACE // LANES):
                piece = dens[:, half * LANES : (half + 1) * LANES]
                out_ref[slot, pl.ds(2 * x + half, 1), :] = piece
                if x in (0, EDGE - 1):
                    corner_buf[2 * (x // (EDGE - 1)) + half, pl.ds(k, 1), :] = piece

    shape = (items, LANES)
    lane = iota(shape, 1)
    place = lane % 4
    low = jnp.where(place % 2 == 1, EDGE - 1, 0)
    high = (FACE - EDGE) % LANES + low
    source = jnp.where(place >= 2, high, low)
    found = [lane_pick(corner_buf[n], source) for n in range(4)]
    corner = lane % 8
    first = jnp.where(corner % 4 >= 2, found[1], found[0])
    last = jnp.where(corner % 4 >= 2, found[3], found[2])
    values = jnp.where(corner >= 4, last, first)
    row = iota(shape, 0)
    brick = jnp.zeros(shape, jnp.int32)
    for k in range(items):
        target = dest_ref[k] // slot_depth * bricks_group + tag_ref[k]
        brick = jnp.where(row == k, target, brick)
    meta = jnp.where(lane < 8, values, brick.astype(jnp.float32))
    if slots != items:

        @pl.loop(0, slots)
        def _(s):
            out_ref[s, ROWS:, :] = jnp.where(lane >= LANES - 8, -1.0, meta)

    for k in range(items):
        tag = tag_ref[k].astype(jnp.float32)
        out_ref[dest_ref[k], ROWS:, :] = jnp.where(lane >= LANES - 8, tag, meta)


def group_kernel(bricks_dev, in_ref, *outs):
    owners = len(outs)
    me = lax.axis_index("basis")
    table_rows = outs[0].shape[0] - bricks_dev * ROWS
    shape = (META, LANES)
    lane = iota(shape, 1)
    index_tag = jnp.full(shape, LANES - 1, jnp.int32)
    slots = range(in_ref.shape[0])
    for b in range(bricks_dev):
        for d in range(owners):
            brick = (partner(me, d, owners) * bricks_dev + b).astype(jnp.float32)
            total = jnp.zeros((ROWS, LANES), jnp.float32)
            for s in slots:
                tag = lane_pick(in_ref[s, ROWS:, :], index_tag)
                hit = jnp.tile(tag, (ROWS // META, 1)) == brick
                total = total + jnp.where(hit, in_ref[s, :ROWS, :], 0.0)
            outs[d][b * ROWS : (b + 1) * ROWS, :] = total
    lines = [jnp.zeros((1, LANES), jnp.float32) for _ in range(table_rows)]
    for s in slots:
        meta = in_ref[s, ROWS:, :]
        values = lane_pick(meta, lane % 8)
        brick = lane_pick(meta, jnp.full(shape, 8, jnp.int32)).astype(jnp.int32)
        values = jnp.where(brick % 16 == lane // 8, values, 0.0)
        line = brick // 16
        for r in range(table_rows):
            part = jnp.sum(jnp.where(line == r, values, 0.0), axis=0, keepdims=True)
            lines[r] = lines[r] + part
    table = jnp.concatenate(lines, axis=0)
    for out in outs:
        out[bricks_dev * ROWS :, :] = table


def cell_kernel(*refs):
    *ins, cells_ref, refs_ref, out_ref = refs
    bricks_dev, cells = cells_ref.shape
    table_rows = ins[0].shape[0] - bricks_dev * ROWS

    total = ins[0][...]
    for part in ins[1:]:
        total = total + part[...]
    table = total[bricks_dev * ROWS :]
    chunk = (8, LANES)
    refs = [
        [refs_ref[b, :, c * LANES : (c + 1) * LANES] for c in range(cells // LANES)]
        for b in range(bricks_dev)
    ]
    picked = [[jnp.zeros(chunk, jnp.float32) for _ in row] for row in refs]
    for r in range(table_rows):
        line = jnp.broadcast_to(table[r : r + 1, :], chunk)
        for b in range(bricks_dev):
            for c, index in enumerate(refs[b]):
                found = lane_pick(line, index % LANES)
                picked[b][c] = jnp.where(index // LANES == r, found, picked[b][c])
    for b in range(bricks_dev):
        mean = jnp.concatenate(
            [jnp.sum(p, axis=0, keepdims=True) for p in picked[b]], axis=1
        ) * (0.5 / 8.0)
        position = cells_ref[b : b + 1, :]
        high = (position // LANES == iota((ROWS, cells), 0)).astype(jnp.float32)
        here = position % LANES == iota((LANES, cells), 0)

        def spread(values):
            return lax.dot_general(
                high,
                values,
                (((1,), (1,)), ((), ())),
                precision=lax.Precision.HIGHEST,
                preferred_element_type=jnp.float32,
            )

        hit = spread(here.astype(jnp.float32))
        new = spread(jnp.where(here, mean, 0.0))
        own = total[b * ROWS : (b + 1) * ROWS]
        result = jnp.where(hit > 0.5, 0.5 * own + new, own)
        for row in range(ROWS):
            out_ref[b : b + 1, row * LANES : (row + 1) * LANES] = result[row : row + 1, :]


def partner(index, shift, count):
    if count & (count - 1) == 0:
        return index ^ shift
    return (index + shift) % count


def shifted(pieces, axes):
    count = len(pieces)
    moved = list(pieces)
    for d in range(count - 1, 0, -1):
        pairs = [(i, partner(i, d, count)) for i in range(count)]
        moved[d] = lax.ppermute(pieces[d], axes, pairs)
    return moved


def vmem():
    return pl.BlockSpec(memory_space=pltpu.VMEM)


def body(
    block_data, item_pairs, dest_slot, brick_tag, centres, exponents, levels, cell_pos, corner_refs
):
    groups = lax.axis_size("row") * lax.axis_size("col")
    owners = lax.axis_size("basis")
    items = block_data.shape[0]
    slot_depth = max(1, items // groups)
    slots = groups * slot_depth
    bricks = levels.shape[0]
    bricks_group = bricks // groups
    bricks_dev = bricks_group // owners
    table_rows = -(-bricks * 8 // (8 * LANES)) * 8
    basis = block_data.shape[1]
    params = pltpu.CompilerParams(vmem_limit_bytes=32 * 1024 * 1024)

    outgoing = pl.pallas_call(
        functools.partial(pair_kernel, slot_depth, bricks_group),
        out_shape=jax.ShapeDtypeStruct((slots, SLOT_ROWS, LANES), jnp.float32),
        in_specs=[pl.BlockSpec(memory_space=pltpu.HBM)] * 7,
        out_specs=vmem(),
        scratch_shapes=[
            pltpu.SMEM((2, items), jnp.int32),
            pltpu.SMEM((items,), jnp.int32),
            pltpu.SMEM((items,), jnp.int32),
            pltpu.SMEM((bricks,), jnp.int32),
            pltpu.VMEM(block_data.shape, block_data.dtype),
            pltpu.VMEM((2 * items, 3, 1, basis), jnp.float32),
            pltpu.VMEM((2 * items, 1, basis), jnp.float32),
            pltpu.VMEM((4, items, LANES), jnp.float32),
            pltpu.SemaphoreType.DMA((2, 2 * items)),
            pltpu.SemaphoreType.DMA((4,)),
            pltpu.SemaphoreType.DMA((items,)),
        ],
        compiler_params=params,
        name="pair_density",
    )(
        *(
            pltpu.with_memory_space_constraint(operand, pltpu.HBM)
            for operand in (
                item_pairs.T,
                dest_slot,
                brick_tag,
                levels,
                block_data,
                jnp.transpose(centres, (1, 0, 2)),
                exponents,
            )
        )
    )
    arrived = lax.all_to_all(outgoing, ("row", "col"), split_axis=0, concat_axis=0, tiled=True)
    partial = pl.pallas_call(
        functools.partial(group_kernel, bricks_dev),
        out_shape=[jax.ShapeDtypeStruct((bricks_dev * ROWS + table_rows, LANES), jnp.float32)]
        * owners,
        in_specs=[vmem()],
        out_specs=[vmem()] * owners,
        compiler_params=params,
        name="group_sum",
    )(arrived)
    parts = shifted(partial, "basis")
    return pl.pallas_call(
        cell_kernel,
        out_shape=jax.ShapeDtypeStruct((bricks_dev, EDGE * FACE), jnp.float32),
        in_specs=[vmem()] * (owners + 2),
        out_specs=vmem(),
        compiler_params=params,
        name="cells",
    )(*parts, cell_pos, jnp.transpose(corner_refs, (0, 2, 1)))


def solution(mesh):
    split = ("row", "col", "basis")
    return jax.shard_map(
        body,
        mesh=mesh,
        in_specs=(
            P(split, None, None),
            P(split, None),
            P(split),
            P(split),
            P(),
            P(),
            P(),
            P(split, None),
            P(split, None, None),
        ),
        out_specs=P(split, None),
        check_vma=False,
    )
```

```python
import functools

import jax
import jax.numpy as jnp
from jax import lax
from jax.experimental import pallas as pl
from jax.experimental.pallas import tpu as pltpu
from jax.sharding import PartitionSpec as P

EDGE = 16
FACE = EDGE * EDGE
LANES = 128
ROWS = EDGE * FACE // LANES
COARSE = 0.2
META = 8
SLOT_ROWS = ROWS + META


def lane_pick(values, index):
    return jnp.take_along_axis(values, index, axis=1, mode="promise_in_bounds")


def iota(shape, axis):
    return lax.broadcasted_iota(jnp.int32, shape, axis)


def axis_factors(coords, middle, decay):
    return jnp.exp(-decay * (coords - middle) ** 2)


def pair_kernel(
    slot_depth,
    bricks_group,
    pairs_hbm,
    dest_hbm,
    tag_hbm,
    levels_hbm,
    blocks_hbm,
    centres_ref,
    exponents_ref,
    out_ref,
    pairs_ref,
    dest_ref,
    tag_ref,
    levels_ref,
    blocks_ref,
    centre_buf,
    decay_buf,
    corner_buf,
    sems,
    list_sems,
    block_sems,
):
    items = blocks_ref.shape[0]
    slots = out_ref.shape[0]
    lists = [
        pltpu.make_async_copy(source, target, list_sems.at[n])
        for n, (source, target) in enumerate(
            (
                (pairs_hbm, pairs_ref),
                (dest_hbm, dest_ref),
                (tag_hbm, tag_ref),
                (levels_hbm, levels_ref),
            )
        )
    ]
    for copy in lists:
        copy.start()

    def block_copy(k):
        return pltpu.make_async_copy(blocks_hbm.at[k], blocks_ref.at[k], block_sems.at[k])

    for k in range(items):
        block_copy(k).start()
    lists[0].wait()

    def copies(k, side):
        block = pairs_ref[side, k]
        at = 2 * k + side
        return (
            pltpu.make_async_copy(
                centres_ref.at[:, pl.ds(block, 1), :], centre_buf.at[at], sems.at[0, at]
            ),
            pltpu.make_async_copy(
                exponents_ref.at[pl.ds(block, 1), :], decay_buf.at[at], sems.at[1, at]
            ),
        )

    for k in range(items):
        for side in range(2):
            for copy in copies(k, side):
                copy.start()
    for copy in lists[1:]:
        copy.wait()
    if slots != items:
        out_ref[...] = jnp.zeros_like(out_ref)
    steps = iota((EDGE, LANES), 0).astype(jnp.float32) - (EDGE - 1) / 2.0

    for k in range(items):
        for side in range(2):
            for copy in copies(k, side):
                copy.wait()
        block_copy(k).wait()

    def one(k):
        slot = dest_ref[k]
        target = slot // slot_depth * bricks_group + tag_ref[k]
        spacing = jnp.where(levels_ref[target] == 1, COARSE * 0.5, COARSE)
        coords = steps * spacing

        def factors(side):
            at = 2 * k + side
            decay = decay_buf[at]
            found = [axis_factors(coords, centre_buf[at, d], decay) for d in range(3)]
            face = jnp.concatenate(
                [found[1][y : y + 1, :] * found[2] for y in range(EDGE)], axis=0
            )
            return found[0], face

        row_x, row_face = factors(0)
        col_x, col_face = factors(1)
        row_x = row_x.T
        row_face = row_face.T
        block = blocks_ref[k]
        for x in range(EDGE):
            col = (col_x[x : x + 1, :] * col_face).astype(jnp.bfloat16)
            product = lax.dot_general(
                block, col, (((1,), (1,)), ((), ())), preferred_element_type=jnp.float32
            )
            dens = jnp.sum(row_x[:, x : x + 1] * row_face * product, axis=0, keepdims=True)
            for half in range(FACE // LANES):
                piece = dens[:, half * LANES : (half + 1) * LANES]
                out_ref[slot, pl.ds(2 * x + half, 1), :] = piece
                if x in (0, EDGE - 1):
                    corner_buf[2 * (x // (EDGE - 1)) + half, pl.ds(k, 1), :] = piece

    for k in range(items):
        one(k)

    shape = (items, LANES)
    lane = iota(shape, 1)
    place = lane % 4
    low = jnp.where(place % 2 == 1, EDGE - 1, 0)
    high = (FACE - EDGE) % LANES + low
    source = jnp.where(place >= 2, high, low)
    found = [lane_pick(corner_buf[n], source) for n in range(4)]
    corner = lane % 8
    first = jnp.where(corner % 4 >= 2, found[1], found[0])
    last = jnp.where(corner % 4 >= 2, found[3], found[2])
    values = jnp.where(corner >= 4, last, first)
    row = iota(shape, 0)
    brick = jnp.zeros(shape, jnp.int32)
    for k in range(items):
        target = dest_ref[k] // slot_depth * bricks_group + tag_ref[k]
        brick = jnp.where(row == k, target, brick)
    meta = jnp.where(lane < 8, values, brick.astype(jnp.float32))
    if slots != items:

        @pl.loop(0, slots)
        def _(s):
            out_ref[s, ROWS:, :] = jnp.where(lane >= LANES - 8, -1.0, meta)

    for k in range(items):
        tag = tag_ref[k].astype(jnp.float32)
        out_ref[dest_ref[k], ROWS:, :] = jnp.where(lane >= LANES - 8, tag, meta)


def group_kernel(bricks_dev, in_ref, *outs):
    owners = len(outs)
    me = lax.axis_index("basis")
    table_rows = outs[0].shape[0] - bricks_dev * ROWS
    shape = (META, LANES)
    lane = iota(shape, 1)
    index_tag = jnp.full(shape, LANES - 1, jnp.int32)
    slots = range(in_ref.shape[0])
    for b in range(bricks_dev):
        for d in range(owners):
            brick = (partner(me, d, owners) * bricks_dev + b).astype(jnp.float32)
            total = jnp.zeros((ROWS, LANES), jnp.float32)
            for s in slots:
                tag = lane_pick(in_ref[s, ROWS:, :], index_tag)
                hit = jnp.tile(tag, (ROWS // META, 1)) == brick
                total = total + jnp.where(hit, in_ref[s, :ROWS, :], 0.0)
            outs[d][b * ROWS : (b + 1) * ROWS, :] = total
    lines = [jnp.zeros((1, LANES), jnp.float32) for _ in range(table_rows)]
    for s in slots:
        meta = in_ref[s, ROWS:, :]
        values = lane_pick(meta, lane % 8)
        brick = lane_pick(meta, jnp.full(shape, 8, jnp.int32)).astype(jnp.int32)
        values = jnp.where(brick % 16 == lane // 8, values, 0.0)
        line = brick // 16
        for r in range(table_rows):
            part = jnp.sum(jnp.where(line == r, values, 0.0), axis=0, keepdims=True)
            lines[r] = lines[r] + part
    table = jnp.concatenate(lines, axis=0)
    for out in outs:
        out[bricks_dev * ROWS :, :] = table


def cell_kernel(*refs):
    *ins, cells_ref, refs_ref, out_ref = refs
    bricks_dev, cells = cells_ref.shape
    table_rows = ins[0].shape[0] - bricks_dev * ROWS

    total = ins[0][...]
    for part in ins[1:]:
        total = total + part[...]
    table = total[bricks_dev * ROWS :]
    chunk = (8, LANES)
    refs = [
        [refs_ref[b, :, c * LANES : (c + 1) * LANES] for c in range(cells // LANES)]
        for b in range(bricks_dev)
    ]
    picked = [[jnp.zeros(chunk, jnp.float32) for _ in row] for row in refs]
    for r in range(table_rows):
        line = jnp.broadcast_to(table[r : r + 1, :], chunk)
        for b in range(bricks_dev):
            for c, index in enumerate(refs[b]):
                found = lane_pick(line, index % LANES)
                picked[b][c] = jnp.where(index // LANES == r, found, picked[b][c])
    for b in range(bricks_dev):
        mean = jnp.concatenate(
            [jnp.sum(p, axis=0, keepdims=True) for p in picked[b]], axis=1
        ) * (0.5 / 8.0)
        position = cells_ref[b : b + 1, :]
        high = (position // LANES == iota((ROWS, cells), 0)).astype(jnp.float32)
        here = position % LANES == iota((LANES, cells), 0)

        def spread(values):
            return lax.dot_general(
                high,
                values,
                (((1,), (1,)), ((), ())),
                precision=lax.Precision.HIGHEST,
                preferred_element_type=jnp.float32,
            )

        hit = spread(here.astype(jnp.float32))
        new = spread(jnp.where(here, mean, 0.0))
        own = total[b * ROWS : (b + 1) * ROWS]
        result = jnp.where(hit > 0.5, 0.5 * own + new, own)
        for row in range(ROWS):
            out_ref[b : b + 1, row * LANES : (row + 1) * LANES] = result[row : row + 1, :]


def partner(index, shift, count):
    if count & (count - 1) == 0:
        return index ^ shift
    return (index + shift) % count


def shifted(pieces, axes):
    count = len(pieces)
    moved = list(pieces)
    for d in range(count - 1, 0, -1):
        pairs = [(i, partner(i, d, count)) for i in range(count)]
        moved[d] = lax.ppermute(pieces[d], axes, pairs)
    return moved


def vmem():
    return pl.BlockSpec(memory_space=pltpu.VMEM)


def body(
    block_data, item_pairs, dest_slot, brick_tag, centres, exponents, levels, cell_pos, corner_refs
):
    groups = lax.axis_size("row") * lax.axis_size("col")
    owners = lax.axis_size("basis")
    items = block_data.shape[0]
    slot_depth = max(1, items // groups)
    slots = groups * slot_depth
    bricks = levels.shape[0]
    bricks_group = bricks // groups
    bricks_dev = bricks_group // owners
    table_rows = -(-bricks * 8 // (8 * LANES)) * 8
    basis = block_data.shape[1]
    params = pltpu.CompilerParams(vmem_limit_bytes=32 * 1024 * 1024)

    outgoing = pl.pallas_call(
        functools.partial(pair_kernel, slot_depth, bricks_group),
        out_shape=jax.ShapeDtypeStruct((slots, SLOT_ROWS, LANES), jnp.float32),
        in_specs=[pl.BlockSpec(memory_space=pltpu.HBM)] * 7,
        out_specs=vmem(),
        scratch_shapes=[
            pltpu.SMEM((2, items), jnp.int32),
            pltpu.SMEM((items,), jnp.int32),
            pltpu.SMEM((items,), jnp.int32),
            pltpu.SMEM((bricks,), jnp.int32),
            pltpu.VMEM(block_data.shape, block_data.dtype),
            pltpu.VMEM((2 * items, 3, 1, basis), jnp.float32),
            pltpu.VMEM((2 * items, 1, basis), jnp.float32),
            pltpu.VMEM((4, items, LANES), jnp.float32),
            pltpu.SemaphoreType.DMA((2, 2 * items)),
            pltpu.SemaphoreType.DMA((4,)),
            pltpu.SemaphoreType.DMA((items,)),
        ],
        compiler_params=params,
        name="pair_density",
    )(
        *(
            pltpu.with_memory_space_constraint(operand, pltpu.HBM)
            for operand in (
                item_pairs.T,
                dest_slot,
                brick_tag,
                levels,
                block_data,
                jnp.transpose(centres, (1, 0, 2)),
                exponents,
            )
        )
    )
    arrived = lax.all_to_all(outgoing, ("row", "col"), split_axis=0, concat_axis=0, tiled=True)
    partial = pl.pallas_call(
        functools.partial(group_kernel, bricks_dev),
        out_shape=[jax.ShapeDtypeStruct((bricks_dev * ROWS + table_rows, LANES), jnp.float32)]
        * owners,
        in_specs=[vmem()],
        out_specs=[vmem()] * owners,
        compiler_params=params,
        name="group_sum",
    )(arrived)
    parts = shifted(partial, "basis")
    return pl.pallas_call(
        cell_kernel,
        out_shape=jax.ShapeDtypeStruct((bricks_dev, EDGE * FACE), jnp.float32),
        in_specs=[vmem()] * (owners + 2),
        out_specs=vmem(),
        compiler_params=params,
        name="cells",
    )(*parts, cell_pos, jnp.transpose(corner_refs, (0, 2, 1)))


def solution(mesh):
    split = ("row", "col", "basis")
    return jax.shard_map(
        body,
        mesh=mesh,
        in_specs=(
            P(split, None, None),
            P(split, None),
            P(split),
            P(split),
            P(),
            P(),
            P(),
            P(split, None),
            P(split, None, None),
        ),
        out_specs=P(split, None),
        check_vma=False,
    )
```

```python
import functools

import jax
import jax.numpy as jnp
from jax import lax
from jax.experimental import pallas as pl
from jax.experimental.pallas import tpu as pltpu
from jax.sharding import PartitionSpec as P

EDGE = 16
FACE = EDGE * EDGE
LANES = 128
ROWS = EDGE * FACE // LANES
COARSE = 0.2
TILE = 8


def lane_pick(values, index):
    return jnp.take_along_axis(values, index, axis=1, mode="promise_in_bounds")


def iota(shape, axis):
    return lax.broadcasted_iota(jnp.int32, shape, axis)


def axis_factors(coords, middle, decay):
    return jnp.exp(-decay * (coords - middle) ** 2)


def pair_kernel(
    slot_depth,
    width,
    bricks_group,
    pairs_hbm,
    dest_hbm,
    tag_hbm,
    levels_hbm,
    blocks_hbm,
    centres_ref,
    exponents_ref,
    out_ref,
    pairs_ref,
    dest_ref,
    tag_ref,
    levels_ref,
    blocks_ref,
    centre_buf,
    decay_buf,
    corner_buf,
    sems,
    list_sems,
    block_sems,
):
    items = blocks_ref.shape[0]
    part_rows = ROWS // width
    chunks = out_ref.shape[0] // (part_rows + 1)
    lists = [
        pltpu.make_async_copy(source, target, list_sems.at[n])
        for n, (source, target) in enumerate(
            (
                (pairs_hbm, pairs_ref),
                (dest_hbm, dest_ref),
                (tag_hbm, tag_ref),
                (levels_hbm, levels_ref),
            )
        )
    ]
    for copy in lists:
        copy.start()

    def block_copy(k):
        return pltpu.make_async_copy(blocks_hbm.at[k], blocks_ref.at[k], block_sems.at[k])

    for k in range(items):
        block_copy(k).start()
    lists[0].wait()

    def copies(k, side):
        block = pairs_ref[side, k]
        at = 2 * k + side
        return (
            pltpu.make_async_copy(
                centres_ref.at[:, pl.ds(block, 1), :], centre_buf.at[at], sems.at[0, at]
            ),
            pltpu.make_async_copy(
                exponents_ref.at[pl.ds(block, 1), :], decay_buf.at[at], sems.at[1, at]
            ),
        )

    for k in range(items):
        for side in range(2):
            for copy in copies(k, side):
                copy.start()
    for copy in lists[1:]:
        copy.wait()
    if chunks != items * width:
        out_ref[...] = jnp.zeros_like(out_ref)

    def first_row(k, part):
        slot = dest_ref[k]
        chunk = (slot // slot_depth * width + part) * slot_depth + lax.rem(slot, slot_depth)
        return chunk * (part_rows + 1)

    steps = iota((EDGE, LANES), 0).astype(jnp.float32) - (EDGE - 1) / 2.0

    for k in range(items):
        for side in range(2):
            for copy in copies(k, side):
                copy.wait()
        block_copy(k).wait()

    def one(k):
        target = dest_ref[k] // slot_depth * bricks_group + tag_ref[k]
        spacing = jnp.where(levels_ref[target] == 1, COARSE * 0.5, COARSE)
        coords = steps * spacing

        def factors(side):
            at = 2 * k + side
            decay = decay_buf[at]
            found = [axis_factors(coords, centre_buf[at, d], decay) for d in range(3)]
            face = jnp.concatenate(
                [found[1][y : y + 1, :] * found[2] for y in range(EDGE)], axis=0
            )
            return found[0], face

        row_x, row_face = factors(0)
        col_x, col_face = factors(1)
        row_x = row_x.T
        row_face = row_face.T
        block = blocks_ref[k]
        for x in range(EDGE):
            col = (col_x[x : x + 1, :] * col_face).astype(jnp.bfloat16)
            product = lax.dot_general(
                block, col, (((1,), (1,)), ((), ())), preferred_element_type=jnp.float32
            )
            dens = jnp.sum(row_x[:, x : x + 1] * row_face * product, axis=0, keepdims=True)
            for half in range(FACE // LANES):
                piece = dens[:, half * LANES : (half + 1) * LANES]
                part, row = divmod(2 * x + half, part_rows)
                out_ref[pl.ds(first_row(k, part) + row, 1), :] = piece
                if x in (0, EDGE - 1):
                    corner_buf[2 * (x // (EDGE - 1)) + half, pl.ds(k, 1), :] = piece

    for k in range(items):
        one(k)

    shape = (items, LANES)
    lane = iota(shape, 1)
    place = lane % 4
    low = jnp.where(place % 2 == 1, EDGE - 1, 0)
    high = (FACE - EDGE) % LANES + low
    source = jnp.where(place >= 2, high, low)
    found = [lane_pick(corner_buf[n], source) for n in range(4)]
    corner = lane % 8
    first = jnp.where(corner % 4 >= 2, found[1], found[0])
    last = jnp.where(corner % 4 >= 2, found[3], found[2])
    values = jnp.where(corner >= 4, last, first)
    row = iota(shape, 0)
    brick = jnp.zeros(shape, jnp.int32)
    for k in range(items):
        target = dest_ref[k] // slot_depth * bricks_group + tag_ref[k]
        brick = jnp.where(row == k, target, brick)
    placed = jnp.where(lane // 8 == row, values, 0.0)
    placed = jnp.where(lane == 8 * items + row, brick.astype(jnp.float32), placed)
    meta = jnp.sum(placed, axis=0, keepdims=True)
    last_lane = iota((1, LANES), 1) == LANES - 1
    if chunks != items * width:

        @pl.loop(0, chunks)
        def _(n):
            out_ref[pl.ds(n * (part_rows + 1) + part_rows, 1), :] = jnp.where(
                last_lane, -1.0, meta
            )

    for k in range(items):
        tagged = jnp.where(last_lane, tag_ref[k].astype(jnp.float32), meta)
        for part in range(width):
            out_ref[pl.ds(first_row(k, part) + part_rows, 1), :] = tagged


def group_kernel(items, bricks_dev, width, in_ref, *outs):
    owners = len(outs)
    me = lax.axis_index("basis")
    part_rows = ROWS // width
    chunks = in_ref.shape[0] // (part_rows + 1)
    meta = [
        in_ref[n * (part_rows + 1) + part_rows : (n + 1) * (part_rows + 1), :]
        for n in range(chunks)
    ]
    tags = [
        jnp.broadcast_to(line[:, LANES - 1 :], (part_rows, LANES)) for line in meta
    ]
    for d in range(owners):
        for b in range(bricks_dev):
            brick = (owner_of(me, d, owners, width) * bricks_dev + b).astype(jnp.float32)
            total = jnp.zeros((part_rows, LANES), jnp.float32)
            for n in range(chunks):
                dens = in_ref[n * (part_rows + 1) : n * (part_rows + 1) + part_rows, :]
                total = total + jnp.where(tags[n] == brick, dens, 0.0)
            outs[d][b * part_rows : (b + 1) * part_rows, :] = total
    table_rows = outs[0].shape[0] - bricks_dev * part_rows
    shape = (TILE, LANES)
    lane = iota(shape, 1)
    lines = [jnp.zeros(shape, jnp.float32) for _ in range(table_rows)]
    for first in range(0, chunks, TILE):
        block = jnp.concatenate(meta[first : first + TILE], axis=0)
        for k in range(items):
            values = lane_pick(block, 8 * k + lane % 8)
            brick = lane_pick(block, jnp.full(shape, 8 * items + k, jnp.int32)).astype(jnp.int32)
            values = jnp.where(brick % 16 == lane // 8, values, 0.0)
            for r in range(table_rows):
                lines[r] = lines[r] + jnp.where(brick // 16 == r, values, 0.0)
    table = jnp.concatenate([jnp.sum(line, axis=0, keepdims=True) for line in lines], axis=0)
    for out in outs[::width]:
        out[bricks_dev * part_rows :, :] = table


def cell_kernel(width, *refs):
    *ins, cells_ref, refs_ref, out_ref = refs
    bricks_dev, cells = cells_ref.shape
    part_rows = ROWS // width
    table_rows = ins[0].shape[0] - bricks_dev * part_rows
    mine = lax.axis_index("basis") % width

    totals = []
    for offset in range(width):
        total = ins[offset][...]
        for part in ins[offset + width :: width]:
            total = total + part[...]
        totals.append(total)
    table = totals[0][bricks_dev * part_rows :]

    def own_points(b):
        halves = [total[b * part_rows : (b + 1) * part_rows] for total in totals]
        if width == 1:
            return halves[0]
        straight = jnp.concatenate(halves, axis=0)
        crossed = jnp.concatenate(halves[::-1], axis=0)
        return jnp.where(mine == 0, straight, crossed)

    chunk = (8, LANES)
    refs = [
        [refs_ref[b, :, c * LANES : (c + 1) * LANES] for c in range(cells // LANES)]
        for b in range(bricks_dev)
    ]
    picked = [[jnp.zeros(chunk, jnp.float32) for _ in row] for row in refs]
    for r in range(table_rows):
        line = jnp.broadcast_to(table[r : r + 1, :], chunk)
        for b in range(bricks_dev):
            for c, index in enumerate(refs[b]):
                found = lane_pick(line, index % LANES)
                picked[b][c] = jnp.where(index // LANES == r, found, picked[b][c])
    for b in range(bricks_dev):
        mean = jnp.concatenate(
            [jnp.sum(p, axis=0, keepdims=True) for p in picked[b]], axis=1
        ) * (0.5 / 8.0)
        position = cells_ref[b : b + 1, :]
        high = (position // LANES == iota((ROWS, cells), 0)).astype(jnp.float32)
        here = position % LANES == iota((LANES, cells), 0)

        def spread(values):
            return lax.dot_general(
                high,
                values,
                (((1,), (1,)), ((), ())),
                precision=lax.Precision.HIGHEST,
                preferred_element_type=jnp.float32,
            )

        hit = spread(here.astype(jnp.float32))
        new = spread(jnp.where(here, mean, 0.0))
        own = own_points(b)
        result = jnp.where(hit > 0.5, 0.5 * own + new, own)
        for row in range(ROWS):
            out_ref[b : b + 1, row * LANES : (row + 1) * LANES] = result[row : row + 1, :]


def owner_of(index, shift, owners, width):
    sets = owners // width
    pair, side = index // width, index % width
    jump, turn = divmod(shift, width)
    pair = pair ^ jump if sets & (sets - 1) == 0 else (pair + jump) % sets
    return pair * width + (side ^ turn)


def shifted(pieces, axis, width):
    owners = len(pieces)
    moved = list(pieces)
    for d in range(owners - 1, 0, -1):
        pairs = [(i, owner_of(i, d, owners, width)) for i in range(owners)]
        moved[d] = lax.ppermute(pieces[d], axis, pairs)
    return moved


def vmem():
    return pl.BlockSpec(memory_space=pltpu.VMEM)


def body(
    block_data, item_pairs, dest_slot, brick_tag, centres, exponents, levels, cell_pos, corner_refs
):
    groups = lax.axis_size("row") * lax.axis_size("col")
    owners = lax.axis_size("basis")
    items = block_data.shape[0]
    slot_depth = max(1, items // groups)
    slots = groups * slot_depth
    bricks = levels.shape[0]
    bricks_group = bricks // groups
    bricks_dev = bricks_group // owners
    table_rows = -(-bricks * 8 // (8 * LANES)) * 8
    basis = block_data.shape[1]
    width = 2 if owners % 2 == 0 else 1
    part_rows = ROWS // width
    chunks = slots * width
    params = pltpu.CompilerParams(vmem_limit_bytes=32 * 1024 * 1024)

    outgoing = pl.pallas_call(
        functools.partial(pair_kernel, slot_depth, width, bricks_group),
        out_shape=jax.ShapeDtypeStruct((chunks * (part_rows + 1), LANES), jnp.float32),
        in_specs=[pl.BlockSpec(memory_space=pltpu.HBM)] * 7,
        out_specs=vmem(),
        scratch_shapes=[
            pltpu.SMEM((2, items), jnp.int32),
            pltpu.SMEM((items,), jnp.int32),
            pltpu.SMEM((items,), jnp.int32),
            pltpu.SMEM((bricks,), jnp.int32),
            pltpu.VMEM(block_data.shape, block_data.dtype),
            pltpu.VMEM((2 * items, 3, 1, basis), jnp.float32),
            pltpu.VMEM((2 * items, 1, basis), jnp.float32),
            pltpu.VMEM((4, items, LANES), jnp.float32),
            pltpu.SemaphoreType.DMA((2, 2 * items)),
            pltpu.SemaphoreType.DMA((4,)),
            pltpu.SemaphoreType.DMA((items,)),
        ],
        compiler_params=params,
        name="pair_density",
    )(
        *(
            pltpu.with_memory_space_constraint(operand, pltpu.HBM)
            for operand in (
                item_pairs.T,
                dest_slot,
                brick_tag,
                levels,
                block_data,
                jnp.transpose(centres, (1, 0, 2)),
                exponents,
            )
        )
    )
    sets = [
        [g * owners + first + side for g in range(groups) for side in range(width)]
        for first in range(0, owners, width)
    ]
    arrived = lax.all_to_all(
        outgoing.reshape(chunks, 1, (part_rows + 1) * LANES),
        ("row", "col", "basis"),
        split_axis=0,
        concat_axis=0,
        tiled=True,
        axis_index_groups=sets,
    ).reshape(outgoing.shape)
    partial = pl.pallas_call(
        functools.partial(group_kernel, items, bricks_dev, width),
        out_shape=[
            jax.ShapeDtypeStruct(
                (bricks_dev * part_rows + (0 if d % width else table_rows), LANES), jnp.float32
            )
            for d in range(owners)
        ],
        in_specs=[vmem()],
        out_specs=[vmem()] * owners,
        compiler_params=params,
        name="group_sum",
    )(arrived)
    parts = shifted(partial, "basis", width)
    return pl.pallas_call(
        functools.partial(cell_kernel, width),
        out_shape=jax.ShapeDtypeStruct((bricks_dev, EDGE * FACE), jnp.float32),
        in_specs=[vmem()] * (owners + 2),
        out_specs=vmem(),
        compiler_params=params,
        name="cells",
    )(*parts, cell_pos, jnp.transpose(corner_refs, (0, 2, 1)))


def solution(mesh):
    split = ("row", "col", "basis")
    return jax.shard_map(
        body,
        mesh=mesh,
        in_specs=(
            P(split, None, None),
            P(split, None),
            P(split),
            P(split),
            P(),
            P(),
            P(),
            P(split, None),
            P(split, None, None),
        ),
        out_specs=P(split, None),
        check_vma=False,
    )
```

```python
import functools

import jax
import jax.numpy as jnp
from jax import lax
from jax.experimental import pallas as pl
from jax.experimental.pallas import tpu as pltpu
from jax.sharding import PartitionSpec as P

EDGE = 16
FACE = EDGE * EDGE
LANES = 128
ROWS = EDGE * FACE // LANES
COARSE = 0.2
TILE = 8


def lane_pick(values, index):
    return jnp.take_along_axis(values, index, axis=1, mode="promise_in_bounds")


def iota(shape, axis):
    return lax.broadcasted_iota(jnp.int32, shape, axis)


def axis_factors(coords, middle, decay):
    return jnp.exp(-decay * (coords - middle) ** 2)


def pair_kernel(
    slot_depth,
    width,
    bricks_group,
    pairs_hbm,
    dest_hbm,
    tag_hbm,
    levels_hbm,
    blocks_hbm,
    centres_ref,
    exponents_ref,
    out_ref,
    pairs_ref,
    dest_ref,
    tag_ref,
    levels_ref,
    blocks_ref,
    centre_buf,
    decay_buf,
    corner_buf,
    sems,
    list_sems,
    block_sems,
):
    items = blocks_ref.shape[0]
    part_rows = ROWS // width
    chunks = out_ref.shape[0] // (part_rows + 1)
    lists = [
        pltpu.make_async_copy(source, target, list_sems.at[n])
        for n, (source, target) in enumerate(
            (
                (pairs_hbm, pairs_ref),
                (dest_hbm, dest_ref),
                (tag_hbm, tag_ref),
                (levels_hbm, levels_ref),
            )
        )
    ]
    for copy in lists:
        copy.start()

    def block_copy(k):
        return pltpu.make_async_copy(blocks_hbm.at[k], blocks_ref.at[k], block_sems.at[k])

    for k in range(items):
        block_copy(k).start()
    lists[0].wait()

    def copies(k, side):
        block = pairs_ref[side, k]
        at = 2 * k + side
        return (
            pltpu.make_async_copy(
                centres_ref.at[:, pl.ds(block, 1), :], centre_buf.at[at], sems.at[0, at]
            ),
            pltpu.make_async_copy(
                exponents_ref.at[pl.ds(block, 1), :], decay_buf.at[at], sems.at[1, at]
            ),
        )

    for k in range(items):
        for side in range(2):
            for copy in copies(k, side):
                copy.start()
    for copy in lists[1:]:
        copy.wait()
    if chunks != items * width:
        out_ref[...] = jnp.zeros_like(out_ref)

    def first_row(k, part):
        slot = dest_ref[k]
        chunk = (slot // slot_depth * width + part) * slot_depth + lax.rem(slot, slot_depth)
        return chunk * (part_rows + 1)

    steps = iota((EDGE, LANES), 0).astype(jnp.float32) - (EDGE - 1) / 2.0

    for k in range(items):
        for side in range(2):
            for copy in copies(k, side):
                copy.wait()
        block_copy(k).wait()

    def one(k):
        target = dest_ref[k] // slot_depth * bricks_group + tag_ref[k]
        spacing = jnp.where(levels_ref[target] == 1, COARSE * 0.5, COARSE)
        coords = steps * spacing

        def factors(side):
            at = 2 * k + side
            decay = decay_buf[at]
            found = [axis_factors(coords, centre_buf[at, d], decay) for d in range(3)]
            face = jnp.concatenate(
                [found[1][y : y + 1, :] * found[2] for y in range(EDGE)], axis=0
            )
            return found[0], face

        row_x, row_face = factors(0)
        col_x, col_face = factors(1)
        row_x = row_x.T
        row_face = row_face.T
        block = blocks_ref[k]
        for x in range(EDGE):
            col = (col_x[x : x + 1, :] * col_face).astype(jnp.bfloat16)
            product = lax.dot_general(
                block, col, (((1,), (1,)), ((), ())), preferred_element_type=jnp.float32
            )
            dens = jnp.sum(row_x[:, x : x + 1] * row_face * product, axis=0, keepdims=True)
            for half in range(FACE // LANES):
                piece = dens[:, half * LANES : (half + 1) * LANES]
                part, row = divmod(2 * x + half, part_rows)
                out_ref[pl.ds(first_row(k, part) + row, 1), :] = piece
                if x in (0, EDGE - 1):
                    corner_buf[2 * (x // (EDGE - 1)) + half, pl.ds(k, 1), :] = piece

    for k in range(items):
        one(k)

    shape = (items, LANES)
    lane = iota(shape, 1)
    place = lane % 4
    low = jnp.where(place % 2 == 1, EDGE - 1, 0)
    high = (FACE - EDGE) % LANES + low
    source = jnp.where(place >= 2, high, low)
    found = [lane_pick(corner_buf[n], source) for n in range(4)]
    corner = lane % 8
    first = jnp.where(corner % 4 >= 2, found[1], found[0])
    last = jnp.where(corner % 4 >= 2, found[3], found[2])
    values = jnp.where(corner >= 4, last, first)
    row = iota(shape, 0)
    brick = jnp.zeros(shape, jnp.int32)
    for k in range(items):
        target = dest_ref[k] // slot_depth * bricks_group + tag_ref[k]
        brick = jnp.where(row == k, target, brick)
    placed = jnp.where(lane // 8 == row, values, 0.0)
    placed = jnp.where(lane == 8 * items + row, brick.astype(jnp.float32), placed)
    meta = jnp.sum(placed, axis=0, keepdims=True)
    last_lane = iota((1, LANES), 1) == LANES - 1
    if chunks != items * width:

        @pl.loop(0, chunks)
        def _(n):
            out_ref[pl.ds(n * (part_rows + 1) + part_rows, 1), :] = jnp.where(
                last_lane, -1.0, meta
            )

    for k in range(items):
        tagged = jnp.where(last_lane, tag_ref[k].astype(jnp.float32), meta)
        for part in range(width):
            out_ref[pl.ds(first_row(k, part) + part_rows, 1), :] = tagged


def group_kernel(items, bricks_dev, width, owners, shifts, in_ref, *outs):
    me = lax.axis_index("basis")
    part_rows = ROWS // width
    chunks = in_ref.shape[0] // (part_rows + 1)
    meta = [
        in_ref[n * (part_rows + 1) + part_rows : (n + 1) * (part_rows + 1), :]
        for n in range(chunks)
    ]
    tags = [
        jnp.broadcast_to(line[:, LANES - 1 :], (part_rows, LANES)) for line in meta
    ]
    for d in range(owners):
        for b in range(bricks_dev):
            brick = (owner_of(me, d, owners, width) * bricks_dev + b).astype(jnp.float32)
            total = jnp.zeros((part_rows, LANES), jnp.float32)
            for n in range(chunks):
                dens = in_ref[n * (part_rows + 1) : n * (part_rows + 1) + part_rows, :]
                total = total + jnp.where(tags[n] == brick, dens, 0.0)
            for out, shift in zip(outs, shifts):
                if shift == d:
                    out[b * part_rows : (b + 1) * part_rows, :] = total
    table_rows = outs[0].shape[0] - bricks_dev * part_rows
    shape = (TILE, LANES)
    lane = iota(shape, 1)
    lines = [jnp.zeros(shape, jnp.float32) for _ in range(table_rows)]
    for first in range(0, chunks, TILE):
        block = jnp.concatenate(meta[first : first + TILE], axis=0)
        for k in range(items):
            values = lane_pick(block, 8 * k + lane % 8)
            brick = lane_pick(block, jnp.full(shape, 8 * items + k, jnp.int32)).astype(jnp.int32)
            values = jnp.where(brick % 16 == lane // 8, values, 0.0)
            for r in range(table_rows):
                lines[r] = lines[r] + jnp.where(brick // 16 == r, values, 0.0)
    table = jnp.concatenate([jnp.sum(line, axis=0, keepdims=True) for line in lines], axis=0)
    for out, shift in zip(outs, shifts):
        if shift % width == 0:
            out[bricks_dev * part_rows :, :] = table


def cell_kernel(width, *refs):
    *ins, cells_ref, refs_ref, out_ref = refs
    bricks_dev, cells = cells_ref.shape
    part_rows = ROWS // width
    table_rows = ins[0].shape[0] - bricks_dev * part_rows
    mine = lax.axis_index("basis") % width

    totals = []
    for offset in range(width):
        total = ins[offset][...]
        for part in ins[offset + width :: width]:
            total = total + part[...]
        totals.append(total)
    table = totals[0][bricks_dev * part_rows :]

    def own_points(b):
        halves = [total[b * part_rows : (b + 1) * part_rows] for total in totals]
        if width == 1:
            return halves[0]
        straight = jnp.concatenate(halves, axis=0)
        crossed = jnp.concatenate(halves[::-1], axis=0)
        return jnp.where(mine == 0, straight, crossed)

    chunk = (8, LANES)
    refs = [
        [refs_ref[b, :, c * LANES : (c + 1) * LANES] for c in range(cells // LANES)]
        for b in range(bricks_dev)
    ]
    picked = [[jnp.zeros(chunk, jnp.float32) for _ in row] for row in refs]
    for r in range(table_rows):
        line = jnp.broadcast_to(table[r : r + 1, :], chunk)
        for b in range(bricks_dev):
            for c, index in enumerate(refs[b]):
                found = lane_pick(line, index % LANES)
                picked[b][c] = jnp.where(index // LANES == r, found, picked[b][c])
    for b in range(bricks_dev):
        mean = jnp.concatenate(
            [jnp.sum(p, axis=0, keepdims=True) for p in picked[b]], axis=1
        ) * (0.5 / 8.0)
        position = cells_ref[b : b + 1, :]
        high = (position // LANES == iota((ROWS, cells), 0)).astype(jnp.float32)
        here = position % LANES == iota((LANES, cells), 0)

        def spread(values):
            return lax.dot_general(
                high,
                values,
                (((1,), (1,)), ((), ())),
                precision=lax.Precision.HIGHEST,
                preferred_element_type=jnp.float32,
            )

        hit = spread(here.astype(jnp.float32))
        new = spread(jnp.where(here, mean, 0.0))
        own = own_points(b)
        result = jnp.where(hit > 0.5, 0.5 * own + new, own)
        for row in range(ROWS):
            out_ref[b : b + 1, row * LANES : (row + 1) * LANES] = result[row : row + 1, :]


def owner_of(index, shift, owners, width):
    sets = owners // width
    pair, side = index // width, index % width
    jump, turn = divmod(shift, width)
    pair = pair ^ jump if sets & (sets - 1) == 0 else (pair + jump) % sets
    return pair * width + (side ^ turn)


def exchanges(owners, width):
    if width > 1 or owners & (owners - 1) or owners > 8:
        return [
            (d, [(i, owner_of(i, d, owners, width)) for i in range(owners)])
            for d in range(1, owners)
        ]
    return [
        (low ^ high, [(low, high), (high, low)]) for high in range(1, owners) for low in range(high)
    ]


def vmem():
    return pl.BlockSpec(memory_space=pltpu.VMEM)


def body(
    block_data, item_pairs, dest_slot, brick_tag, centres, exponents, levels, cell_pos, corner_refs
):
    groups = lax.axis_size("row") * lax.axis_size("col")
    owners = lax.axis_size("basis")
    items = block_data.shape[0]
    slot_depth = max(1, items // groups)
    slots = groups * slot_depth
    bricks = levels.shape[0]
    bricks_group = bricks // groups
    bricks_dev = bricks_group // owners
    table_rows = -(-bricks * 8 // (8 * LANES)) * 8
    basis = block_data.shape[1]
    width = 1
    part_rows = ROWS // width
    chunks = slots * width
    params = pltpu.CompilerParams(vmem_limit_bytes=32 * 1024 * 1024)

    outgoing = pl.pallas_call(
        functools.partial(pair_kernel, slot_depth, width, bricks_group),
        out_shape=jax.ShapeDtypeStruct((chunks * (part_rows + 1), LANES), jnp.float32),
        in_specs=[pl.BlockSpec(memory_space=pltpu.HBM)] * 7,
        out_specs=vmem(),
        scratch_shapes=[
            pltpu.SMEM((2, items), jnp.int32),
            pltpu.SMEM((items,), jnp.int32),
            pltpu.SMEM((items,), jnp.int32),
            pltpu.SMEM((bricks,), jnp.int32),
            pltpu.VMEM(block_data.shape, block_data.dtype),
            pltpu.VMEM((2 * items, 3, 1, basis), jnp.float32),
            pltpu.VMEM((2 * items, 1, basis), jnp.float32),
            pltpu.VMEM((4, items, LANES), jnp.float32),
            pltpu.SemaphoreType.DMA((2, 2 * items)),
            pltpu.SemaphoreType.DMA((4,)),
            pltpu.SemaphoreType.DMA((items,)),
        ],
        compiler_params=params,
        name="pair_density",
    )(
        *(
            pltpu.with_memory_space_constraint(operand, pltpu.HBM)
            for operand in (
                item_pairs.T,
                dest_slot,
                brick_tag,
                levels,
                block_data,
                jnp.transpose(centres, (1, 0, 2)),
                exponents,
            )
        )
    )
    sets = [
        [g * owners + first + side for g in range(groups) for side in range(width)]
        for first in range(0, owners, width)
    ]
    arrived = lax.all_to_all(
        outgoing.reshape(chunks, 1, (part_rows + 1) * LANES),
        ("row", "col", "basis"),
        split_axis=0,
        concat_axis=0,
        tiled=True,
        axis_index_groups=sets,
    ).reshape(outgoing.shape)
    moves = exchanges(owners, width)
    shifts = [0] + [d for d, _ in moves]
    partial = pl.pallas_call(
        functools.partial(group_kernel, items, bricks_dev, width, owners, shifts),
        out_shape=[
            jax.ShapeDtypeStruct(
                (bricks_dev * part_rows + (0 if d % width else table_rows), LANES), jnp.float32
            )
            for d in shifts
        ],
        in_specs=[vmem()],
        out_specs=[vmem()] * len(shifts),
        compiler_params=params,
        name="group_sum",
    )(arrived)
    parts = [partial[0]] + [
        lax.ppermute(piece, "basis", pairs) for piece, (_, pairs) in zip(partial[1:], moves)
    ]
    return pl.pallas_call(
        functools.partial(cell_kernel, width),
        out_shape=jax.ShapeDtypeStruct((bricks_dev, EDGE * FACE), jnp.float32),
        in_specs=[vmem()] * (len(parts) + 2),
        out_specs=vmem(),
        compiler_params=params,
        name="cells",
    )(*parts, cell_pos, jnp.transpose(corner_refs, (0, 2, 1)))


def solution(mesh):
    split = ("row", "col", "basis")
    return jax.shard_map(
        body,
        mesh=mesh,
        in_specs=(
            P(split, None, None),
            P(split, None),
            P(split),
            P(split),
            P(),
            P(),
            P(),
            P(split, None),
            P(split, None, None),
        ),
        out_specs=P(split, None),
        check_vma=False,
    )
```

```python
import functools

import jax
import jax.numpy as jnp
from jax import lax
from jax.experimental import pallas as pl
from jax.experimental.pallas import tpu as pltpu
from jax.sharding import PartitionSpec as P

EDGE = 16
FACE = EDGE * EDGE
LANES = 128
SHIFT = 7
ROWS = EDGE * FACE // LANES
COARSE = 0.2
TILE = 8


def lane_pick(values, index):
    return jnp.take_along_axis(values, index, axis=1, mode="promise_in_bounds")


def iota(shape, axis):
    return lax.broadcasted_iota(jnp.int32, shape, axis)


def axis_factors(coords, middle, decay):
    return jnp.exp(-decay * (coords - middle) ** 2)


def pair_kernel(
    slot_depth,
    width,
    bricks_group,
    pairs_hbm,
    dest_hbm,
    tag_hbm,
    levels_hbm,
    blocks_hbm,
    centres_ref,
    exponents_ref,
    out_ref,
    pairs_ref,
    dest_ref,
    tag_ref,
    levels_ref,
    blocks_ref,
    centre_buf,
    decay_buf,
    corner_buf,
    sems,
    list_sems,
    block_sems,
):
    items = blocks_ref.shape[0]
    part_rows = ROWS // width
    chunks = out_ref.shape[0] // (part_rows + 1)
    lists = [
        pltpu.make_async_copy(source, target, list_sems.at[n])
        for n, (source, target) in enumerate(
            (
                (pairs_hbm, pairs_ref),
                (dest_hbm, dest_ref),
                (tag_hbm, tag_ref),
                (levels_hbm, levels_ref),
            )
        )
    ]
    for copy in lists:
        copy.start()

    def block_copy(k):
        return pltpu.make_async_copy(blocks_hbm.at[k], blocks_ref.at[k], block_sems.at[k])

    for k in range(items):
        block_copy(k).start()
    lists[0].wait()

    def copies(k, side):
        block = pairs_ref[side, k]
        at = 2 * k + side
        return (
            pltpu.make_async_copy(
                centres_ref.at[:, pl.ds(block, 1), :], centre_buf.at[at], sems.at[0, at]
            ),
            pltpu.make_async_copy(
                exponents_ref.at[pl.ds(block, 1), :], decay_buf.at[at], sems.at[1, at]
            ),
        )

    for k in range(items):
        for side in range(2):
            for copy in copies(k, side):
                copy.start()
    for copy in lists[1:]:
        copy.wait()
    if chunks != items * width:
        out_ref[...] = jnp.zeros_like(out_ref)

    def first_row(k, part):
        slot = dest_ref[k]
        chunk = (slot // slot_depth * width + part) * slot_depth + lax.rem(slot, slot_depth)
        return chunk * (part_rows + 1)

    steps = iota((EDGE, LANES), 0).astype(jnp.float32) - (EDGE - 1) / 2.0

    for k in range(items):
        for side in range(2):
            for copy in copies(k, side):
                copy.wait()
        block_copy(k).wait()

    def one(k):
        target = dest_ref[k] // slot_depth * bricks_group + tag_ref[k]
        spacing = jnp.where(levels_ref[target] == 1, COARSE * 0.5, COARSE)
        coords = steps * spacing

        def factors(side):
            at = 2 * k + side
            decay = decay_buf[at]
            found = [axis_factors(coords, centre_buf[at, d], decay) for d in range(3)]
            face = jnp.concatenate(
                [found[1][y : y + 1, :] * found[2] for y in range(EDGE)], axis=0
            )
            return found[0], face

        row_x, row_face = factors(0)
        col_x, col_face = factors(1)
        row_x = row_x.T
        row_face = row_face.T
        block = blocks_ref[k]
        for x in range(EDGE):
            col = (col_x[x : x + 1, :] * col_face).astype(jnp.bfloat16)
            product = lax.dot_general(
                block, col, (((1,), (1,)), ((), ())), preferred_element_type=jnp.float32
            )
            dens = jnp.sum(row_x[:, x : x + 1] * row_face * product, axis=0, keepdims=True)
            for half in range(FACE // LANES):
                piece = dens[:, half * LANES : (half + 1) * LANES]
                part, row = divmod(2 * x + half, part_rows)
                out_ref[pl.ds(first_row(k, part) + row, 1), :] = piece
                if x in (0, EDGE - 1):
                    corner_buf[2 * (x // (EDGE - 1)) + half, pl.ds(k, 1), :] = piece

    unroll = 4 if items % 4 == 0 else 1

    @pl.loop(0, items // unroll)
    def _(step):
        for n in range(unroll):
            one(step * unroll + n)

    shape = (items, LANES)
    lane = iota(shape, 1)
    place = lane % 4
    low = jnp.where(place % 2 == 1, EDGE - 1, 0)
    high = (FACE - EDGE) % LANES + low
    source = jnp.where(place >= 2, high, low)
    found = [lane_pick(corner_buf[n], source) for n in range(4)]
    corner = lane % 8
    first = jnp.where(corner % 4 >= 2, found[1], found[0])
    last = jnp.where(corner % 4 >= 2, found[3], found[2])
    values = jnp.where(corner >= 4, last, first)
    row = iota(shape, 0)
    brick = jnp.zeros(shape, jnp.int32)
    for k in range(items):
        target = dest_ref[k] // slot_depth * bricks_group + tag_ref[k]
        brick = jnp.where(row == k, target, brick)
    placed = jnp.where(lane // 8 == row, values, 0.0)
    placed = jnp.where(lane == 8 * items + row, brick.astype(jnp.float32), placed)
    meta = jnp.sum(placed, axis=0, keepdims=True)
    last_lane = iota((1, LANES), 1) == LANES - 1
    if chunks != items * width:

        @pl.loop(0, chunks)
        def _(n):
            out_ref[pl.ds(n * (part_rows + 1) + part_rows, 1), :] = jnp.where(
                last_lane, -1.0, meta
            )

    for k in range(items):
        tagged = jnp.where(last_lane, tag_ref[k].astype(jnp.float32), meta)
        for part in range(width):
            out_ref[pl.ds(first_row(k, part) + part_rows, 1), :] = tagged


def group_kernel(items, bricks_dev, width, owners, shifts, in_ref, *outs):
    me = lax.axis_index("basis")
    part_rows = ROWS // width
    chunks = in_ref.shape[0] // (part_rows + 1)
    meta = [
        in_ref[n * (part_rows + 1) + part_rows : (n + 1) * (part_rows + 1), :]
        for n in range(chunks)
    ]
    tags = [
        jnp.broadcast_to(line[:, LANES - 1 :], (part_rows, LANES)) for line in meta
    ]
    for d in range(owners):
        for b in range(bricks_dev):
            brick = (owner_of(me, d, owners, width) * bricks_dev + b).astype(jnp.float32)
            total = jnp.zeros((part_rows, LANES), jnp.float32)
            for n in range(chunks):
                dens = in_ref[n * (part_rows + 1) : n * (part_rows + 1) + part_rows, :]
                total = total + jnp.where(tags[n] == brick, dens, 0.0)
            for out, shift in zip(outs, shifts):
                if shift == d:
                    out[b * part_rows : (b + 1) * part_rows, :] = total
    table_rows = outs[0].shape[0] - bricks_dev * part_rows
    shape = (TILE, LANES)
    lane = iota(shape, 1)
    lines = [jnp.zeros(shape, jnp.float32) for _ in range(table_rows)]
    for first in range(0, chunks, TILE):
        block = jnp.concatenate(meta[first : first + TILE], axis=0)
        for k in range(items):
            values = lane_pick(block, 8 * k + (lane & 7))
            brick = lane_pick(block, jnp.full(shape, 8 * items + k, jnp.int32)).astype(jnp.int32)
            values = jnp.where((brick & 15) == lane >> 3, values, 0.0)
            for r in range(table_rows):
                lines[r] = lines[r] + jnp.where(brick >> 4 == r, values, 0.0)
    table = jnp.concatenate([jnp.sum(line, axis=0, keepdims=True) for line in lines], axis=0)
    for out, shift in zip(outs, shifts):
        if shift % width == 0:
            out[bricks_dev * part_rows :, :] = table


def map_kernel(cells_ref, out_ref):
    bricks_dev, cells = cells_ref.shape
    cell = (iota((LANES, cells), 1) + 1).astype(jnp.float32)
    for b in range(bricks_dev):
        position = cells_ref[b : b + 1, :]
        high = position >> SHIFT == iota((ROWS, cells), 0)
        low = (position & (LANES - 1)) == iota((LANES, cells), 0)
        found = lax.dot_general(
            high.astype(jnp.float32).astype(jnp.bfloat16),
            jnp.where(low, cell, 0.0).astype(jnp.bfloat16),
            (((1,), (1,)), ((), ())),
            preferred_element_type=jnp.float32,
        )
        out_ref[b] = found.astype(jnp.int32) - 1


def cell_kernel(width, shifts, *refs):
    *ins, map_ref, refs_ref, out_ref = refs
    bricks_dev, _, cells = refs_ref.shape
    part_rows = ROWS // width
    mine = lax.axis_index("basis") % width

    totals = []
    for offset in range(width):
        parts = [part for part, shift in zip(ins, shifts) if shift % width == offset]
        total = parts[0][...]
        for part in parts[1:]:
            total = total + part[...]
        totals.append(total)
    table = totals[0][bricks_dev * part_rows :]

    def own_points(b):
        halves = [total[b * part_rows : (b + 1) * part_rows] for total in totals]
        if width == 1:
            return halves[0]
        straight = jnp.concatenate(halves, axis=0)
        crossed = jnp.concatenate(halves[::-1], axis=0)
        return jnp.where(mine == 0, straight, crossed)

    chunk = (TILE, LANES)
    tiles = cells // LANES
    refs = [
        [refs_ref[b, :, c * LANES : (c + 1) * LANES] for c in range(tiles)]
        for b in range(bricks_dev)
    ]
    picked = [[jnp.zeros(chunk, jnp.float32) for _ in row] for row in refs]
    for r in range(table.shape[0]):
        line = jnp.broadcast_to(table[r : r + 1, :], chunk)
        for b in range(bricks_dev):
            for c, index in enumerate(refs[b]):
                found = lane_pick(line, (index & (LANES - 1)))
                picked[b][c] = jnp.where(index >> SHIFT == r, found, picked[b][c])
    for b in range(bricks_dev):
        cell = map_ref[b]
        mean = jnp.zeros((ROWS, LANES), jnp.float32)
        for c in range(tiles):
            line = jnp.sum(picked[b][c], axis=0, keepdims=True) * (0.5 / 8.0)
            found = lane_pick(jnp.broadcast_to(line, (ROWS, LANES)), (cell & (LANES - 1)))
            mean = jnp.where(cell >> SHIFT == c, found, mean)
        own = own_points(b)
        result = jnp.where(cell >= 0, 0.5 * own + mean, own)
        for row in range(ROWS):
            out_ref[b : b + 1, row * LANES : (row + 1) * LANES] = result[row : row + 1, :]


def owner_of(index, shift, owners, width):
    sets = owners // width
    pair, side = index // width, index % width
    jump, turn = divmod(shift, width)
    pair = pair ^ jump if sets & (sets - 1) == 0 else (pair + jump) % sets
    return pair * width + (side ^ turn)


def exchanges(owners, width):
    return [
        (d, [(i, owner_of(i, d, owners, width)) for i in range(owners)])
        for d in range(owners - 1, 0, -1)
    ]


def vmem():
    return pl.BlockSpec(memory_space=pltpu.VMEM)


def body(
    block_data, item_pairs, dest_slot, brick_tag, centres, exponents, levels, cell_pos, corner_refs
):
    groups = lax.axis_size("row") * lax.axis_size("col")
    owners = lax.axis_size("basis")
    items = block_data.shape[0]
    slot_depth = max(1, items // groups)
    slots = groups * slot_depth
    bricks = levels.shape[0]
    bricks_group = bricks // groups
    bricks_dev = bricks_group // owners
    table_rows = -(-bricks * 8 // (8 * LANES)) * 8
    basis = block_data.shape[1]
    width = 1
    part_rows = ROWS // width
    chunks = slots * width
    params = pltpu.CompilerParams(vmem_limit_bytes=32 * 1024 * 1024)

    outgoing = pl.pallas_call(
        functools.partial(pair_kernel, slot_depth, width, bricks_group),
        out_shape=jax.ShapeDtypeStruct((chunks * (part_rows + 1), LANES), jnp.float32),
        in_specs=[pl.BlockSpec(memory_space=pltpu.HBM)] * 7,
        out_specs=vmem(),
        scratch_shapes=[
            pltpu.SMEM((2, items), jnp.int32),
            pltpu.SMEM((items,), jnp.int32),
            pltpu.SMEM((items,), jnp.int32),
            pltpu.SMEM((bricks,), jnp.int32),
            pltpu.VMEM(block_data.shape, block_data.dtype),
            pltpu.VMEM((2 * items, 3, 1, basis), jnp.float32),
            pltpu.VMEM((2 * items, 1, basis), jnp.float32),
            pltpu.VMEM((4, items, LANES), jnp.float32),
            pltpu.SemaphoreType.DMA((2, 2 * items)),
            pltpu.SemaphoreType.DMA((4,)),
            pltpu.SemaphoreType.DMA((items,)),
        ],
        compiler_params=params,
        name="pair_density",
    )(
        *(
            pltpu.with_memory_space_constraint(operand, pltpu.HBM)
            for operand in (
                item_pairs.T,
                dest_slot,
                brick_tag,
                levels,
                block_data,
                jnp.transpose(centres, (1, 0, 2)),
                exponents,
            )
        )
    )
    sets = [
        [g * owners + first + side for g in range(groups) for side in range(width)]
        for first in range(0, owners, width)
    ]
    arrived = lax.all_to_all(
        outgoing.reshape(chunks, 1, (part_rows + 1) * LANES),
        ("row", "col", "basis"),
        split_axis=0,
        concat_axis=0,
        tiled=True,
        axis_index_groups=sets,
    ).reshape(outgoing.shape)
    moves = exchanges(owners, width)
    shifts = [0] + [d for d, _ in moves]
    partial = pl.pallas_call(
        functools.partial(group_kernel, items, bricks_dev, width, owners, shifts),
        out_shape=[
            jax.ShapeDtypeStruct(
                (bricks_dev * part_rows + (0 if d % width else table_rows), LANES), jnp.float32
            )
            for d in shifts
        ],
        in_specs=[vmem()],
        out_specs=[vmem()] * len(shifts),
        compiler_params=params,
        name="group_sum",
    )(arrived)
    parts = [partial[0]] + [
        lax.ppermute(piece, "basis", pairs) for piece, (_, pairs) in zip(partial[1:], moves)
    ]
    cell_map = pl.pallas_call(
        map_kernel,
        out_shape=jax.ShapeDtypeStruct((bricks_dev, ROWS, LANES), jnp.int32),
        in_specs=[vmem()],
        out_specs=vmem(),
        compiler_params=params,
        cost_estimate=pl.CostEstimate(flops=4_000_000, bytes_accessed=200_000, transcendentals=0),
        name="cell_map",
    )(cell_pos)
    return pl.pallas_call(
        functools.partial(cell_kernel, width, shifts),
        out_shape=jax.ShapeDtypeStruct((bricks_dev, EDGE * FACE), jnp.float32),
        in_specs=[vmem()] * (len(parts) + 2),
        out_specs=vmem(),
        compiler_params=params,
        name="cells",
    )(*parts, cell_map, jnp.transpose(corner_refs, (0, 2, 1)))


def solution(mesh):
    split = ("row", "col", "basis")
    return jax.shard_map(
        body,
        mesh=mesh,
        in_specs=(
            P(split, None, None),
            P(split, None),
            P(split),
            P(split),
            P(),
            P(),
            P(),
            P(split, None),
            P(split, None, None),
        ),
        out_specs=P(split, None),
        check_vma=False,
    )
```

```python
import functools

import jax
import jax.numpy as jnp
from jax import lax
from jax.experimental import pallas as pl
from jax.experimental.pallas import tpu as pltpu
from jax.sharding import PartitionSpec as P

EDGE = 16
FACE = EDGE * EDGE
LANES = 128
SHIFT = 7
ROWS = EDGE * FACE // LANES
COARSE = 0.2
TILE = 8


def lane_pick(values, index):
    return jnp.take_along_axis(values, index, axis=1, mode="promise_in_bounds")


def iota(shape, axis):
    return lax.broadcasted_iota(jnp.int32, shape, axis)


def axis_factors(coords, middle, decay):
    return jnp.exp(-decay * (coords - middle) ** 2)


def pair_kernel(
    slot_depth,
    width,
    bricks_group,
    pairs_hbm,
    dest_hbm,
    tag_hbm,
    levels_hbm,
    blocks_hbm,
    centres_ref,
    exponents_ref,
    out_ref,
    pairs_ref,
    dest_ref,
    tag_ref,
    levels_ref,
    blocks_ref,
    centre_buf,
    decay_buf,
    corner_buf,
    sems,
    list_sems,
    block_sems,
):
    items = blocks_ref.shape[0]
    part_rows = ROWS // width
    chunks = out_ref.shape[0] // (part_rows + 1)
    lists = [
        pltpu.make_async_copy(source, target, list_sems.at[n])
        for n, (source, target) in enumerate(
            (
                (pairs_hbm, pairs_ref),
                (dest_hbm, dest_ref),
                (tag_hbm, tag_ref),
                (levels_hbm, levels_ref),
            )
        )
    ]
    for copy in lists:
        copy.start()

    def block_copy(k):
        return pltpu.make_async_copy(blocks_hbm.at[k], blocks_ref.at[k], block_sems.at[k])

    for k in range(items):
        block_copy(k).start()
    lists[0].wait()

    def copies(k, side):
        block = pairs_ref[side, k]
        at = 2 * k + side
        return (
            pltpu.make_async_copy(
                centres_ref.at[:, pl.ds(block, 1), :], centre_buf.at[at], sems.at[0, at]
            ),
            pltpu.make_async_copy(
                exponents_ref.at[pl.ds(block, 1), :], decay_buf.at[at], sems.at[1, at]
            ),
        )

    for k in range(items):
        for side in range(2):
            for copy in copies(k, side):
                copy.start()
    for copy in lists[1:]:
        copy.wait()
    if chunks != items * width:
        out_ref[...] = jnp.zeros_like(out_ref)

    def first_row(k, part):
        slot = dest_ref[k]
        chunk = (slot // slot_depth * width + part) * slot_depth + lax.rem(slot, slot_depth)
        return chunk * (part_rows + 1)

    steps = iota((EDGE, LANES), 0).astype(jnp.float32) - (EDGE - 1) / 2.0

    for k in range(items):
        for side in range(2):
            for copy in copies(k, side):
                copy.wait()
        block_copy(k).wait()

    def one(k):
        target = dest_ref[k] // slot_depth * bricks_group + tag_ref[k]
        spacing = jnp.where(levels_ref[target] == 1, COARSE * 0.5, COARSE)
        coords = steps * spacing

        def factors(side):
            at = 2 * k + side
            decay = decay_buf[at]
            found = [axis_factors(coords, centre_buf[at, d], decay) for d in range(3)]
            face = jnp.concatenate(
                [found[1][y : y + 1, :] * found[2] for y in range(EDGE)], axis=0
            )
            return found[0], face

        row_x, row_face = factors(0)
        col_x, col_face = factors(1)
        row_x = row_x.T
        row_face = row_face.T
        block = blocks_ref[k]
        for x in range(EDGE):
            col = (col_x[x : x + 1, :] * col_face).astype(jnp.bfloat16)
            product = lax.dot_general(
                block, col, (((1,), (1,)), ((), ())), preferred_element_type=jnp.float32
            )
            dens = jnp.sum(row_x[:, x : x + 1] * row_face * product, axis=0, keepdims=True)
            for half in range(FACE // LANES):
                piece = dens[:, half * LANES : (half + 1) * LANES]
                part, row = divmod(2 * x + half, part_rows)
                out_ref[pl.ds(first_row(k, part) + row, 1), :] = piece
                if x in (0, EDGE - 1):
                    corner_buf[2 * (x // (EDGE - 1)) + half, pl.ds(k, 1), :] = piece

    unroll = 4 if items % 4 == 0 else 1

    @pl.loop(0, items // unroll)
    def _(step):
        for n in range(unroll):
            one(step * unroll + n)

    shape = (items, LANES)
    lane = iota(shape, 1)
    place = lane % 4
    low = jnp.where(place % 2 == 1, EDGE - 1, 0)
    high = (FACE - EDGE) % LANES + low
    source = jnp.where(place >= 2, high, low)
    found = [lane_pick(corner_buf[n], source) for n in range(4)]
    corner = lane % 8
    first = jnp.where(corner % 4 >= 2, found[1], found[0])
    last = jnp.where(corner % 4 >= 2, found[3], found[2])
    values = jnp.where(corner >= 4, last, first)
    row = iota(shape, 0)
    brick = jnp.zeros(shape, jnp.int32)
    for k in range(items):
        target = dest_ref[k] // slot_depth * bricks_group + tag_ref[k]
        brick = jnp.where(row == k, target, brick)
    placed = jnp.where(lane // 8 == row, values, 0.0)
    placed = jnp.where(lane == 8 * items + row, brick.astype(jnp.float32), placed)
    meta = jnp.sum(placed, axis=0, keepdims=True)
    last_lane = iota((1, LANES), 1) == LANES - 1
    if chunks != items * width:

        @pl.loop(0, chunks)
        def _(n):
            out_ref[pl.ds(n * (part_rows + 1) + part_rows, 1), :] = jnp.where(
                last_lane, -1.0, meta
            )

    for k in range(items):
        tagged = jnp.where(last_lane, tag_ref[k].astype(jnp.float32), meta)
        for part in range(width):
            out_ref[pl.ds(first_row(k, part) + part_rows, 1), :] = tagged


def group_kernel(items, bricks_dev, width, owners, shifts, in_ref, *outs):
    me = lax.axis_index("basis")
    part_rows = ROWS // width
    chunks = in_ref.shape[0] // (part_rows + 1)
    meta = [
        in_ref[n * (part_rows + 1) + part_rows : (n + 1) * (part_rows + 1), :]
        for n in range(chunks)
    ]
    tags = [
        jnp.broadcast_to(line[:, LANES - 1 :], (part_rows, LANES)) for line in meta
    ]
    for d in range(owners):
        for b in range(bricks_dev):
            brick = (owner_of(me, d, owners, width) * bricks_dev + b).astype(jnp.float32)
            total = jnp.zeros((part_rows, LANES), jnp.float32)
            for n in range(chunks):
                dens = in_ref[n * (part_rows + 1) : n * (part_rows + 1) + part_rows, :]
                total = total + jnp.where(tags[n] == brick, dens, 0.0)
            for out, shift in zip(outs, shifts):
                if shift == d:
                    out[b * part_rows : (b + 1) * part_rows, :] = total
    table_rows = outs[0].shape[0] - bricks_dev * part_rows
    shape = (TILE, LANES)
    lane = iota(shape, 1)
    lines = [jnp.zeros(shape, jnp.float32) for _ in range(table_rows)]
    for first in range(0, chunks, TILE):
        block = jnp.concatenate(meta[first : first + TILE], axis=0)
        for k in range(items):
            values = lane_pick(block, 8 * k + (lane & 7))
            brick = lane_pick(block, jnp.full(shape, 8 * items + k, jnp.int32)).astype(jnp.int32)
            values = jnp.where((brick & 15) == lane >> 3, values, 0.0)
            for r in range(table_rows):
                lines[r] = lines[r] + jnp.where(brick >> 4 == r, values, 0.0)
    table = jnp.concatenate([jnp.sum(line, axis=0, keepdims=True) for line in lines], axis=0)
    for out in outs:
        out[bricks_dev * part_rows :, :] = table


def map_kernel(cells_ref, out_ref):
    bricks_dev, cells = cells_ref.shape
    cell = (iota((LANES, cells), 1) + 1).astype(jnp.float32)
    for b in range(bricks_dev):
        position = cells_ref[b : b + 1, :]
        high = position >> SHIFT == iota((ROWS, cells), 0)
        low = (position & (LANES - 1)) == iota((LANES, cells), 0)
        found = lax.dot_general(
            high.astype(jnp.float32).astype(jnp.bfloat16),
            jnp.where(low, cell, 0.0).astype(jnp.bfloat16),
            (((1,), (1,)), ((), ())),
            preferred_element_type=jnp.float32,
        )
        out_ref[b] = found.astype(jnp.int32) - 1


def cell_kernel(width, shifts, *refs):
    *ins, map_ref, refs_ref, out_ref = refs
    bricks_dev, _, cells = refs_ref.shape
    part_rows = ROWS // width
    mine = lax.axis_index("basis") % width

    totals = []
    for offset in range(width):
        parts = [part for part, shift in zip(ins, shifts) if shift % width == offset]
        total = parts[0][...]
        for part in parts[1:]:
            total = total + part[...]
        totals.append(total)
    table = totals[0][bricks_dev * part_rows :]

    def own_points(b):
        halves = [total[b * part_rows : (b + 1) * part_rows] for total in totals]
        if width == 1:
            return halves[0]
        straight = jnp.concatenate(halves, axis=0)
        crossed = jnp.concatenate(halves[::-1], axis=0)
        return jnp.where(mine == 0, straight, crossed)

    chunk = (TILE, LANES)
    tiles = cells // LANES
    refs = [
        [refs_ref[b, :, c * LANES : (c + 1) * LANES] for c in range(tiles)]
        for b in range(bricks_dev)
    ]
    picked = [[jnp.zeros(chunk, jnp.float32) for _ in row] for row in refs]
    for r in range(table.shape[0]):
        line = jnp.broadcast_to(table[r : r + 1, :], chunk)
        for b in range(bricks_dev):
            for c, index in enumerate(refs[b]):
                found = lane_pick(line, (index & (LANES - 1)))
                picked[b][c] = jnp.where(index >> SHIFT == r, found, picked[b][c])
    for b in range(bricks_dev):
        cell = map_ref[b]
        mean = jnp.zeros((ROWS, LANES), jnp.float32)
        for c in range(tiles):
            line = jnp.sum(picked[b][c], axis=0, keepdims=True) * (0.5 / 8.0)
            found = lane_pick(jnp.broadcast_to(line, (ROWS, LANES)), (cell & (LANES - 1)))
            mean = jnp.where(cell >> SHIFT == c, found, mean)
        own = own_points(b)
        result = jnp.where(cell >= 0, 0.5 * own + mean, own)
        for row in range(ROWS):
            out_ref[b : b + 1, row * LANES : (row + 1) * LANES] = result[row : row + 1, :]


def owner_of(index, shift, owners, width):
    sets = owners // width
    pair, side = index // width, index % width
    jump, turn = divmod(shift, width)
    pair = pair ^ jump if sets & (sets - 1) == 0 else (pair + jump) % sets
    return pair * width + (side ^ turn)


def exchanges(owners, width):
    return [
        (d, [(i, owner_of(i, d, owners, width)) for i in range(owners)])
        for d in range(owners - 1, 0, -1)
    ]


def vmem():
    return pl.BlockSpec(memory_space=pltpu.VMEM)


def body(
    block_data, item_pairs, dest_slot, brick_tag, centres, exponents, levels, cell_pos, corner_refs
):
    groups = lax.axis_size("row") * lax.axis_size("col")
    owners = lax.axis_size("basis")
    items = block_data.shape[0]
    slot_depth = max(1, items // groups)
    slots = groups * slot_depth
    bricks = levels.shape[0]
    bricks_group = bricks // groups
    bricks_dev = bricks_group // owners
    table_rows = -(-bricks * 8 // (8 * LANES)) * 8
    basis = block_data.shape[1]
    width = 2 if owners % 2 == 0 else 1
    part_rows = ROWS // width
    chunks = slots * width
    params = pltpu.CompilerParams(vmem_limit_bytes=32 * 1024 * 1024)

    outgoing = pl.pallas_call(
        functools.partial(pair_kernel, slot_depth, width, bricks_group),
        out_shape=jax.ShapeDtypeStruct((chunks * (part_rows + 1), LANES), jnp.float32),
        in_specs=[pl.BlockSpec(memory_space=pltpu.HBM)] * 7,
        out_specs=vmem(),
        scratch_shapes=[
            pltpu.SMEM((2, items), jnp.int32),
            pltpu.SMEM((items,), jnp.int32),
            pltpu.SMEM((items,), jnp.int32),
            pltpu.SMEM((bricks,), jnp.int32),
            pltpu.VMEM(block_data.shape, block_data.dtype),
            pltpu.VMEM((2 * items, 3, 1, basis), jnp.float32),
            pltpu.VMEM((2 * items, 1, basis), jnp.float32),
            pltpu.VMEM((4, items, LANES), jnp.float32),
            pltpu.SemaphoreType.DMA((2, 2 * items)),
            pltpu.SemaphoreType.DMA((4,)),
            pltpu.SemaphoreType.DMA((items,)),
        ],
        compiler_params=params,
        name="pair_density",
    )(
        *(
            pltpu.with_memory_space_constraint(operand, pltpu.HBM)
            for operand in (
                item_pairs.T,
                dest_slot,
                brick_tag,
                levels,
                block_data,
                jnp.transpose(centres, (1, 0, 2)),
                exponents,
            )
        )
    )
    sets = [
        [g * owners + first + side for g in range(groups) for side in range(width)]
        for first in range(0, owners, width)
    ]
    arrived = lax.all_to_all(
        outgoing.reshape(chunks, 1, (part_rows + 1) * LANES),
        ("row", "col", "basis"),
        split_axis=0,
        concat_axis=0,
        tiled=True,
        axis_index_groups=sets,
    ).reshape(outgoing.shape)
    moves = exchanges(owners, width)
    shifts = [0] + [d for d, _ in moves]
    partial = pl.pallas_call(
        functools.partial(group_kernel, items, bricks_dev, width, owners, shifts),
        out_shape=[
            jax.ShapeDtypeStruct((bricks_dev * part_rows + table_rows, LANES), jnp.float32)
            for _ in shifts
        ],
        in_specs=[vmem()],
        out_specs=[vmem()] * len(shifts),
        compiler_params=params,
        name="group_sum",
    )(arrived)
    parts = [partial[0]] + [
        lax.ppermute(piece, "basis", pairs) for piece, (_, pairs) in zip(partial[1:], moves)
    ]
    cell_map = pl.pallas_call(
        map_kernel,
        out_shape=jax.ShapeDtypeStruct((bricks_dev, ROWS, LANES), jnp.int32),
        in_specs=[vmem()],
        out_specs=vmem(),
        compiler_params=params,
        cost_estimate=pl.CostEstimate(flops=4_000_000, bytes_accessed=200_000, transcendentals=0),
        name="cell_map",
    )(cell_pos)
    return pl.pallas_call(
        functools.partial(cell_kernel, width, shifts),
        out_shape=jax.ShapeDtypeStruct((bricks_dev, EDGE * FACE), jnp.float32),
        in_specs=[vmem()] * (len(parts) + 2),
        out_specs=vmem(),
        compiler_params=params,
        name="cells",
    )(*parts, cell_map, jnp.transpose(corner_refs, (0, 2, 1)))


def solution(mesh):
    split = ("row", "col", "basis")
    return jax.shard_map(
        body,
        mesh=mesh,
        in_specs=(
            P(split, None, None),
            P(split, None),
            P(split),
            P(split),
            P(),
            P(),
            P(),
            P(split, None),
            P(split, None, None),
        ),
        out_specs=P(split, None),
        check_vma=False,
    )
```

```python
import functools

import jax
import jax.numpy as jnp
from jax import lax
from jax.experimental import pallas as pl
from jax.experimental.pallas import tpu as pltpu
from jax.sharding import PartitionSpec as P

EDGE = 16
FACE = EDGE * EDGE
LANES = 128
SHIFT = 7
ROWS = EDGE * FACE // LANES
COARSE = 0.2
TILE = 8


def lane_pick(values, index):
    return jnp.take_along_axis(values, index, axis=1, mode="promise_in_bounds")


def iota(shape, axis):
    return lax.broadcasted_iota(jnp.int32, shape, axis)


def axis_factors(coords, middle, decay):
    return jnp.exp(-decay * (coords - middle) ** 2)


def pair_kernel(
    slot_depth,
    width,
    bricks_group,
    pairs_hbm,
    dest_hbm,
    tag_hbm,
    levels_hbm,
    blocks_hbm,
    centres_ref,
    exponents_ref,
    out_ref,
    pairs_ref,
    dest_ref,
    tag_ref,
    levels_ref,
    blocks_ref,
    centre_buf,
    decay_buf,
    corner_buf,
    sems,
    list_sems,
    block_sems,
):
    items = blocks_ref.shape[0]
    part_rows = ROWS // width
    chunks = out_ref.shape[0] // (part_rows + 1)
    lists = [
        pltpu.make_async_copy(source, target, list_sems.at[n])
        for n, (source, target) in enumerate(
            (
                (pairs_hbm, pairs_ref),
                (dest_hbm, dest_ref),
                (tag_hbm, tag_ref),
                (levels_hbm, levels_ref),
            )
        )
    ]
    for copy in lists:
        copy.start()

    def block_copy(k):
        return pltpu.make_async_copy(blocks_hbm.at[k], blocks_ref.at[k], block_sems.at[k])

    for k in range(items):
        block_copy(k).start()
    lists[0].wait()

    def copies(k, side):
        block = pairs_ref[side, k]
        at = 2 * k + side
        return (
            pltpu.make_async_copy(
                centres_ref.at[:, pl.ds(block, 1), :], centre_buf.at[at], sems.at[0, at]
            ),
            pltpu.make_async_copy(
                exponents_ref.at[pl.ds(block, 1), :], decay_buf.at[at], sems.at[1, at]
            ),
        )

    for k in range(items):
        for side in range(2):
            for copy in copies(k, side):
                copy.start()
    for copy in lists[1:]:
        copy.wait()
    if chunks != items * width:
        out_ref[...] = jnp.zeros_like(out_ref)

    def first_row(k, part):
        slot = dest_ref[k]
        chunk = (slot // slot_depth * width + part) * slot_depth + lax.rem(slot, slot_depth)
        return chunk * (part_rows + 1)

    steps = iota((EDGE, LANES), 0).astype(jnp.float32) - (EDGE - 1) / 2.0

    for k in range(items):
        for side in range(2):
            for copy in copies(k, side):
                copy.wait()
        block_copy(k).wait()

    def one(k):
        target = dest_ref[k] // slot_depth * bricks_group + tag_ref[k]
        spacing = jnp.where(levels_ref[target] == 1, COARSE * 0.5, COARSE)
        coords = steps * spacing

        def factors(side):
            at = 2 * k + side
            decay = decay_buf[at]
            found = [axis_factors(coords, centre_buf[at, d], decay) for d in range(3)]
            face = jnp.concatenate(
                [found[1][y : y + 1, :] * found[2] for y in range(EDGE)], axis=0
            )
            return found[0], face

        row_x, row_face = factors(0)
        col_x, col_face = factors(1)
        row_x = row_x.T
        row_face = row_face.T
        block = blocks_ref[k]
        for x in range(EDGE):
            col = (col_x[x : x + 1, :] * col_face).astype(jnp.bfloat16)
            product = lax.dot_general(
                block, col, (((1,), (1,)), ((), ())), preferred_element_type=jnp.float32
            )
            total = jnp.zeros((TILE, FACE), jnp.float32)
            for first in range(0, block.shape[0], TILE):
                rows = slice(first, first + TILE)
                total = total + row_x[rows, x : x + 1] * row_face[rows] * product[rows]
            dens = jnp.sum(total, axis=0, keepdims=True)
            for half in range(FACE // LANES):
                piece = dens[:, half * LANES : (half + 1) * LANES]
                part, row = divmod(2 * x + half, part_rows)
                out_ref[pl.ds(first_row(k, part) + row, 1), :] = piece
                if x in (0, EDGE - 1):
                    corner_buf[2 * (x // (EDGE - 1)) + half, pl.ds(k, 1), :] = piece

    unroll = 4 if items % 4 == 0 else 1

    @pl.loop(0, items // unroll)
    def _(step):
        for n in range(unroll):
            one(step * unroll + n)

    shape = (items, LANES)
    lane = iota(shape, 1)
    place = lane % 4
    low = jnp.where(place % 2 == 1, EDGE - 1, 0)
    high = (FACE - EDGE) % LANES + low
    source = jnp.where(place >= 2, high, low)
    found = [lane_pick(corner_buf[n], source) for n in range(4)]
    corner = lane % 8
    first = jnp.where(corner % 4 >= 2, found[1], found[0])
    last = jnp.where(corner % 4 >= 2, found[3], found[2])
    values = jnp.where(corner >= 4, last, first)
    row = iota(shape, 0)
    brick = jnp.zeros(shape, jnp.int32)
    for k in range(items):
        target = dest_ref[k] // slot_depth * bricks_group + tag_ref[k]
        brick = jnp.where(row == k, target, brick)
    placed = jnp.where(lane // 8 == row, values, 0.0)
    placed = jnp.where(lane == 8 * items + row, brick.astype(jnp.float32), placed)
    meta = jnp.sum(placed, axis=0, keepdims=True)
    last_lane = iota((1, LANES), 1) == LANES - 1
    if chunks != items * width:

        @pl.loop(0, chunks)
        def _(n):
            out_ref[pl.ds(n * (part_rows + 1) + part_rows, 1), :] = jnp.where(
                last_lane, -1.0, meta
            )

    for k in range(items):
        tagged = jnp.where(last_lane, tag_ref[k].astype(jnp.float32), meta)
        for part in range(width):
            out_ref[pl.ds(first_row(k, part) + part_rows, 1), :] = tagged


def group_kernel(items, bricks_dev, width, owners, shifts, in_ref, *outs):
    me = lax.axis_index("basis")
    part_rows = ROWS // width
    chunks = in_ref.shape[0] // (part_rows + 1)
    meta = [
        in_ref[n * (part_rows + 1) + part_rows : (n + 1) * (part_rows + 1), :]
        for n in range(chunks)
    ]
    tags = [
        jnp.broadcast_to(line[:, LANES - 1 :], (part_rows, LANES)) for line in meta
    ]
    for d in range(owners):
        for b in range(bricks_dev):
            brick = (owner_of(me, d, owners, width) * bricks_dev + b).astype(jnp.float32)
            total = jnp.zeros((part_rows, LANES), jnp.float32)
            for n in range(chunks):
                dens = in_ref[n * (part_rows + 1) : n * (part_rows + 1) + part_rows, :]
                total = total + jnp.where(tags[n] == brick, dens, 0.0)
            for out, shift in zip(outs, shifts):
                if shift == d:
                    out[b * part_rows : (b + 1) * part_rows, :] = total
    table_rows = outs[0].shape[0] - bricks_dev * part_rows
    shape = (TILE, LANES)
    lane = iota(shape, 1)
    lines = [jnp.zeros(shape, jnp.float32) for _ in range(table_rows)]
    for first in range(0, chunks, TILE):
        block = jnp.concatenate(meta[first : first + TILE], axis=0)
        for k in range(items):
            values = lane_pick(block, 8 * k + (lane & 7))
            brick = lane_pick(block, jnp.full(shape, 8 * items + k, jnp.int32)).astype(jnp.int32)
            values = jnp.where((brick & 15) == lane >> 3, values, 0.0)
            for r in range(table_rows):
                lines[r] = lines[r] + jnp.where(brick >> 4 == r, values, 0.0)
    table = jnp.concatenate([jnp.sum(line, axis=0, keepdims=True) for line in lines], axis=0)
    for out, shift in zip(outs, shifts):
        if shift % width == 0:
            out[bricks_dev * part_rows :, :] = table


def map_kernel(cells_ref, out_ref):
    bricks_dev, cells = cells_ref.shape
    cell = (iota((LANES, cells), 1) + 1).astype(jnp.float32)
    for b in range(bricks_dev):
        position = cells_ref[b : b + 1, :]
        high = position >> SHIFT == iota((ROWS, cells), 0)
        low = (position & (LANES - 1)) == iota((LANES, cells), 0)
        found = lax.dot_general(
            high.astype(jnp.float32).astype(jnp.bfloat16),
            jnp.where(low, cell, 0.0).astype(jnp.bfloat16),
            (((1,), (1,)), ((), ())),
            preferred_element_type=jnp.float32,
        )
        out_ref[b] = found.astype(jnp.int32) - 1


def cell_kernel(width, shifts, *refs):
    *ins, map_ref, refs_ref, out_ref = refs
    bricks_dev, _, cells = refs_ref.shape
    part_rows = ROWS // width
    mine = lax.axis_index("basis") % width

    totals = []
    for offset in range(width):
        parts = [part for part, shift in zip(ins, shifts) if shift % width == offset]
        total = parts[0][...]
        for part in parts[1:]:
            total = total + part[...]
        totals.append(total)
    table = totals[0][bricks_dev * part_rows :]

    def own_points(b):
        halves = [total[b * part_rows : (b + 1) * part_rows] for total in totals]
        if width == 1:
            return halves[0]
        straight = jnp.concatenate(halves, axis=0)
        crossed = jnp.concatenate(halves[::-1], axis=0)
        return jnp.where(mine == 0, straight, crossed)

    chunk = (TILE, LANES)
    tiles = cells // LANES
    refs = [
        [refs_ref[b, :, c * LANES : (c + 1) * LANES] for c in range(tiles)]
        for b in range(bricks_dev)
    ]
    picked = [[jnp.zeros(chunk, jnp.float32) for _ in row] for row in refs]
    for r in range(table.shape[0]):
        line = jnp.broadcast_to(table[r : r + 1, :], chunk)
        for b in range(bricks_dev):
            for c, index in enumerate(refs[b]):
                found = lane_pick(line, (index & (LANES - 1)))
                picked[b][c] = jnp.where(index >> SHIFT == r, found, picked[b][c])
    for b in range(bricks_dev):
        cell = map_ref[b]
        mean = jnp.zeros((ROWS, LANES), jnp.float32)
        for c in range(tiles):
            line = jnp.sum(picked[b][c], axis=0, keepdims=True) * (0.5 / 8.0)
            found = lane_pick(jnp.broadcast_to(line, (ROWS, LANES)), (cell & (LANES - 1)))
            mean = jnp.where(cell >> SHIFT == c, found, mean)
        own = own_points(b)
        result = jnp.where(cell >= 0, 0.5 * own + mean, own)
        for row in range(ROWS):
            out_ref[b : b + 1, row * LANES : (row + 1) * LANES] = result[row : row + 1, :]


def owner_of(index, shift, owners, width):
    sets = owners // width
    pair, side = index // width, index % width
    jump, turn = divmod(shift, width)
    pair = pair ^ jump if sets & (sets - 1) == 0 else (pair + jump) % sets
    return pair * width + (side ^ turn)


def exchanges(owners, width):
    return [
        (d, [(i, owner_of(i, d, owners, width)) for i in range(owners)])
        for d in range(owners - 1, 0, -1)
    ]


def vmem():
    return pl.BlockSpec(memory_space=pltpu.VMEM)


def body(
    block_data, item_pairs, dest_slot, brick_tag, centres, exponents, levels, cell_pos, corner_refs
):
    groups = lax.axis_size("row") * lax.axis_size("col")
    owners = lax.axis_size("basis")
    items = block_data.shape[0]
    slot_depth = max(1, items // groups)
    slots = groups * slot_depth
    bricks = levels.shape[0]
    bricks_group = bricks // groups
    bricks_dev = bricks_group // owners
    table_rows = -(-bricks * 8 // (8 * LANES)) * 8
    basis = block_data.shape[1]
    width = 1
    part_rows = ROWS // width
    chunks = slots * width
    params = pltpu.CompilerParams(vmem_limit_bytes=32 * 1024 * 1024)

    outgoing = pl.pallas_call(
        functools.partial(pair_kernel, slot_depth, width, bricks_group),
        out_shape=jax.ShapeDtypeStruct((chunks * (part_rows + 1), LANES), jnp.float32),
        in_specs=[pl.BlockSpec(memory_space=pltpu.HBM)] * 7,
        out_specs=vmem(),
        scratch_shapes=[
            pltpu.SMEM((2, items), jnp.int32),
            pltpu.SMEM((items,), jnp.int32),
            pltpu.SMEM((items,), jnp.int32),
            pltpu.SMEM((bricks,), jnp.int32),
            pltpu.VMEM(block_data.shape, block_data.dtype),
            pltpu.VMEM((2 * items, 3, 1, basis), jnp.float32),
            pltpu.VMEM((2 * items, 1, basis), jnp.float32),
            pltpu.VMEM((4, items, LANES), jnp.float32),
            pltpu.SemaphoreType.DMA((2, 2 * items)),
            pltpu.SemaphoreType.DMA((4,)),
            pltpu.SemaphoreType.DMA((items,)),
        ],
        compiler_params=params,
        name="pair_density",
    )(
        *(
            pltpu.with_memory_space_constraint(operand, pltpu.HBM)
            for operand in (
                item_pairs.T,
                dest_slot,
                brick_tag,
                levels,
                block_data,
                jnp.transpose(centres, (1, 0, 2)),
                exponents,
            )
        )
    )
    sets = [
        [g * owners + first + side for g in range(groups) for side in range(width)]
        for first in range(0, owners, width)
    ]
    arrived = lax.all_to_all(
        outgoing.reshape(chunks, 1, (part_rows + 1) * LANES),
        ("row", "col", "basis"),
        split_axis=0,
        concat_axis=0,
        tiled=True,
        axis_index_groups=sets,
    ).reshape(outgoing.shape)
    moves = exchanges(owners, width)
    shifts = [0] + [d for d, _ in moves]
    partial = pl.pallas_call(
        functools.partial(group_kernel, items, bricks_dev, width, owners, shifts),
        out_shape=[
            jax.ShapeDtypeStruct(
                (bricks_dev * part_rows + (0 if d % width else table_rows), LANES), jnp.float32
            )
            for d in shifts
        ],
        in_specs=[vmem()],
        out_specs=[vmem()] * len(shifts),
        compiler_params=params,
        name="group_sum",
    )(arrived)
    parts = [partial[0]] + [
        lax.ppermute(piece, "basis", pairs) for piece, (_, pairs) in zip(partial[1:], moves)
    ]
    cell_map = pl.pallas_call(
        map_kernel,
        out_shape=jax.ShapeDtypeStruct((bricks_dev, ROWS, LANES), jnp.int32),
        in_specs=[vmem()],
        out_specs=vmem(),
        compiler_params=params,
        cost_estimate=pl.CostEstimate(flops=4_000_000, bytes_accessed=200_000, transcendentals=0),
        name="cell_map",
    )(cell_pos)
    return pl.pallas_call(
        functools.partial(cell_kernel, width, shifts),
        out_shape=jax.ShapeDtypeStruct((bricks_dev, EDGE * FACE), jnp.float32),
        in_specs=[vmem()] * (len(parts) + 2),
        out_specs=vmem(),
        compiler_params=params,
        name="cells",
    )(*parts, cell_map, jnp.transpose(corner_refs, (0, 2, 1)))


def solution(mesh):
    split = ("row", "col", "basis")
    return jax.shard_map(
        body,
        mesh=mesh,
        in_specs=(
            P(split, None, None),
            P(split, None),
            P(split),
            P(split),
            P(),
            P(),
            P(),
            P(split, None),
            P(split, None, None),
        ),
        out_specs=P(split, None),
        check_vma=False,
    )
```

```python
import functools

import jax
import jax.numpy as jnp
from jax import lax
from jax.experimental import pallas as pl
from jax.experimental.pallas import tpu as pltpu
from jax.sharding import PartitionSpec as P

EDGE = 16
FACE = EDGE * EDGE
LANES = 128
SHIFT = 7
ROWS = EDGE * FACE // LANES
COARSE = 0.2
SLOT_ROWS = ROWS + 1
TILE = 8


def lane_pick(values, index):
    return jnp.take_along_axis(values, index, axis=1, mode="promise_in_bounds")


def iota(shape, axis):
    return lax.broadcasted_iota(jnp.int32, shape, axis)


def axis_factors(coords, middle, decay):
    return jnp.exp(-decay * (coords - middle) ** 2)


def pair_kernel(
    slot_depth,
    bricks_group,
    pairs_hbm,
    dest_hbm,
    tag_hbm,
    levels_hbm,
    blocks_hbm,
    centres_ref,
    exponents_ref,
    out_ref,
    pairs_ref,
    dest_ref,
    tag_ref,
    levels_ref,
    blocks_ref,
    centre_buf,
    decay_buf,
    corner_buf,
    sems,
    list_sems,
    block_sems,
):
    items = blocks_ref.shape[0]
    slots = out_ref.shape[0] // SLOT_ROWS
    lists = [
        pltpu.make_async_copy(source, target, list_sems.at[n])
        for n, (source, target) in enumerate(
            (
                (pairs_hbm, pairs_ref),
                (dest_hbm, dest_ref),
                (tag_hbm, tag_ref),
                (levels_hbm, levels_ref),
            )
        )
    ]
    for copy in lists:
        copy.start()

    def block_copy(k):
        return pltpu.make_async_copy(blocks_hbm.at[k], blocks_ref.at[k], block_sems.at[k])

    for k in range(items):
        block_copy(k).start()
    lists[0].wait()

    def copies(k, side):
        block = pairs_ref[side, k]
        at = 2 * k + side
        return (
            pltpu.make_async_copy(
                centres_ref.at[:, pl.ds(block, 1), :], centre_buf.at[at], sems.at[0, at]
            ),
            pltpu.make_async_copy(
                exponents_ref.at[pl.ds(block, 1), :], decay_buf.at[at], sems.at[1, at]
            ),
        )

    for k in range(items):
        for side in range(2):
            for copy in copies(k, side):
                copy.start()
    for copy in lists[1:]:
        copy.wait()
    if slots != items:
        out_ref[...] = jnp.zeros_like(out_ref)
    steps = iota((EDGE, LANES), 0).astype(jnp.float32) - (EDGE - 1) / 2.0

    for k in range(items):
        for side in range(2):
            for copy in copies(k, side):
                copy.wait()
        block_copy(k).wait()

    def one(k):
        target = dest_ref[k] // slot_depth * bricks_group + tag_ref[k]
        spacing = jnp.where(levels_ref[target] == 1, COARSE * 0.5, COARSE)
        coords = steps * spacing

        def factors(side):
            at = 2 * k + side
            decay = decay_buf[at]
            found = [axis_factors(coords, centre_buf[at, d], decay) for d in range(3)]
            face = jnp.concatenate(
                [found[1][y : y + 1, :] * found[2] for y in range(EDGE)], axis=0
            )
            return found[0], face

        row_x, row_face = factors(0)
        col_x, col_face = factors(1)
        row_face = row_face.T
        block = blocks_ref[k]
        for x in range(EDGE):
            col = (col_x[x : x + 1, :] * col_face).astype(jnp.bfloat16)
            product = lax.dot_general(
                block, col, (((1,), (1,)), ((), ())), preferred_element_type=jnp.float32
            )
            weight = jnp.broadcast_to(row_x[x : x + 1, :], (LANES, block.shape[0])).T
            weight = jnp.concatenate([weight] * (FACE // LANES), axis=1)
            dens = jnp.sum(weight * row_face * product, axis=0, keepdims=True)
            for half in range(FACE // LANES):
                piece = dens[:, half * LANES : (half + 1) * LANES]
                out_ref[pl.ds(dest_ref[k] * SLOT_ROWS + 2 * x + half, 1), :] = piece
                if x in (0, EDGE - 1):
                    corner_buf[2 * (x // (EDGE - 1)) + half, pl.ds(k, 1), :] = piece

    for k in range(items):
        one(k)

    shape = (items, LANES)
    lane = iota(shape, 1)
    place = lane % 4
    low = jnp.where(place % 2 == 1, EDGE - 1, 0)
    high = (FACE - EDGE) % LANES + low
    source = jnp.where(place >= 2, high, low)
    found = [lane_pick(corner_buf[n], source) for n in range(4)]
    corner = lane % 8
    first = jnp.where(corner % 4 >= 2, found[1], found[0])
    last = jnp.where(corner % 4 >= 2, found[3], found[2])
    values = jnp.where(corner >= 4, last, first)
    row = iota(shape, 0)
    brick = jnp.zeros(shape, jnp.int32)
    for k in range(items):
        target = dest_ref[k] // slot_depth * bricks_group + tag_ref[k]
        brick = jnp.where(row == k, target, brick)
    placed = jnp.where(lane // 8 == row, values, 0.0)
    placed = jnp.where(lane == 8 * items + row, brick.astype(jnp.float32), placed)
    meta = jnp.sum(placed, axis=0, keepdims=True)
    last_lane = iota((1, LANES), 1) == LANES - 1
    if slots != items:

        @pl.loop(0, slots)
        def _(n):
            out_ref[pl.ds(n * SLOT_ROWS + ROWS, 1), :] = jnp.where(last_lane, -1.0, meta)

    for k in range(items):
        tagged = jnp.where(last_lane, tag_ref[k].astype(jnp.float32), meta)
        out_ref[pl.ds(dest_ref[k] * SLOT_ROWS + ROWS, 1), :] = tagged


def group_kernel(items, bricks_dev, moves, in_ref, *outs):
    me = lax.axis_index("basis")
    slots = in_ref.shape[0] // SLOT_ROWS
    meta = [in_ref[n * SLOT_ROWS + ROWS : (n + 1) * SLOT_ROWS, :] for n in range(slots)]
    tags = [jnp.broadcast_to(line[:, LANES - 1 :], (ROWS, LANES)) for line in meta]
    for out, move in zip(outs, [range(len(outs)), *moves]):
        owner = sum(jnp.where(me == i, to, 0) for i, to in enumerate(move))
        for b in range(bricks_dev):
            brick = (owner * bricks_dev + b).astype(jnp.float32)
            total = jnp.zeros((ROWS, LANES), jnp.float32)
            for n in range(slots):
                dens = in_ref[n * SLOT_ROWS : n * SLOT_ROWS + ROWS, :]
                total = total + jnp.where(tags[n] == brick, dens, 0.0)
            out[b * ROWS : (b + 1) * ROWS, :] = total
    table_rows = outs[0].shape[0] - bricks_dev * ROWS
    shape = (TILE, LANES)
    lane = iota(shape, 1)
    lines = [jnp.zeros(shape, jnp.float32) for _ in range(table_rows)]
    for first in range(0, slots, TILE):
        block = jnp.concatenate(meta[first : first + TILE], axis=0)
        for k in range(items):
            values = lane_pick(block, 8 * k + (lane & 7))
            brick = lane_pick(block, jnp.full(shape, 8 * items + k, jnp.int32)).astype(jnp.int32)
            values = jnp.where((brick & 15) == lane >> 3, values, 0.0)
            for r in range(table_rows):
                lines[r] = lines[r] + jnp.where(brick >> 4 == r, values, 0.0)
    table = jnp.concatenate([jnp.sum(line, axis=0, keepdims=True) for line in lines], axis=0)
    for out in outs:
        out[bricks_dev * ROWS :, :] = table


def map_kernel(cells_ref, out_ref):
    bricks_dev, cells = cells_ref.shape
    cell = (iota((LANES, cells), 1) + 1).astype(jnp.float32)
    for b in range(bricks_dev):
        position = cells_ref[b : b + 1, :]
        high = position >> SHIFT == iota((ROWS, cells), 0)
        low = (position & (LANES - 1)) == iota((LANES, cells), 0)
        found = lax.dot_general(
            high.astype(jnp.float32).astype(jnp.bfloat16),
            jnp.where(low, cell, 0.0).astype(jnp.bfloat16),
            (((1,), (1,)), ((), ())),
            preferred_element_type=jnp.float32,
        )
        out_ref[b] = found.astype(jnp.int32) - 1


def cell_kernel(*refs):
    *ins, map_ref, refs_ref, out_ref = refs
    bricks_dev, _, cells = refs_ref.shape
    total = ins[0][...]
    for part in ins[1:]:
        total = total + part[...]
    table = total[bricks_dev * ROWS :]
    chunk = (TILE, LANES)
    tiles = cells // LANES
    refs = [
        [refs_ref[b, :, c * LANES : (c + 1) * LANES] for c in range(tiles)]
        for b in range(bricks_dev)
    ]
    picked = [[jnp.zeros(chunk, jnp.float32) for _ in row] for row in refs]
    for r in range(table.shape[0]):
        line = jnp.broadcast_to(table[r : r + 1, :], chunk)
        for b in range(bricks_dev):
            for c, index in enumerate(refs[b]):
                found = lane_pick(line, (index & (LANES - 1)))
                picked[b][c] = jnp.where(index >> SHIFT == r, found, picked[b][c])
    for b in range(bricks_dev):
        cell = map_ref[b]
        mean = jnp.zeros((ROWS, LANES), jnp.float32)
        for c in range(tiles):
            line = jnp.sum(picked[b][c], axis=0, keepdims=True) * (0.5 / 8.0)
            found = lane_pick(jnp.broadcast_to(line, (ROWS, LANES)), (cell & (LANES - 1)))
            mean = jnp.where(cell >> SHIFT == c, found, mean)
        own = total[b * ROWS : (b + 1) * ROWS]
        result = jnp.where(cell >= 0, 0.5 * own + mean, own)
        for row in range(ROWS):
            out_ref[b : b + 1, row * LANES : (row + 1) * LANES] = result[row : row + 1, :]


def moves_of(owners):
    if owners == 4:
        return [(2, 3, 1, 0), (3, 2, 0, 1), (1, 0, 3, 2)]
    return [tuple((i + d) % owners for i in range(owners)) for d in range(1, owners)]


def vmem():
    return pl.BlockSpec(memory_space=pltpu.VMEM)


def body(
    block_data, item_pairs, dest_slot, brick_tag, centres, exponents, levels, cell_pos, corner_refs
):
    groups = lax.axis_size("row") * lax.axis_size("col")
    owners = lax.axis_size("basis")
    items = block_data.shape[0]
    slot_depth = max(1, items // groups)
    slots = groups * slot_depth
    bricks = levels.shape[0]
    bricks_group = bricks // groups
    bricks_dev = bricks_group // owners
    table_rows = -(-bricks * 8 // (8 * LANES)) * 8
    basis = block_data.shape[1]
    params = pltpu.CompilerParams(vmem_limit_bytes=32 * 1024 * 1024)

    outgoing = pl.pallas_call(
        functools.partial(pair_kernel, slot_depth, bricks_group),
        out_shape=jax.ShapeDtypeStruct((slots * SLOT_ROWS, LANES), jnp.float32),
        in_specs=[pl.BlockSpec(memory_space=pltpu.HBM)] * 7,
        out_specs=vmem(),
        scratch_shapes=[
            pltpu.SMEM((2, items), jnp.int32),
            pltpu.SMEM((items,), jnp.int32),
            pltpu.SMEM((items,), jnp.int32),
            pltpu.SMEM((bricks,), jnp.int32),
            pltpu.VMEM(block_data.shape, block_data.dtype),
            pltpu.VMEM((2 * items, 3, 1, basis), jnp.float32),
            pltpu.VMEM((2 * items, 1, basis), jnp.float32),
            pltpu.VMEM((4, items, LANES), jnp.float32),
            pltpu.SemaphoreType.DMA((2, 2 * items)),
            pltpu.SemaphoreType.DMA((4,)),
            pltpu.SemaphoreType.DMA((items,)),
        ],
        compiler_params=params,
        name="pair_density",
    )(
        *(
            pltpu.with_memory_space_constraint(operand, pltpu.HBM)
            for operand in (
                item_pairs.T,
                dest_slot,
                brick_tag,
                levels,
                block_data,
                jnp.transpose(centres, (1, 0, 2)),
                exponents,
            )
        )
    )
    arrived = lax.all_to_all(
        outgoing.reshape(slots, 1, SLOT_ROWS * LANES),
        ("row", "col"),
        split_axis=0,
        concat_axis=0,
        tiled=True,
    ).reshape(outgoing.shape)
    moves = moves_of(owners)
    partial = pl.pallas_call(
        functools.partial(group_kernel, items, bricks_dev, moves),
        out_shape=[jax.ShapeDtypeStruct((bricks_dev * ROWS + table_rows, LANES), jnp.float32)]
        * owners,
        in_specs=[vmem()],
        out_specs=[vmem()] * owners,
        compiler_params=params,
        name="group_sum",
    )(arrived)
    parts = [partial[0]] + [
        lax.ppermute(piece, "basis", list(enumerate(move)))
        for piece, move in zip(partial[1:], moves)
    ]
    cell_map = pl.pallas_call(
        map_kernel,
        out_shape=jax.ShapeDtypeStruct((bricks_dev, ROWS, LANES), jnp.int32),
        in_specs=[vmem()],
        out_specs=vmem(),
        compiler_params=params,
        cost_estimate=pl.CostEstimate(flops=4_000_000, bytes_accessed=200_000, transcendentals=0),
        name="cell_map",
    )(cell_pos)
    return pl.pallas_call(
        cell_kernel,
        out_shape=jax.ShapeDtypeStruct((bricks_dev, EDGE * FACE), jnp.float32),
        in_specs=[vmem()] * (len(parts) + 2),
        out_specs=vmem(),
        compiler_params=params,
        name="cells",
    )(*parts, cell_map, jnp.transpose(corner_refs, (0, 2, 1)))


def solution(mesh):
    split = ("row", "col", "basis")
    return jax.shard_map(
        body,
        mesh=mesh,
        in_specs=(
            P(split, None, None),
            P(split, None),
            P(split),
            P(split),
            P(),
            P(),
            P(),
            P(split, None),
            P(split, None, None),
        ),
        out_specs=P(split, None),
        check_vma=False,
    )
```

```python
import functools

import jax
import jax.numpy as jnp
from jax import lax
from jax.experimental import pallas as pl
from jax.experimental.pallas import tpu as pltpu
from jax.sharding import PartitionSpec as P

EDGE = 16
FACE = EDGE * EDGE
LANES = 128
SHIFT = 7
ROWS = EDGE * FACE // LANES
COARSE = 0.2
SLOT_ROWS = ROWS + 1
TILE = 8


def lane_pick(values, index):
    return jnp.take_along_axis(values, index, axis=1, mode="promise_in_bounds")


def iota(shape, axis):
    return lax.broadcasted_iota(jnp.int32, shape, axis)


def axis_factors(coords, middle, decay):
    return jnp.exp(-decay * (coords - middle) ** 2)


def pair_kernel(
    slot_depth,
    bricks_group,
    pairs_hbm,
    dest_hbm,
    tag_hbm,
    levels_hbm,
    blocks_hbm,
    centres_hbm,
    exponents_hbm,
    out_ref,
    pairs_ref,
    dest_ref,
    tag_ref,
    levels_ref,
    blocks_ref,
    centres_ref,
    exponents_ref,
    corner_buf,
    list_sems,
    table_sems,
):
    items = blocks_ref.shape[0]
    slots = out_ref.shape[0] // SLOT_ROWS
    lists = [
        pltpu.make_async_copy(source, target, list_sems.at[n])
        for n, (source, target) in enumerate(
            (
                (pairs_hbm, pairs_ref),
                (dest_hbm, dest_ref),
                (tag_hbm, tag_ref),
                (levels_hbm, levels_ref),
            )
        )
    ]
    for copy in lists:
        copy.start()

    tables = [
        pltpu.make_async_copy(centres_hbm.at[d], centres_ref.at[d], table_sems.at[d])
        for d in range(3)
    ]
    tables.append(pltpu.make_async_copy(exponents_hbm, exponents_ref, table_sems.at[3]))
    tables.append(pltpu.make_async_copy(blocks_hbm, blocks_ref, table_sems.at[4]))
    for copy in tables:
        copy.start()
    for copy in lists + tables:
        copy.wait()
    if slots != items:
        out_ref[...] = jnp.zeros_like(out_ref)
    steps = iota((EDGE, LANES), 0).astype(jnp.float32) - (EDGE - 1) / 2.0

    def one(k):
        target = dest_ref[k] // slot_depth * bricks_group + tag_ref[k]
        spacing = jnp.where(levels_ref[target] == 1, COARSE * 0.5, COARSE)
        coords = steps * spacing

        def factors(side):
            row = pl.ds(pairs_ref[side, k], 1)
            decay = exponents_ref[row, :]
            found = [axis_factors(coords, centres_ref[d, row, :], decay) for d in range(3)]
            face = jnp.concatenate(
                [found[1][y : y + 1, :] * found[2] for y in range(EDGE)], axis=0
            )
            return found[0], face

        row_x, row_face = factors(0)
        col_x, col_face = factors(1)
        row_face = row_face.T
        block = blocks_ref[k]
        for x in range(EDGE):
            col = (col_x[x : x + 1, :] * col_face).astype(jnp.bfloat16)
            product = lax.dot_general(
                block, col, (((1,), (1,)), ((), ())), preferred_element_type=jnp.float32
            )
            weight = jnp.broadcast_to(row_x[x : x + 1, :], (LANES, block.shape[0])).T
            weight = jnp.concatenate([weight] * (FACE // LANES), axis=1)
            dens = jnp.sum(weight * row_face * product, axis=0, keepdims=True)
            for half in range(FACE // LANES):
                piece = dens[:, half * LANES : (half + 1) * LANES]
                out_ref[pl.ds(dest_ref[k] * SLOT_ROWS + 2 * x + half, 1), :] = piece
                if x in (0, EDGE - 1):
                    corner_buf[2 * (x // (EDGE - 1)) + half, pl.ds(k, 1), :] = piece

    for k in range(items):
        one(k)

    shape = (items, LANES)
    lane = iota(shape, 1)
    place = lane % 4
    low = jnp.where(place % 2 == 1, EDGE - 1, 0)
    high = (FACE - EDGE) % LANES + low
    source = jnp.where(place >= 2, high, low)
    found = [lane_pick(corner_buf[n], source) for n in range(4)]
    corner = lane % 8
    first = jnp.where(corner % 4 >= 2, found[1], found[0])
    last = jnp.where(corner % 4 >= 2, found[3], found[2])
    values = jnp.where(corner >= 4, last, first)
    row = iota(shape, 0)
    brick = jnp.zeros(shape, jnp.int32)
    for k in range(items):
        target = dest_ref[k] // slot_depth * bricks_group + tag_ref[k]
        brick = jnp.where(row == k, target, brick)
    placed = jnp.where(lane // 8 == row, values, 0.0)
    placed = jnp.where(lane == 8 * items + row, brick.astype(jnp.float32), placed)
    meta = jnp.sum(placed, axis=0, keepdims=True)
    last_lane = iota((1, LANES), 1) == LANES - 1
    if slots != items:

        @pl.loop(0, slots)
        def _(n):
            out_ref[pl.ds(n * SLOT_ROWS + ROWS, 1), :] = jnp.where(last_lane, -1.0, meta)

    for k in range(items):
        tagged = jnp.where(last_lane, tag_ref[k].astype(jnp.float32), meta)
        out_ref[pl.ds(dest_ref[k] * SLOT_ROWS + ROWS, 1), :] = tagged


def group_kernel(items, bricks_dev, moves, in_ref, *outs):
    me = lax.axis_index("basis")
    slots = in_ref.shape[0] // SLOT_ROWS
    meta = [in_ref[n * SLOT_ROWS + ROWS : (n + 1) * SLOT_ROWS, :] for n in range(slots)]
    tags = [jnp.broadcast_to(line[:, LANES - 1 :], (ROWS, LANES)) for line in meta]
    for out, move in zip(outs, [range(len(outs)), *moves]):
        owner = sum(jnp.where(me == i, to, 0) for i, to in enumerate(move))
        for b in range(bricks_dev):
            brick = (owner * bricks_dev + b).astype(jnp.float32)
            total = jnp.zeros((ROWS, LANES), jnp.float32)
            for n in range(slots):
                dens = in_ref[n * SLOT_ROWS : n * SLOT_ROWS + ROWS, :]
                total = total + jnp.where(tags[n] == brick, dens, 0.0)
            out[b * ROWS : (b + 1) * ROWS, :] = total
    table_rows = outs[0].shape[0] - bricks_dev * ROWS
    shape = (TILE, LANES)
    lane = iota(shape, 1)
    lines = [jnp.zeros(shape, jnp.float32) for _ in range(table_rows)]
    for first in range(0, slots, TILE):
        block = jnp.concatenate(meta[first : first + TILE], axis=0)
        for k in range(items):
            values = lane_pick(block, 8 * k + (lane & 7))
            brick = lane_pick(block, jnp.full(shape, 8 * items + k, jnp.int32)).astype(jnp.int32)
            values = jnp.where((brick & 15) == lane >> 3, values, 0.0)
            for r in range(table_rows):
                lines[r] = lines[r] + jnp.where(brick >> 4 == r, values, 0.0)
    table = jnp.concatenate([jnp.sum(line, axis=0, keepdims=True) for line in lines], axis=0)
    for out in outs:
        out[bricks_dev * ROWS :, :] = table


def map_kernel(cells_ref, out_ref):
    bricks_dev, cells = cells_ref.shape
    cell = (iota((LANES, cells), 1) + 1).astype(jnp.float32)
    for b in range(bricks_dev):
        position = cells_ref[b : b + 1, :]
        high = position >> SHIFT == iota((ROWS, cells), 0)
        low = (position & (LANES - 1)) == iota((LANES, cells), 0)
        found = lax.dot_general(
            high.astype(jnp.float32).astype(jnp.bfloat16),
            jnp.where(low, cell, 0.0).astype(jnp.bfloat16),
            (((1,), (1,)), ((), ())),
            preferred_element_type=jnp.float32,
        )
        out_ref[b] = found.astype(jnp.int32) - 1


def cell_kernel(*refs):
    *ins, map_ref, refs_ref, out_ref = refs
    bricks_dev, _, cells = refs_ref.shape
    total = ins[0][...]
    for part in ins[1:]:
        total = total + part[...]
    table = total[bricks_dev * ROWS :]
    chunk = (TILE, LANES)
    tiles = cells // LANES
    refs = [
        [refs_ref[b, :, c * LANES : (c + 1) * LANES] for c in range(tiles)]
        for b in range(bricks_dev)
    ]
    picked = [[jnp.zeros(chunk, jnp.float32) for _ in row] for row in refs]
    for r in range(table.shape[0]):
        line = jnp.broadcast_to(table[r : r + 1, :], chunk)
        for b in range(bricks_dev):
            for c, index in enumerate(refs[b]):
                found = lane_pick(line, (index & (LANES - 1)))
                picked[b][c] = jnp.where(index >> SHIFT == r, found, picked[b][c])
    for b in range(bricks_dev):
        cell = map_ref[b]
        mean = jnp.zeros((ROWS, LANES), jnp.float32)
        for c in range(tiles):
            line = jnp.sum(picked[b][c], axis=0, keepdims=True) * (0.5 / 8.0)
            found = lane_pick(jnp.broadcast_to(line, (ROWS, LANES)), (cell & (LANES - 1)))
            mean = jnp.where(cell >> SHIFT == c, found, mean)
        own = total[b * ROWS : (b + 1) * ROWS]
        result = jnp.where(cell >= 0, 0.5 * own + mean, own)
        for row in range(ROWS):
            out_ref[b : b + 1, row * LANES : (row + 1) * LANES] = result[row : row + 1, :]


def moves_of(owners):
    if owners == 4:
        return [(2, 3, 1, 0), (3, 2, 0, 1), (1, 0, 3, 2)]
    return [tuple((i + d) % owners for i in range(owners)) for d in range(1, owners)]


def vmem():
    return pl.BlockSpec(memory_space=pltpu.VMEM)


def body(
    block_data, item_pairs, dest_slot, brick_tag, centres, exponents, levels, cell_pos, corner_refs
):
    groups = lax.axis_size("row") * lax.axis_size("col")
    owners = lax.axis_size("basis")
    items = block_data.shape[0]
    slot_depth = max(1, items // groups)
    slots = groups * slot_depth
    bricks = levels.shape[0]
    bricks_group = bricks // groups
    bricks_dev = bricks_group // owners
    table_rows = -(-bricks * 8 // (8 * LANES)) * 8
    basis = block_data.shape[1]
    params = pltpu.CompilerParams(vmem_limit_bytes=32 * 1024 * 1024)

    outgoing = pl.pallas_call(
        functools.partial(pair_kernel, slot_depth, bricks_group),
        out_shape=jax.ShapeDtypeStruct((slots * SLOT_ROWS, LANES), jnp.float32),
        in_specs=[pl.BlockSpec(memory_space=pltpu.HBM)] * 7,
        out_specs=vmem(),
        scratch_shapes=[
            pltpu.SMEM((2, items), jnp.int32),
            pltpu.SMEM((items,), jnp.int32),
            pltpu.SMEM((items,), jnp.int32),
            pltpu.SMEM((bricks,), jnp.int32),
            pltpu.VMEM(block_data.shape, block_data.dtype),
            pltpu.VMEM((3, centres.shape[0], basis), jnp.float32),
            pltpu.VMEM(exponents.shape, jnp.float32),
            pltpu.VMEM((4, items, LANES), jnp.float32),
            pltpu.SemaphoreType.DMA((4,)),
            pltpu.SemaphoreType.DMA((5,)),
        ],
        compiler_params=params,
        name="pair_density",
    )(
        *(
            pltpu.with_memory_space_constraint(operand, pltpu.HBM)
            for operand in (
                item_pairs.T,
                dest_slot,
                brick_tag,
                levels,
                block_data,
                jnp.transpose(centres, (1, 0, 2)),
                exponents,
            )
        )
    )
    arrived = lax.all_to_all(
        outgoing.reshape(slots, 1, SLOT_ROWS * LANES),
        ("row", "col"),
        split_axis=0,
        concat_axis=0,
        tiled=True,
    ).reshape(outgoing.shape)
    moves = moves_of(owners)
    partial = pl.pallas_call(
        functools.partial(group_kernel, items, bricks_dev, moves),
        out_shape=[jax.ShapeDtypeStruct((bricks_dev * ROWS + table_rows, LANES), jnp.float32)]
        * owners,
        in_specs=[vmem()],
        out_specs=[vmem()] * owners,
        compiler_params=params,
        name="group_sum",
    )(arrived)
    parts = [partial[0]] + [
        lax.ppermute(piece, "basis", list(enumerate(move)))
        for piece, move in zip(partial[1:], moves)
    ]
    cell_map = pl.pallas_call(
        map_kernel,
        out_shape=jax.ShapeDtypeStruct((bricks_dev, ROWS, LANES), jnp.int32),
        in_specs=[vmem()],
        out_specs=vmem(),
        compiler_params=params,
        cost_estimate=pl.CostEstimate(flops=4_000_000, bytes_accessed=200_000, transcendentals=0),
        name="cell_map",
    )(cell_pos)
    return pl.pallas_call(
        cell_kernel,
        out_shape=jax.ShapeDtypeStruct((bricks_dev, EDGE * FACE), jnp.float32),
        in_specs=[vmem()] * (len(parts) + 2),
        out_specs=vmem(),
        compiler_params=params,
        name="cells",
    )(*parts, cell_map, jnp.transpose(corner_refs, (0, 2, 1)))


def solution(mesh):
    split = ("row", "col", "basis")
    return jax.shard_map(
        body,
        mesh=mesh,
        in_specs=(
            P(split, None, None),
            P(split, None),
            P(split),
            P(split),
            P(),
            P(),
            P(),
            P(split, None),
            P(split, None, None),
        ),
        out_specs=P(split, None),
        check_vma=False,
    )
```

```python
import functools

import jax
import jax.numpy as jnp
from jax import lax
from jax.experimental import pallas as pl
from jax.experimental.pallas import tpu as pltpu
from jax.sharding import PartitionSpec as P

EDGE = 16
FACE = EDGE * EDGE
LANES = 128
SHIFT = 7
ROWS = EDGE * FACE // LANES
COARSE = 0.2
SLOT_ROWS = ROWS + 1
TILE = 8


def lane_pick(values, index):
    return jnp.take_along_axis(values, index, axis=1, mode="promise_in_bounds")


def iota(shape, axis):
    return lax.broadcasted_iota(jnp.int32, shape, axis)


def axis_factors(coords, middle, decay):
    return jnp.exp(-decay * (coords - middle) ** 2)


def pair_kernel(
    slot_depth,
    bricks_group,
    pairs_hbm,
    dest_hbm,
    tag_hbm,
    levels_hbm,
    blocks_hbm,
    centres_hbm,
    exponents_hbm,
    out_ref,
    pairs_ref,
    dest_ref,
    tag_ref,
    levels_ref,
    blocks_ref,
    centres_ref,
    exponents_ref,
    corner_buf,
    list_sems,
    table_sems,
    block_sem,
):
    items = blocks_ref.shape[0]
    slots = out_ref.shape[0] // SLOT_ROWS
    lists = [
        pltpu.make_async_copy(source, target, list_sems.at[n])
        for n, (source, target) in enumerate(
            (
                (pairs_hbm, pairs_ref),
                (dest_hbm, dest_ref),
                (tag_hbm, tag_ref),
                (levels_hbm, levels_ref),
            )
        )
    ]
    for copy in lists:
        copy.start()

    pieces = 4
    rows = exponents_ref.shape[0] // pieces
    tables = []
    for n in range(pieces):
        part = pl.ds(n * rows, rows)
        tables.append((exponents_hbm.at[part], exponents_ref.at[part]))
        tables.extend((centres_hbm.at[d, part], centres_ref.at[d, part]) for d in range(3))
    tables = [
        pltpu.make_async_copy(source, target, table_sems.at[n])
        for n, (source, target) in enumerate(tables)
    ]
    blocks = pltpu.make_async_copy(blocks_hbm, blocks_ref, block_sem)
    for copy in tables + [blocks]:
        copy.start()
    for copy in lists + tables:
        copy.wait()
    if slots != items:
        out_ref[...] = jnp.zeros_like(out_ref)
    steps = iota((EDGE, LANES), 0).astype(jnp.float32) - (EDGE - 1) / 2.0

    def one(k):
        target = dest_ref[k] // slot_depth * bricks_group + tag_ref[k]
        spacing = jnp.where(levels_ref[target] == 1, COARSE * 0.5, COARSE)
        coords = steps * spacing

        def factors(side):
            row = pl.ds(pairs_ref[side, k], 1)
            decay = exponents_ref[row, :]
            found = [axis_factors(coords, centres_ref[d, row, :], decay) for d in range(3)]
            face = jnp.concatenate(
                [found[1][y : y + 1, :] * found[2] for y in range(EDGE)], axis=0
            )
            return found[0], face

        row_x, row_face = factors(0)
        col_x, col_face = factors(1)
        row_face = row_face.T
        if k == 0:
            blocks.wait()
        block = blocks_ref[k]
        for x in range(EDGE):
            col = (col_x[x : x + 1, :] * col_face).astype(jnp.bfloat16)
            product = lax.dot_general(
                block, col, (((1,), (1,)), ((), ())), preferred_element_type=jnp.float32
            )
            weight = jnp.broadcast_to(row_x[x : x + 1, :], (LANES, block.shape[0])).T
            weight = jnp.concatenate([weight] * (FACE // LANES), axis=1)
            dens = jnp.sum(weight * row_face * product, axis=0, keepdims=True)
            for half in range(FACE // LANES):
                piece = dens[:, half * LANES : (half + 1) * LANES]
                out_ref[pl.ds(dest_ref[k] * SLOT_ROWS + 2 * x + half, 1), :] = piece
                if x in (0, EDGE - 1):
                    corner_buf[2 * (x // (EDGE - 1)) + half, pl.ds(k, 1), :] = piece

    for k in range(items):
        one(k)

    shape = (items, LANES)
    lane = iota(shape, 1)
    place = lane % 4
    low = jnp.where(place % 2 == 1, EDGE - 1, 0)
    high = (FACE - EDGE) % LANES + low
    source = jnp.where(place >= 2, high, low)
    found = [lane_pick(corner_buf[n], source) for n in range(4)]
    corner = lane % 8
    first = jnp.where(corner % 4 >= 2, found[1], found[0])
    last = jnp.where(corner % 4 >= 2, found[3], found[2])
    values = jnp.where(corner >= 4, last, first)
    row = iota(shape, 0)
    brick = jnp.zeros(shape, jnp.int32)
    for k in range(items):
        target = dest_ref[k] // slot_depth * bricks_group + tag_ref[k]
        brick = jnp.where(row == k, target, brick)
    placed = jnp.where(lane // 8 == row, values, 0.0)
    placed = jnp.where(lane == 8 * items + row, brick.astype(jnp.float32), placed)
    meta = jnp.sum(placed, axis=0, keepdims=True)
    last_lane = iota((1, LANES), 1) == LANES - 1
    if slots != items:

        @pl.loop(0, slots)
        def _(n):
            out_ref[pl.ds(n * SLOT_ROWS + ROWS, 1), :] = jnp.where(last_lane, -1.0, meta)

    for k in range(items):
        tagged = jnp.where(last_lane, tag_ref[k].astype(jnp.float32), meta)
        out_ref[pl.ds(dest_ref[k] * SLOT_ROWS + ROWS, 1), :] = tagged


def group_kernel(items, bricks_dev, moves, in_ref, *outs):
    me = lax.axis_index("basis")
    slots = in_ref.shape[0] // SLOT_ROWS
    meta = [in_ref[n * SLOT_ROWS + ROWS : (n + 1) * SLOT_ROWS, :] for n in range(slots)]
    tags = [jnp.broadcast_to(line[:, LANES - 1 :], (ROWS, LANES)) for line in meta]
    for out, move in zip(outs, [range(len(outs)), *moves]):
        owner = sum(jnp.where(me == i, to, 0) for i, to in enumerate(move))
        for b in range(bricks_dev):
            brick = (owner * bricks_dev + b).astype(jnp.float32)
            total = jnp.zeros((ROWS, LANES), jnp.float32)
            for n in range(slots):
                dens = in_ref[n * SLOT_ROWS : n * SLOT_ROWS + ROWS, :]
                total = total + jnp.where(tags[n] == brick, dens, 0.0)
            out[b * ROWS : (b + 1) * ROWS, :] = total
    table_rows = outs[0].shape[0] - bricks_dev * ROWS
    shape = (TILE, LANES)
    lane = iota(shape, 1)
    lines = [jnp.zeros(shape, jnp.float32) for _ in range(table_rows)]
    for first in range(0, slots, TILE):
        block = jnp.concatenate(meta[first : first + TILE], axis=0)
        for k in range(items):
            values = lane_pick(block, 8 * k + (lane & 7))
            brick = lane_pick(block, jnp.full(shape, 8 * items + k, jnp.int32)).astype(jnp.int32)
            values = jnp.where((brick & 15) == lane >> 3, values, 0.0)
            for r in range(table_rows):
                lines[r] = lines[r] + jnp.where(brick >> 4 == r, values, 0.0)
    table = jnp.concatenate([jnp.sum(line, axis=0, keepdims=True) for line in lines], axis=0)
    for out in outs:
        out[bricks_dev * ROWS :, :] = table


def map_kernel(cells_ref, out_ref):
    bricks_dev, cells = cells_ref.shape
    cell = (iota((LANES, cells), 1) + 1).astype(jnp.float32)
    for b in range(bricks_dev):
        position = cells_ref[b : b + 1, :]
        high = position >> SHIFT == iota((ROWS, cells), 0)
        low = (position & (LANES - 1)) == iota((LANES, cells), 0)
        found = lax.dot_general(
            high.astype(jnp.float32).astype(jnp.bfloat16),
            jnp.where(low, cell, 0.0).astype(jnp.bfloat16),
            (((1,), (1,)), ((), ())),
            preferred_element_type=jnp.float32,
        )
        out_ref[b] = found.astype(jnp.int32) - 1


def cell_kernel(*refs):
    *ins, map_ref, refs_ref, out_ref = refs
    bricks_dev, _, cells = refs_ref.shape
    total = ins[0][...]
    for part in ins[1:]:
        total = total + part[...]
    table = total[bricks_dev * ROWS :]
    chunk = (TILE, LANES)
    tiles = cells // LANES
    refs = [
        [refs_ref[b, :, c * LANES : (c + 1) * LANES] for c in range(tiles)]
        for b in range(bricks_dev)
    ]
    picked = [[jnp.zeros(chunk, jnp.float32) for _ in row] for row in refs]
    for r in range(table.shape[0]):
        line = jnp.broadcast_to(table[r : r + 1, :], chunk)
        for b in range(bricks_dev):
            for c, index in enumerate(refs[b]):
                found = lane_pick(line, (index & (LANES - 1)))
                picked[b][c] = jnp.where(index >> SHIFT == r, found, picked[b][c])
    for b in range(bricks_dev):
        cell = map_ref[b]
        mean = jnp.zeros((ROWS, LANES), jnp.float32)
        for c in range(tiles):
            line = jnp.sum(picked[b][c], axis=0, keepdims=True) * (0.5 / 8.0)
            found = lane_pick(jnp.broadcast_to(line, (ROWS, LANES)), (cell & (LANES - 1)))
            mean = jnp.where(cell >> SHIFT == c, found, mean)
        own = total[b * ROWS : (b + 1) * ROWS]
        result = jnp.where(cell >= 0, 0.5 * own + mean, own)
        for row in range(ROWS):
            out_ref[b : b + 1, row * LANES : (row + 1) * LANES] = result[row : row + 1, :]


def moves_of(owners):
    if owners == 4:
        return [(2, 3, 1, 0), (3, 2, 0, 1), (1, 0, 3, 2)]
    return [tuple((i + d) % owners for i in range(owners)) for d in range(1, owners)]


def vmem():
    return pl.BlockSpec(memory_space=pltpu.VMEM)


def body(
    block_data, item_pairs, dest_slot, brick_tag, centres, exponents, levels, cell_pos, corner_refs
):
    groups = lax.axis_size("row") * lax.axis_size("col")
    owners = lax.axis_size("basis")
    items = block_data.shape[0]
    slot_depth = max(1, items // groups)
    slots = groups * slot_depth
    bricks = levels.shape[0]
    bricks_group = bricks // groups
    bricks_dev = bricks_group // owners
    table_rows = -(-bricks * 8 // (8 * LANES)) * 8
    basis = block_data.shape[1]
    params = pltpu.CompilerParams(vmem_limit_bytes=32 * 1024 * 1024)

    outgoing = pl.pallas_call(
        functools.partial(pair_kernel, slot_depth, bricks_group),
        out_shape=jax.ShapeDtypeStruct((slots * SLOT_ROWS, LANES), jnp.float32),
        in_specs=[pl.BlockSpec(memory_space=pltpu.HBM)] * 7,
        out_specs=vmem(),
        scratch_shapes=[
            pltpu.SMEM((2, items), jnp.int32),
            pltpu.SMEM((items,), jnp.int32),
            pltpu.SMEM((items,), jnp.int32),
            pltpu.SMEM((bricks,), jnp.int32),
            pltpu.VMEM(block_data.shape, block_data.dtype),
            pltpu.VMEM((3, centres.shape[0], basis), jnp.float32),
            pltpu.VMEM(exponents.shape, jnp.float32),
            pltpu.VMEM((4, items, LANES), jnp.float32),
            pltpu.SemaphoreType.DMA((4,)),
            pltpu.SemaphoreType.DMA((16,)),
            pltpu.SemaphoreType.DMA,
        ],
        compiler_params=params,
        name="pair_density",
    )(
        *(
            pltpu.with_memory_space_constraint(operand, pltpu.HBM)
            for operand in (
                item_pairs.T,
                dest_slot,
                brick_tag,
                levels,
                block_data,
                jnp.transpose(centres, (1, 0, 2)),
                exponents,
            )
        )
    )
    arrived = lax.all_to_all(
        outgoing.reshape(slots, 1, SLOT_ROWS * LANES),
        ("row", "col"),
        split_axis=0,
        concat_axis=0,
        tiled=True,
    ).reshape(outgoing.shape)
    moves = moves_of(owners)
    partial = pl.pallas_call(
        functools.partial(group_kernel, items, bricks_dev, moves),
        out_shape=[jax.ShapeDtypeStruct((bricks_dev * ROWS + table_rows, LANES), jnp.float32)]
        * owners,
        in_specs=[vmem()],
        out_specs=[vmem()] * owners,
        compiler_params=params,
        name="group_sum",
    )(arrived)
    parts = [partial[0]] + [
        lax.ppermute(piece, "basis", list(enumerate(move)))
        for piece, move in zip(partial[1:], moves)
    ]
    cell_map = pl.pallas_call(
        map_kernel,
        out_shape=jax.ShapeDtypeStruct((bricks_dev, ROWS, LANES), jnp.int32),
        in_specs=[vmem()],
        out_specs=vmem(),
        compiler_params=params,
        cost_estimate=pl.CostEstimate(flops=4_000_000, bytes_accessed=200_000, transcendentals=0),
        name="cell_map",
    )(cell_pos)
    return pl.pallas_call(
        cell_kernel,
        out_shape=jax.ShapeDtypeStruct((bricks_dev, EDGE * FACE), jnp.float32),
        in_specs=[vmem()] * (len(parts) + 2),
        out_specs=vmem(),
        compiler_params=params,
        name="cells",
    )(*parts, cell_map, jnp.transpose(corner_refs, (0, 2, 1)))


def solution(mesh):
    split = ("row", "col", "basis")
    return jax.shard_map(
        body,
        mesh=mesh,
        in_specs=(
            P(split, None, None),
            P(split, None),
            P(split),
            P(split),
            P(),
            P(),
            P(),
            P(split, None),
            P(split, None, None),
        ),
        out_specs=P(split, None),
        check_vma=False,
    )
```

```python
import functools

import jax
import jax.numpy as jnp
from jax import lax
from jax.experimental import pallas as pl
from jax.experimental.pallas import tpu as pltpu
from jax.sharding import PartitionSpec as P

EDGE = 16
FACE = EDGE * EDGE
LANES = 128
SHIFT = 7
ROWS = EDGE * FACE // LANES
COARSE = 0.2
SLOT_ROWS = ROWS + 1
TILE = 8


def lane_pick(values, index):
    return jnp.take_along_axis(values, index, axis=1, mode="promise_in_bounds")


def iota(shape, axis):
    return lax.broadcasted_iota(jnp.int32, shape, axis)


def axis_factors(coords, middle, decay):
    return jnp.exp(-decay * (coords - middle) ** 2)


def pair_kernel(
    slot_depth,
    bricks_group,
    pairs_hbm,
    dest_hbm,
    tag_hbm,
    levels_hbm,
    blocks_hbm,
    centres_hbm,
    exponents_hbm,
    out_ref,
    pairs_ref,
    dest_ref,
    tag_ref,
    levels_ref,
    blocks_ref,
    centres_ref,
    exponents_ref,
    corner_buf,
    list_sems,
    table_sems,
):
    items = blocks_ref.shape[0]
    slots = out_ref.shape[0] // SLOT_ROWS
    lists = [
        pltpu.make_async_copy(source, target, list_sems.at[n])
        for n, (source, target) in enumerate(
            (
                (pairs_hbm, pairs_ref),
                (dest_hbm, dest_ref),
                (tag_hbm, tag_ref),
                (levels_hbm, levels_ref),
            )
        )
    ]
    for copy in lists:
        copy.start()

    tables = [
        pltpu.make_async_copy(centres_hbm.at[d], centres_ref.at[d], table_sems.at[d])
        for d in range(3)
    ]
    tables.append(pltpu.make_async_copy(exponents_hbm, exponents_ref, table_sems.at[3]))
    tables.append(pltpu.make_async_copy(blocks_hbm, blocks_ref, table_sems.at[4]))
    for copy in tables:
        copy.start()
    for copy in lists + tables:
        copy.wait()
    if slots != items:
        out_ref[...] = jnp.zeros_like(out_ref)
    steps = iota((EDGE, LANES), 0).astype(jnp.float32) - (EDGE - 1) / 2.0

    def one(k):
        target = dest_ref[k] // slot_depth * bricks_group + tag_ref[k]
        spacing = jnp.where(levels_ref[target] == 1, COARSE * 0.5, COARSE)
        coords = steps * spacing

        def factors(side):
            row = pl.ds(pairs_ref[side, k], 1)
            decay = exponents_ref[row, :]
            found = [axis_factors(coords, centres_ref[d, row, :], decay) for d in range(3)]
            face = jnp.concatenate(
                [found[1][y : y + 1, :] * found[2] for y in range(EDGE)], axis=0
            )
            return found[0], face

        row_x, row_face = factors(0)
        col_x, col_face = factors(1)
        row_face = row_face.T
        block = blocks_ref[k]
        for x in range(EDGE):
            col = (col_x[x : x + 1, :] * col_face).astype(jnp.bfloat16)
            product = lax.dot_general(
                block, col, (((1,), (1,)), ((), ())), preferred_element_type=jnp.float32
            )
            weight = jnp.broadcast_to(row_x[x : x + 1, :], (LANES, block.shape[0])).T
            weight = jnp.concatenate([weight] * (FACE // LANES), axis=1)
            dens = jnp.sum(weight * row_face * product, axis=0, keepdims=True)
            for half in range(FACE // LANES):
                piece = dens[:, half * LANES : (half + 1) * LANES]
                out_ref[pl.ds(dest_ref[k] * SLOT_ROWS + 2 * x + half, 1), :] = piece
                if x in (0, EDGE - 1):
                    corner_buf[2 * (x // (EDGE - 1)) + half, pl.ds(k, 1), :] = piece

    for k in range(items):
        one(k)

    shape = (items, LANES)
    lane = iota(shape, 1)
    place = lane % 4
    low = jnp.where(place % 2 == 1, EDGE - 1, 0)
    high = (FACE - EDGE) % LANES + low
    source = jnp.where(place >= 2, high, low)
    found = [lane_pick(corner_buf[n], source) for n in range(4)]
    corner = lane % 8
    first = jnp.where(corner % 4 >= 2, found[1], found[0])
    last = jnp.where(corner % 4 >= 2, found[3], found[2])
    values = jnp.where(corner >= 4, last, first)
    row = iota(shape, 0)
    brick = jnp.zeros(shape, jnp.int32)
    for k in range(items):
        target = dest_ref[k] // slot_depth * bricks_group + tag_ref[k]
        brick = jnp.where(row == k, target, brick)
    placed = jnp.where(lane // 8 == row, values, 0.0)
    placed = jnp.where(lane == 8 * items + row, brick.astype(jnp.float32), placed)
    meta = jnp.sum(placed, axis=0, keepdims=True)
    last_lane = iota((1, LANES), 1) == LANES - 1
    if slots != items:

        @pl.loop(0, slots)
        def _(n):
            out_ref[pl.ds(n * SLOT_ROWS + ROWS, 1), :] = jnp.where(last_lane, -1.0, meta)

    for k in range(items):
        tagged = jnp.where(last_lane, tag_ref[k].astype(jnp.float32), meta)
        out_ref[pl.ds(dest_ref[k] * SLOT_ROWS + ROWS, 1), :] = tagged


def group_kernel(items, bricks_dev, moves, in_ref, *outs):
    me = lax.axis_index("basis")
    slots = in_ref.shape[0] // SLOT_ROWS
    meta = [in_ref[n * SLOT_ROWS + ROWS : (n + 1) * SLOT_ROWS, :] for n in range(slots)]
    tags = [jnp.broadcast_to(line[:, LANES - 1 :], (ROWS, LANES)) for line in meta]
    owned = sum(jnp.where(me == i, i, 0) for i in range(len(moves[0])))
    sends = []
    for out, move in zip(outs, [None, *moves]):
        owner = owned
        if move is not None:
            owner = sum(jnp.where(me == i, -1 if i == to else to, 0) for i, to in enumerate(move))
        sends.append(owner)
        for b in range(bricks_dev):
            brick = jnp.where(owner < 0, -2, owner * bricks_dev + b).astype(jnp.float32)
            total = jnp.zeros((ROWS, LANES), jnp.float32)
            for n in range(slots):
                dens = in_ref[n * SLOT_ROWS : n * SLOT_ROWS + ROWS, :]
                total = total + jnp.where(tags[n] == brick, dens, 0.0)
            out[b * ROWS : (b + 1) * ROWS, :] = total
    table_rows = outs[0].shape[0] - bricks_dev * ROWS
    shape = (TILE, LANES)
    lane = iota(shape, 1)
    lines = [jnp.zeros(shape, jnp.float32) for _ in range(table_rows)]
    for first in range(0, slots, TILE):
        block = jnp.concatenate(meta[first : first + TILE], axis=0)
        for k in range(items):
            values = lane_pick(block, 8 * k + (lane & 7))
            brick = lane_pick(block, jnp.full(shape, 8 * items + k, jnp.int32)).astype(jnp.int32)
            values = jnp.where((brick & 15) == lane >> 3, values, 0.0)
            for r in range(table_rows):
                lines[r] = lines[r] + jnp.where(brick >> 4 == r, values, 0.0)
    table = jnp.concatenate([jnp.sum(line, axis=0, keepdims=True) for line in lines], axis=0)
    for out, owner in zip(outs, sends):
        out[bricks_dev * ROWS :, :] = jnp.where(owner < 0, 0.0, table)


def map_kernel(cells_ref, out_ref):
    bricks_dev, cells = cells_ref.shape
    cell = (iota((LANES, cells), 1) + 1).astype(jnp.float32)
    for b in range(bricks_dev):
        position = cells_ref[b : b + 1, :]
        high = position >> SHIFT == iota((ROWS, cells), 0)
        low = (position & (LANES - 1)) == iota((LANES, cells), 0)
        found = lax.dot_general(
            high.astype(jnp.float32).astype(jnp.bfloat16),
            jnp.where(low, cell, 0.0).astype(jnp.bfloat16),
            (((1,), (1,)), ((), ())),
            preferred_element_type=jnp.float32,
        )
        out_ref[b] = found.astype(jnp.int32) - 1


def cell_kernel(*refs):
    *ins, map_ref, refs_ref, out_ref = refs
    bricks_dev, _, cells = refs_ref.shape
    total = ins[0][...]
    for part in ins[1:]:
        total = total + part[...]
    table = total[bricks_dev * ROWS :]
    chunk = (TILE, LANES)
    tiles = cells // LANES
    refs = [
        [refs_ref[b, :, c * LANES : (c + 1) * LANES] for c in range(tiles)]
        for b in range(bricks_dev)
    ]
    picked = [[jnp.zeros(chunk, jnp.float32) for _ in row] for row in refs]
    for r in range(table.shape[0]):
        line = jnp.broadcast_to(table[r : r + 1, :], chunk)
        for b in range(bricks_dev):
            for c, index in enumerate(refs[b]):
                found = lane_pick(line, (index & (LANES - 1)))
                picked[b][c] = jnp.where(index >> SHIFT == r, found, picked[b][c])
    for b in range(bricks_dev):
        cell = map_ref[b]
        mean = jnp.zeros((ROWS, LANES), jnp.float32)
        for c in range(tiles):
            line = jnp.sum(picked[b][c], axis=0, keepdims=True) * (0.5 / 8.0)
            found = lane_pick(jnp.broadcast_to(line, (ROWS, LANES)), (cell & (LANES - 1)))
            mean = jnp.where(cell >> SHIFT == c, found, mean)
        own = total[b * ROWS : (b + 1) * ROWS]
        result = jnp.where(cell >= 0, 0.5 * own + mean, own)
        for row in range(ROWS):
            out_ref[b : b + 1, row * LANES : (row + 1) * LANES] = result[row : row + 1, :]


def moves_of(owners):
    if owners == 4:
        early = [(1, 2, 0, 3), (2, 0, 1, 3)]
        late = [(3, 1, 2, 0), (0, 3, 2, 1), (0, 1, 3, 2)]
        return early + late
    return [tuple((i + d) % owners for i in range(owners)) for d in range(1, owners)]


def vmem():
    return pl.BlockSpec(memory_space=pltpu.VMEM)


def body(
    block_data, item_pairs, dest_slot, brick_tag, centres, exponents, levels, cell_pos, corner_refs
):
    groups = lax.axis_size("row") * lax.axis_size("col")
    owners = lax.axis_size("basis")
    items = block_data.shape[0]
    slot_depth = max(1, items // groups)
    slots = groups * slot_depth
    bricks = levels.shape[0]
    bricks_group = bricks // groups
    bricks_dev = bricks_group // owners
    table_rows = -(-bricks * 8 // (8 * LANES)) * 8
    basis = block_data.shape[1]
    params = pltpu.CompilerParams(vmem_limit_bytes=32 * 1024 * 1024)

    outgoing = pl.pallas_call(
        functools.partial(pair_kernel, slot_depth, bricks_group),
        out_shape=jax.ShapeDtypeStruct((slots * SLOT_ROWS, LANES), jnp.float32),
        in_specs=[pl.BlockSpec(memory_space=pltpu.HBM)] * 7,
        out_specs=vmem(),
        scratch_shapes=[
            pltpu.SMEM((2, items), jnp.int32),
            pltpu.SMEM((items,), jnp.int32),
            pltpu.SMEM((items,), jnp.int32),
            pltpu.SMEM((bricks,), jnp.int32),
            pltpu.VMEM(block_data.shape, block_data.dtype),
            pltpu.VMEM((3, centres.shape[0], basis), jnp.float32),
            pltpu.VMEM(exponents.shape, jnp.float32),
            pltpu.VMEM((4, items, LANES), jnp.float32),
            pltpu.SemaphoreType.DMA((4,)),
            pltpu.SemaphoreType.DMA((5,)),
        ],
        compiler_params=params,
        name="pair_density",
    )(
        *(
            pltpu.with_memory_space_constraint(operand, pltpu.HBM)
            for operand in (
                item_pairs.T,
                dest_slot,
                brick_tag,
                levels,
                block_data,
                jnp.transpose(centres, (1, 0, 2)),
                exponents,
            )
        )
    )
    arrived = lax.all_to_all(
        outgoing.reshape(slots, 1, SLOT_ROWS * LANES),
        ("row", "col"),
        split_axis=0,
        concat_axis=0,
        tiled=True,
    ).reshape(outgoing.shape)
    moves = moves_of(owners)
    partial = pl.pallas_call(
        functools.partial(group_kernel, items, bricks_dev, moves),
        out_shape=[jax.ShapeDtypeStruct((bricks_dev * ROWS + table_rows, LANES), jnp.float32)]
        * (len(moves) + 1),
        in_specs=[vmem()],
        out_specs=[vmem()] * (len(moves) + 1),
        compiler_params=params,
        name="group_sum",
    )(arrived)
    parts = [partial[0]] + [
        lax.ppermute(piece, "basis", list(enumerate(move)))
        for piece, move in zip(partial[1:], moves)
    ]
    cell_map = pl.pallas_call(
        map_kernel,
        out_shape=jax.ShapeDtypeStruct((bricks_dev, ROWS, LANES), jnp.int32),
        in_specs=[vmem()],
        out_specs=vmem(),
        compiler_params=params,
        cost_estimate=pl.CostEstimate(flops=4_000_000, bytes_accessed=200_000, transcendentals=0),
        name="cell_map",
    )(cell_pos)
    return pl.pallas_call(
        cell_kernel,
        out_shape=jax.ShapeDtypeStruct((bricks_dev, EDGE * FACE), jnp.float32),
        in_specs=[vmem()] * (len(parts) + 2),
        out_specs=vmem(),
        compiler_params=params,
        name="cells",
    )(*parts, cell_map, jnp.transpose(corner_refs, (0, 2, 1)))


def solution(mesh):
    split = ("row", "col", "basis")
    return jax.shard_map(
        body,
        mesh=mesh,
        in_specs=(
            P(split, None, None),
            P(split, None),
            P(split),
            P(split),
            P(),
            P(),
            P(),
            P(split, None),
            P(split, None, None),
        ),
        out_specs=P(split, None),
        check_vma=False,
    )
```

```python
import functools

import jax
import jax.numpy as jnp
from jax import lax
from jax.experimental import pallas as pl
from jax.experimental.pallas import tpu as pltpu
from jax.sharding import PartitionSpec as P

EDGE = 16
FACE = EDGE * EDGE
LANES = 128
SHIFT = 7
ROWS = EDGE * FACE // LANES
COARSE = 0.2
SLOT_ROWS = ROWS + 1
TILE = 8


def lane_pick(values, index):
    return jnp.take_along_axis(values, index, axis=1, mode="promise_in_bounds")


def iota(shape, axis):
    return lax.broadcasted_iota(jnp.int32, shape, axis)


def axis_factors(coords, middle, decay):
    return jnp.exp(-decay * (coords - middle) ** 2)


def pair_kernel(
    slot_depth,
    bricks_group,
    pairs_hbm,
    dest_hbm,
    tag_hbm,
    levels_hbm,
    blocks_hbm,
    centres_hbm,
    exponents_hbm,
    out_ref,
    pairs_ref,
    dest_ref,
    tag_ref,
    levels_ref,
    blocks_ref,
    centres_ref,
    exponents_ref,
    corner_buf,
    list_sems,
    table_sems,
):
    items = blocks_ref.shape[0]
    slots = out_ref.shape[0] // SLOT_ROWS
    lists = [
        pltpu.make_async_copy(source, target, list_sems.at[n])
        for n, (source, target) in enumerate(
            (
                (pairs_hbm, pairs_ref),
                (dest_hbm, dest_ref),
                (tag_hbm, tag_ref),
                (levels_hbm, levels_ref),
            )
        )
    ]
    for copy in lists:
        copy.start()

    tables = [
        pltpu.make_async_copy(centres_hbm.at[d], centres_ref.at[d], table_sems.at[d])
        for d in range(3)
    ]
    tables.append(pltpu.make_async_copy(exponents_hbm, exponents_ref, table_sems.at[3]))
    tables.append(pltpu.make_async_copy(blocks_hbm, blocks_ref, table_sems.at[4]))
    for copy in tables:
        copy.start()
    for copy in lists + tables:
        copy.wait()
    if slots != items:
        out_ref[...] = jnp.zeros_like(out_ref)
    steps = iota((EDGE, LANES), 0).astype(jnp.float32) - (EDGE - 1) / 2.0

    def one(k):
        target = dest_ref[k] // slot_depth * bricks_group + tag_ref[k]
        spacing = jnp.where(levels_ref[target] == 1, COARSE * 0.5, COARSE)
        coords = steps * spacing

        def factors(side):
            row = pl.ds(pairs_ref[side, k], 1)
            decay = exponents_ref[row, :]
            found = [axis_factors(coords, centres_ref[d, row, :], decay) for d in range(3)]
            face = jnp.concatenate(
                [found[1][y : y + 1, :] * found[2] for y in range(EDGE)], axis=0
            )
            return found[0], face

        row_x, row_face = factors(0)
        col_x, col_face = factors(1)
        row_face = row_face.T
        block = blocks_ref[k]
        for x in range(EDGE):
            col = (col_x[x : x + 1, :] * col_face).astype(jnp.bfloat16)
            product = lax.dot_general(
                block, col, (((1,), (1,)), ((), ())), preferred_element_type=jnp.float32
            )
            weight = jnp.broadcast_to(row_x[x : x + 1, :], (LANES, block.shape[0])).T
            weight = jnp.concatenate([weight] * (FACE // LANES), axis=1)
            dens = jnp.sum(weight * row_face * product, axis=0, keepdims=True)
            for half in range(FACE // LANES):
                piece = dens[:, half * LANES : (half + 1) * LANES]
                out_ref[pl.ds(dest_ref[k] * SLOT_ROWS + 2 * x + half, 1), :] = piece
                if x in (0, EDGE - 1):
                    corner_buf[2 * (x // (EDGE - 1)) + half, pl.ds(k, 1), :] = piece

    for k in range(items):
        one(k)

    shape = (items, LANES)
    lane = iota(shape, 1)
    place = lane % 4
    low = jnp.where(place % 2 == 1, EDGE - 1, 0)
    high = (FACE - EDGE) % LANES + low
    source = jnp.where(place >= 2, high, low)
    found = [lane_pick(corner_buf[n], source) for n in range(4)]
    corner = lane % 8
    first = jnp.where(corner % 4 >= 2, found[1], found[0])
    last = jnp.where(corner % 4 >= 2, found[3], found[2])
    values = jnp.where(corner >= 4, last, first)
    row = iota(shape, 0)
    brick = jnp.zeros(shape, jnp.int32)
    for k in range(items):
        target = dest_ref[k] // slot_depth * bricks_group + tag_ref[k]
        brick = jnp.where(row == k, target, brick)
    placed = jnp.where(lane // 8 == row, values, 0.0)
    placed = jnp.where(lane == 8 * items + row, brick.astype(jnp.float32), placed)
    meta = jnp.sum(placed, axis=0, keepdims=True)
    last_lane = iota((1, LANES), 1) == LANES - 1
    if slots != items:

        @pl.loop(0, slots)
        def _(n):
            out_ref[pl.ds(n * SLOT_ROWS + ROWS, 1), :] = jnp.where(last_lane, -1.0, meta)

    for k in range(items):
        tagged = jnp.where(last_lane, tag_ref[k].astype(jnp.float32), meta)
        out_ref[pl.ds(dest_ref[k] * SLOT_ROWS + ROWS, 1), :] = tagged


def group_kernel(items, bricks_dev, moves, in_ref, *outs):
    me = lax.axis_index("basis")
    slots = in_ref.shape[0] // SLOT_ROWS
    meta = [in_ref[n * SLOT_ROWS + ROWS : (n + 1) * SLOT_ROWS, :] for n in range(slots)]
    tags = [jnp.broadcast_to(line[:, LANES - 1 :], (ROWS, LANES)) for line in meta]
    owned = sum(jnp.where(me == i, i, 0) for i in range(len(moves[0])))
    sends = []
    for out, move in zip(outs, [None, *moves]):
        owner = owned
        if move is not None:
            owner = sum(jnp.where(me == i, -1 if i == to else to, 0) for i, to in enumerate(move))
        sends.append(owner)
        for b in range(bricks_dev):
            brick = jnp.where(owner < 0, -2, owner * bricks_dev + b).astype(jnp.float32)
            total = jnp.zeros((ROWS, LANES), jnp.float32)
            for n in range(slots):
                dens = in_ref[n * SLOT_ROWS : n * SLOT_ROWS + ROWS, :]
                total = total + jnp.where(tags[n] == brick, dens, 0.0)
            out[b * ROWS : (b + 1) * ROWS, :] = total
    table_rows = outs[0].shape[0] - bricks_dev * ROWS
    shape = (TILE, LANES)
    lane = iota(shape, 1)
    lines = [jnp.zeros(shape, jnp.float32) for _ in range(table_rows)]
    for first in range(0, slots, TILE):
        block = jnp.concatenate(meta[first : first + TILE], axis=0)
        for k in range(items):
            values = lane_pick(block, 8 * k + (lane & 7))
            brick = lane_pick(block, jnp.full(shape, 8 * items + k, jnp.int32)).astype(jnp.int32)
            values = jnp.where((brick & 15) == lane >> 3, values, 0.0)
            for r in range(table_rows):
                lines[r] = lines[r] + jnp.where(brick >> 4 == r, values, 0.0)
    table = jnp.concatenate([jnp.sum(line, axis=0, keepdims=True) for line in lines], axis=0)
    for out, owner in zip(outs, sends):
        out[bricks_dev * ROWS :, :] = jnp.where(owner < 0, 0.0, table)


def map_kernel(cells_ref, out_ref):
    bricks_dev, cells = cells_ref.shape
    cell = (iota((LANES, cells), 1) + 1).astype(jnp.float32)
    for b in range(bricks_dev):
        position = cells_ref[b : b + 1, :]
        high = position >> SHIFT == iota((ROWS, cells), 0)
        low = (position & (LANES - 1)) == iota((LANES, cells), 0)
        found = lax.dot_general(
            high.astype(jnp.float32).astype(jnp.bfloat16),
            jnp.where(low, cell, 0.0).astype(jnp.bfloat16),
            (((1,), (1,)), ((), ())),
            preferred_element_type=jnp.float32,
        )
        out_ref[b] = found.astype(jnp.int32) - 1


def cell_kernel(*refs):
    *ins, map_ref, refs_ref, out_ref = refs
    bricks_dev, _, cells = refs_ref.shape
    total = ins[0][...]
    for part in ins[1:]:
        total = total + part[...]
    table = total[bricks_dev * ROWS :]
    chunk = (TILE, LANES)
    tiles = cells // LANES
    refs = [
        [refs_ref[b, :, c * LANES : (c + 1) * LANES] for c in range(tiles)]
        for b in range(bricks_dev)
    ]
    picked = [[jnp.zeros(chunk, jnp.float32) for _ in row] for row in refs]
    for r in range(table.shape[0]):
        line = jnp.broadcast_to(table[r : r + 1, :], chunk)
        for b in range(bricks_dev):
            for c, index in enumerate(refs[b]):
                found = lane_pick(line, (index & (LANES - 1)))
                picked[b][c] = jnp.where(index >> SHIFT == r, found, picked[b][c])
    for b in range(bricks_dev):
        cell = map_ref[b]
        mean = jnp.zeros((ROWS, LANES), jnp.float32)
        for c in range(tiles):
            line = jnp.sum(picked[b][c], axis=0, keepdims=True) * (0.5 / 8.0)
            found = lane_pick(jnp.broadcast_to(line, (ROWS, LANES)), (cell & (LANES - 1)))
            mean = jnp.where(cell >> SHIFT == c, found, mean)
        own = total[b * ROWS : (b + 1) * ROWS]
        result = jnp.where(cell >= 0, 0.5 * own + mean, own)
        for row in range(ROWS):
            out_ref[b : b + 1, row * LANES : (row + 1) * LANES] = result[row : row + 1, :]


def moves_of(rows, owners):
    if owners == 4 and rows % 2 == 0:
        early = [(1, 2, 0, 3), (2, 0, 1, 3)]
        late = [(3, 1, 2, 0), (0, 3, 2, 1), (0, 1, 3, 2)]
        return early + late
    return [tuple((i + d) % owners for i in range(owners)) for d in range(1, owners)]


def pairs_of(move, rows, cols):
    owners = len(move)
    pairs = []
    for row in range(rows):
        for col in range(cols):
            for z, to in enumerate(move):
                target = row ^ 1 if to == z else row
                source = (row * cols + col) * owners + z
                pairs.append((source, (target * cols + col) * owners + to))
    return pairs


def vmem():
    return pl.BlockSpec(memory_space=pltpu.VMEM)


def body(
    block_data, item_pairs, dest_slot, brick_tag, centres, exponents, levels, cell_pos, corner_refs
):
    groups = lax.axis_size("row") * lax.axis_size("col")
    owners = lax.axis_size("basis")
    items = block_data.shape[0]
    slot_depth = max(1, items // groups)
    slots = groups * slot_depth
    bricks = levels.shape[0]
    bricks_group = bricks // groups
    bricks_dev = bricks_group // owners
    table_rows = -(-bricks * 8 // (8 * LANES)) * 8
    basis = block_data.shape[1]
    params = pltpu.CompilerParams(vmem_limit_bytes=32 * 1024 * 1024)

    outgoing = pl.pallas_call(
        functools.partial(pair_kernel, slot_depth, bricks_group),
        out_shape=jax.ShapeDtypeStruct((slots * SLOT_ROWS, LANES), jnp.float32),
        in_specs=[pl.BlockSpec(memory_space=pltpu.HBM)] * 7,
        out_specs=vmem(),
        scratch_shapes=[
            pltpu.SMEM((2, items), jnp.int32),
            pltpu.SMEM((items,), jnp.int32),
            pltpu.SMEM((items,), jnp.int32),
            pltpu.SMEM((bricks,), jnp.int32),
            pltpu.VMEM(block_data.shape, block_data.dtype),
            pltpu.VMEM((3, centres.shape[0], basis), jnp.float32),
            pltpu.VMEM(exponents.shape, jnp.float32),
            pltpu.VMEM((4, items, LANES), jnp.float32),
            pltpu.SemaphoreType.DMA((4,)),
            pltpu.SemaphoreType.DMA((5,)),
        ],
        compiler_params=params,
        name="pair_density",
    )(
        *(
            pltpu.with_memory_space_constraint(operand, pltpu.HBM)
            for operand in (
                item_pairs.T,
                dest_slot,
                brick_tag,
                levels,
                block_data,
                jnp.transpose(centres, (1, 0, 2)),
                exponents,
            )
        )
    )
    arrived = lax.all_to_all(
        outgoing.reshape(slots, 1, SLOT_ROWS * LANES),
        ("row", "col"),
        split_axis=0,
        concat_axis=0,
        tiled=True,
    ).reshape(outgoing.shape)
    rows, cols = lax.axis_size("row"), lax.axis_size("col")
    moves = moves_of(rows, owners)
    partial = pl.pallas_call(
        functools.partial(group_kernel, items, bricks_dev, moves),
        out_shape=[jax.ShapeDtypeStruct((bricks_dev * ROWS + table_rows, LANES), jnp.float32)]
        * (len(moves) + 1),
        in_specs=[vmem()],
        out_specs=[vmem()] * (len(moves) + 1),
        compiler_params=params,
        name="group_sum",
    )(arrived)
    parts = [partial[0]] + [
        lax.ppermute(piece, ("row", "col", "basis"), pairs_of(move, rows, cols))
        for piece, move in zip(partial[1:], moves)
    ]
    cell_map = pl.pallas_call(
        map_kernel,
        out_shape=jax.ShapeDtypeStruct((bricks_dev, ROWS, LANES), jnp.int32),
        in_specs=[vmem()],
        out_specs=vmem(),
        compiler_params=params,
        cost_estimate=pl.CostEstimate(flops=4_000_000, bytes_accessed=200_000, transcendentals=0),
        name="cell_map",
    )(cell_pos)
    return pl.pallas_call(
        cell_kernel,
        out_shape=jax.ShapeDtypeStruct((bricks_dev, EDGE * FACE), jnp.float32),
        in_specs=[vmem()] * (len(parts) + 2),
        out_specs=vmem(),
        compiler_params=params,
        name="cells",
    )(*parts, cell_map, jnp.transpose(corner_refs, (0, 2, 1)))


def solution(mesh):
    split = ("row", "col", "basis")
    return jax.shard_map(
        body,
        mesh=mesh,
        in_specs=(
            P(split, None, None),
            P(split, None),
            P(split),
            P(split),
            P(),
            P(),
            P(),
            P(split, None),
            P(split, None, None),
        ),
        out_specs=P(split, None),
        check_vma=False,
    )
```

```python
import functools

import jax
import jax.numpy as jnp
from jax import lax
from jax.experimental import pallas as pl
from jax.experimental.pallas import tpu as pltpu
from jax.sharding import PartitionSpec as P

EDGE = 16
FACE = EDGE * EDGE
LANES = 128
SHIFT = 7
ROWS = EDGE * FACE // LANES
COARSE = 0.2
SLOT_ROWS = ROWS + 1
TILE = 8


def lane_pick(values, index):
    return jnp.take_along_axis(values, index, axis=1, mode="promise_in_bounds")


def iota(shape, axis):
    return lax.broadcasted_iota(jnp.int32, shape, axis)


def axis_factors(coords, middle, decay):
    return jnp.exp(-decay * (coords - middle) ** 2)


def pair_kernel(
    slot_depth,
    bricks_group,
    pairs_hbm,
    dest_hbm,
    tag_hbm,
    levels_hbm,
    blocks_hbm,
    centres_hbm,
    exponents_hbm,
    out_ref,
    pairs_ref,
    dest_ref,
    tag_ref,
    levels_ref,
    blocks_ref,
    centres_ref,
    exponents_ref,
    corner_buf,
    list_sems,
    table_sems,
):
    items = blocks_ref.shape[0]
    slots = out_ref.shape[0] // SLOT_ROWS
    lists = [
        pltpu.make_async_copy(source, target, list_sems.at[n])
        for n, (source, target) in enumerate(
            (
                (pairs_hbm, pairs_ref),
                (dest_hbm, dest_ref),
                (tag_hbm, tag_ref),
                (levels_hbm, levels_ref),
            )
        )
    ]
    for copy in lists:
        copy.start()

    tables = [
        pltpu.make_async_copy(exponents_hbm, exponents_ref, table_sems.at[0]),
        pltpu.make_async_copy(centres_hbm, centres_ref, table_sems.at[1]),
    ]
    blocks = pltpu.make_async_copy(blocks_hbm, blocks_ref, table_sems.at[2])
    for copy in tables + [blocks]:
        copy.start()
    for copy in lists + tables:
        copy.wait()
    if slots != items:
        out_ref[...] = jnp.zeros_like(out_ref)
    steps = iota((EDGE, LANES), 0).astype(jnp.float32) - (EDGE - 1) / 2.0

    def one(k):
        target = dest_ref[k] // slot_depth * bricks_group + tag_ref[k]
        spacing = jnp.where(levels_ref[target] == 1, COARSE * 0.5, COARSE)
        coords = steps * spacing

        def factors(side):
            row = pl.ds(pairs_ref[side, k], 1)
            decay = exponents_ref[row, :]
            found = [axis_factors(coords, centres_ref[d, row, :], decay) for d in range(3)]
            face = jnp.concatenate(
                [found[1][y : y + 1, :] * found[2] for y in range(EDGE)], axis=0
            )
            return found[0], face

        row_x, row_face = factors(0)
        col_x, col_face = factors(1)
        row_face = row_face.T
        if k == 0:
            blocks.wait()
        block = blocks_ref[k]
        for x in range(EDGE):
            col = (col_x[x : x + 1, :] * col_face).astype(jnp.bfloat16)
            product = lax.dot_general(
                block, col, (((1,), (1,)), ((), ())), preferred_element_type=jnp.float32
            )
            weight = jnp.broadcast_to(row_x[x : x + 1, :], (LANES, block.shape[0])).T
            weight = jnp.concatenate([weight] * (FACE // LANES), axis=1)
            dens = jnp.sum(weight * row_face * product, axis=0, keepdims=True)
            for half in range(FACE // LANES):
                piece = dens[:, half * LANES : (half + 1) * LANES]
                out_ref[pl.ds(dest_ref[k] * SLOT_ROWS + 2 * x + half, 1), :] = piece
                if x in (0, EDGE - 1):
                    corner_buf[2 * (x // (EDGE - 1)) + half, pl.ds(k, 1), :] = piece

    for k in range(items):
        one(k)

    shape = (items, LANES)
    lane = iota(shape, 1)
    place = lane % 4
    low = jnp.where(place % 2 == 1, EDGE - 1, 0)
    high = (FACE - EDGE) % LANES + low
    source = jnp.where(place >= 2, high, low)
    found = [lane_pick(corner_buf[n], source) for n in range(4)]
    corner = lane % 8
    first = jnp.where(corner % 4 >= 2, found[1], found[0])
    last = jnp.where(corner % 4 >= 2, found[3], found[2])
    values = jnp.where(corner >= 4, last, first)
    row = iota(shape, 0)
    brick = jnp.zeros(shape, jnp.int32)
    for k in range(items):
        target = dest_ref[k] // slot_depth * bricks_group + tag_ref[k]
        brick = jnp.where(row == k, target, brick)
    placed = jnp.where(lane // 8 == row, values, 0.0)
    placed = jnp.where(lane == 8 * items + row, brick.astype(jnp.float32), placed)
    meta = jnp.sum(placed, axis=0, keepdims=True)
    last_lane = iota((1, LANES), 1) == LANES - 1
    if slots != items:

        @pl.loop(0, slots)
        def _(n):
            out_ref[pl.ds(n * SLOT_ROWS + ROWS, 1), :] = jnp.where(last_lane, -1.0, meta)

    for k in range(items):
        tagged = jnp.where(last_lane, tag_ref[k].astype(jnp.float32), meta)
        out_ref[pl.ds(dest_ref[k] * SLOT_ROWS + ROWS, 1), :] = tagged


def group_kernel(items, bricks_dev, moves, in_ref, *outs):
    me = lax.axis_index("basis")
    slots = in_ref.shape[0] // SLOT_ROWS
    meta = [in_ref[n * SLOT_ROWS + ROWS : (n + 1) * SLOT_ROWS, :] for n in range(slots)]
    tags = [jnp.broadcast_to(line[:, LANES - 1 :], (ROWS, LANES)) for line in meta]
    owned = sum(jnp.where(me == i, i, 0) for i in range(len(moves[0])))
    sends = []
    for out, move in zip(outs, [None, *moves]):
        owner = owned
        if move is not None:
            owner = sum(jnp.where(me == i, -1 if i == to else to, 0) for i, to in enumerate(move))
        sends.append(owner)
        for b in range(bricks_dev):
            brick = jnp.where(owner < 0, -2, owner * bricks_dev + b).astype(jnp.float32)
            total = jnp.zeros((ROWS, LANES), jnp.float32)
            for n in range(slots):
                dens = in_ref[n * SLOT_ROWS : n * SLOT_ROWS + ROWS, :]
                total = total + jnp.where(tags[n] == brick, dens, 0.0)
            out[b * ROWS : (b + 1) * ROWS, :] = total
    table_rows = outs[0].shape[0] - bricks_dev * ROWS
    shape = (TILE, LANES)
    lane = iota(shape, 1)
    lines = [jnp.zeros(shape, jnp.float32) for _ in range(table_rows)]
    for first in range(0, slots, TILE):
        block = jnp.concatenate(meta[first : first + TILE], axis=0)
        for k in range(items):
            values = lane_pick(block, 8 * k + (lane & 7))
            brick = lane_pick(block, jnp.full(shape, 8 * items + k, jnp.int32)).astype(jnp.int32)
            values = jnp.where((brick & 15) == lane >> 3, values, 0.0)
            for r in range(table_rows):
                lines[r] = lines[r] + jnp.where(brick >> 4 == r, values, 0.0)
    table = jnp.concatenate([jnp.sum(line, axis=0, keepdims=True) for line in lines], axis=0)
    for out, owner in zip(outs, sends):
        out[bricks_dev * ROWS :, :] = jnp.where(owner < 0, 0.0, table)


def map_kernel(cells_ref, out_ref):
    bricks_dev, cells = cells_ref.shape
    cell = (iota((LANES, cells), 1) + 1).astype(jnp.float32)
    for b in range(bricks_dev):
        position = cells_ref[b : b + 1, :]
        high = position >> SHIFT == iota((ROWS, cells), 0)
        low = (position & (LANES - 1)) == iota((LANES, cells), 0)
        found = lax.dot_general(
            high.astype(jnp.float32).astype(jnp.bfloat16),
            jnp.where(low, cell, 0.0).astype(jnp.bfloat16),
            (((1,), (1,)), ((), ())),
            preferred_element_type=jnp.float32,
        )
        out_ref[b] = found.astype(jnp.int32) - 1


def cell_kernel(*refs):
    *ins, map_ref, refs_ref, out_ref = refs
    bricks_dev, _, cells = refs_ref.shape
    total = ins[0][...]
    for part in ins[1:]:
        total = total + part[...]
    table = total[bricks_dev * ROWS :]
    chunk = (TILE, LANES)
    tiles = cells // LANES
    refs = [
        [refs_ref[b, :, c * LANES : (c + 1) * LANES] for c in range(tiles)]
        for b in range(bricks_dev)
    ]
    picked = [[jnp.zeros(chunk, jnp.float32) for _ in row] for row in refs]
    for r in range(table.shape[0]):
        line = jnp.broadcast_to(table[r : r + 1, :], chunk)
        for b in range(bricks_dev):
            for c, index in enumerate(refs[b]):
                found = lane_pick(line, (index & (LANES - 1)))
                picked[b][c] = jnp.where(index >> SHIFT == r, found, picked[b][c])
    for b in range(bricks_dev):
        cell = map_ref[b]
        mean = jnp.zeros((ROWS, LANES), jnp.float32)
        for c in range(tiles):
            line = jnp.sum(picked[b][c], axis=0, keepdims=True) * (0.5 / 8.0)
            found = lane_pick(jnp.broadcast_to(line, (ROWS, LANES)), (cell & (LANES - 1)))
            mean = jnp.where(cell >> SHIFT == c, found, mean)
        own = total[b * ROWS : (b + 1) * ROWS]
        result = jnp.where(cell >= 0, 0.5 * own + mean, own)
        for row in range(ROWS):
            out_ref[b : b + 1, row * LANES : (row + 1) * LANES] = result[row : row + 1, :]


def moves_of(rows, owners):
    if owners == 4 and rows % 2 == 0:
        return [(1, 3, 2, 0), (2, 1, 0, 3), (3, 0, 1, 2), (0, 2, 3, 1)]
    return [tuple((i + d) % owners for i in range(owners)) for d in range(1, owners)]


def pairs_of(move, rows, cols):
    owners = len(move)
    pairs = []
    for row in range(rows):
        for col in range(cols):
            for z, to in enumerate(move):
                target = row ^ 1 if to == z else row
                source = (row * cols + col) * owners + z
                pairs.append((source, (target * cols + col) * owners + to))
    return pairs


def vmem():
    return pl.BlockSpec(memory_space=pltpu.VMEM)


def body(
    block_data, item_pairs, dest_slot, brick_tag, centres, exponents, levels, cell_pos, corner_refs
):
    groups = lax.axis_size("row") * lax.axis_size("col")
    owners = lax.axis_size("basis")
    items = block_data.shape[0]
    slot_depth = max(1, items // groups)
    slots = groups * slot_depth
    bricks = levels.shape[0]
    bricks_group = bricks // groups
    bricks_dev = bricks_group // owners
    table_rows = -(-bricks * 8 // (8 * LANES)) * 8
    basis = block_data.shape[1]
    params = pltpu.CompilerParams(vmem_limit_bytes=32 * 1024 * 1024)

    outgoing = pl.pallas_call(
        functools.partial(pair_kernel, slot_depth, bricks_group),
        out_shape=jax.ShapeDtypeStruct((slots * SLOT_ROWS, LANES), jnp.float32),
        in_specs=[pl.BlockSpec(memory_space=pltpu.HBM)] * 7,
        out_specs=vmem(),
        scratch_shapes=[
            pltpu.SMEM((2, items), jnp.int32),
            pltpu.SMEM((items,), jnp.int32),
            pltpu.SMEM((items,), jnp.int32),
            pltpu.SMEM((bricks,), jnp.int32),
            pltpu.VMEM(block_data.shape, block_data.dtype),
            pltpu.VMEM((3, centres.shape[0], basis), jnp.float32),
            pltpu.VMEM(exponents.shape, jnp.float32),
            pltpu.VMEM((4, items, LANES), jnp.float32),
            pltpu.SemaphoreType.DMA((4,)),
            pltpu.SemaphoreType.DMA((3,)),
        ],
        compiler_params=params,
        name="pair_density",
    )(
        *(
            pltpu.with_memory_space_constraint(operand, pltpu.HBM)
            for operand in (
                item_pairs.T,
                dest_slot,
                brick_tag,
                levels,
                block_data,
                jnp.transpose(centres, (1, 0, 2)),
                exponents,
            )
        )
    )
    arrived = lax.all_to_all(
        outgoing.reshape(slots, 1, SLOT_ROWS * LANES),
        ("row", "col"),
        split_axis=0,
        concat_axis=0,
        tiled=True,
    ).reshape(outgoing.shape)
    rows, cols = lax.axis_size("row"), lax.axis_size("col")
    moves = moves_of(rows, owners)
    partial = pl.pallas_call(
        functools.partial(group_kernel, items, bricks_dev, moves),
        out_shape=[jax.ShapeDtypeStruct((bricks_dev * ROWS + table_rows, LANES), jnp.float32)]
        * (len(moves) + 1),
        in_specs=[vmem()],
        out_specs=[vmem()] * (len(moves) + 1),
        compiler_params=params,
        name="group_sum",
    )(arrived)
    parts = [partial[0]] + [
        lax.ppermute(piece, ("row", "col", "basis"), pairs_of(move, rows, cols))
        for piece, move in zip(partial[1:], moves)
    ]
    cell_map = pl.pallas_call(
        map_kernel,
        out_shape=jax.ShapeDtypeStruct((bricks_dev, ROWS, LANES), jnp.int32),
        in_specs=[vmem()],
        out_specs=vmem(),
        compiler_params=params,
        cost_estimate=pl.CostEstimate(flops=4_000_000, bytes_accessed=200_000, transcendentals=0),
        name="cell_map",
    )(cell_pos)
    return pl.pallas_call(
        cell_kernel,
        out_shape=jax.ShapeDtypeStruct((bricks_dev, EDGE * FACE), jnp.float32),
        in_specs=[vmem()] * (len(parts) + 2),
        out_specs=vmem(),
        compiler_params=params,
        name="cells",
    )(*parts, cell_map, jnp.transpose(corner_refs, (0, 2, 1)))


def solution(mesh):
    split = ("row", "col", "basis")
    return jax.shard_map(
        body,
        mesh=mesh,
        in_specs=(
            P(split, None, None),
            P(split, None),
            P(split),
            P(split),
            P(),
            P(),
            P(),
            P(split, None),
            P(split, None, None),
        ),
        out_specs=P(split, None),
        check_vma=False,
    )
```

```python
import functools

import jax
import jax.numpy as jnp
from jax import lax
from jax.experimental import pallas as pl
from jax.experimental.pallas import tpu as pltpu
from jax.sharding import PartitionSpec as P

EDGE = 16
FACE = EDGE * EDGE
LANES = 128
SHIFT = 7
ROWS = EDGE * FACE // LANES
COARSE = 0.2
SLOT_ROWS = ROWS + 1
TILE = 8


def lane_pick(values, index):
    return jnp.take_along_axis(values, index, axis=1, mode="promise_in_bounds")


def iota(shape, axis):
    return lax.broadcasted_iota(jnp.int32, shape, axis)


def axis_factors(coords, middle, decay):
    return jnp.exp(-decay * (coords - middle) ** 2)


def pair_kernel(
    slot_depth,
    bricks_group,
    pairs_hbm,
    dest_hbm,
    tag_hbm,
    levels_hbm,
    blocks_hbm,
    centres_hbm,
    exponents_hbm,
    out_ref,
    pairs_ref,
    dest_ref,
    tag_ref,
    levels_ref,
    blocks_ref,
    centres_ref,
    exponents_ref,
    corner_buf,
    list_sems,
    table_sems,
):
    items = blocks_ref.shape[0]
    slots = out_ref.shape[0] // SLOT_ROWS
    lists = [
        pltpu.make_async_copy(source, target, list_sems.at[n])
        for n, (source, target) in enumerate(
            (
                (pairs_hbm, pairs_ref),
                (dest_hbm, dest_ref),
                (tag_hbm, tag_ref),
                (levels_hbm, levels_ref),
            )
        )
    ]
    for copy in lists:
        copy.start()

    tables = [
        pltpu.make_async_copy(centres_hbm.at[d], centres_ref.at[d], table_sems.at[d])
        for d in range(3)
    ]
    tables.append(pltpu.make_async_copy(exponents_hbm, exponents_ref, table_sems.at[3]))
    tables.append(pltpu.make_async_copy(blocks_hbm, blocks_ref, table_sems.at[4]))
    for copy in tables:
        copy.start()
    for copy in lists + tables:
        copy.wait()
    if slots != items:
        out_ref[...] = jnp.zeros_like(out_ref)
    steps = iota((EDGE, LANES), 0).astype(jnp.float32) - (EDGE - 1) / 2.0

    def one(k):
        target = dest_ref[k] // slot_depth * bricks_group + tag_ref[k]
        spacing = jnp.where(levels_ref[target] == 1, COARSE * 0.5, COARSE)
        coords = steps * spacing

        def factors(side):
            row = pl.ds(pairs_ref[side, k], 1)
            decay = exponents_ref[row, :]
            found = [axis_factors(coords, centres_ref[d, row, :], decay) for d in range(3)]
            face = jnp.concatenate(
                [found[1][y : y + 1, :] * found[2] for y in range(EDGE)], axis=0
            )
            return found[0], face

        row_x, row_face = factors(0)
        col_x, col_face = factors(1)
        row_face = row_face.T
        block = blocks_ref[k]
        for x in range(EDGE):
            col = (col_x[x : x + 1, :] * col_face).astype(jnp.bfloat16)
            product = lax.dot_general(
                block, col, (((1,), (1,)), ((), ())), preferred_element_type=jnp.float32
            )
            weight = jnp.broadcast_to(row_x[x : x + 1, :], (LANES, block.shape[0])).T
            weight = jnp.concatenate([weight] * (FACE // LANES), axis=1)
            dens = jnp.sum(weight * row_face * product, axis=0, keepdims=True)
            for half in range(FACE // LANES):
                piece = dens[:, half * LANES : (half + 1) * LANES]
                out_ref[pl.ds(dest_ref[k] * SLOT_ROWS + 2 * x + half, 1), :] = piece
                if x in (0, EDGE - 1):
                    corner_buf[2 * (x // (EDGE - 1)) + half, pl.ds(k, 1), :] = piece

    for k in range(items):
        one(k)

    shape = (items, LANES)
    lane = iota(shape, 1)
    place = lane % 4
    low = jnp.where(place % 2 == 1, EDGE - 1, 0)
    high = (FACE - EDGE) % LANES + low
    source = jnp.where(place >= 2, high, low)
    found = [lane_pick(corner_buf[n], source) for n in range(4)]
    corner = lane % 8
    first = jnp.where(corner % 4 >= 2, found[1], found[0])
    last = jnp.where(corner % 4 >= 2, found[3], found[2])
    values = jnp.where(corner >= 4, last, first)
    row = iota(shape, 0)
    brick = jnp.zeros(shape, jnp.int32)
    for k in range(items):
        target = dest_ref[k] // slot_depth * bricks_group + tag_ref[k]
        brick = jnp.where(row == k, target, brick)
    placed = jnp.where(lane // 8 == row, values, 0.0)
    placed = jnp.where(lane == 8 * items + row, brick.astype(jnp.float32), placed)
    meta = jnp.sum(placed, axis=0, keepdims=True)
    last_lane = iota((1, LANES), 1) == LANES - 1
    if slots != items:

        @pl.loop(0, slots)
        def _(n):
            out_ref[pl.ds(n * SLOT_ROWS + ROWS, 1), :] = jnp.where(last_lane, -1.0, meta)

    for k in range(items):
        tagged = jnp.where(last_lane, tag_ref[k].astype(jnp.float32), meta)
        out_ref[pl.ds(dest_ref[k] * SLOT_ROWS + ROWS, 1), :] = tagged


def group_kernel(items, bricks_dev, moves, in_ref, *outs):
    me = lax.axis_index("basis")
    slots = in_ref.shape[0] // SLOT_ROWS
    meta = [in_ref[n * SLOT_ROWS + ROWS : (n + 1) * SLOT_ROWS, :] for n in range(slots)]
    tags = [jnp.broadcast_to(line[:, LANES - 1 :], (ROWS, LANES)) for line in meta]
    owned = sum(jnp.where(me == i, i, 0) for i in range(len(moves[0])))
    sends = []
    for out, move in zip(outs, [None, *moves]):
        owner = owned
        if move is not None:
            owner = sum(jnp.where(me == i, -1 if i == to else to, 0) for i, to in enumerate(move))
        sends.append(owner)
        for b in range(bricks_dev):
            brick = jnp.where(owner < 0, -2, owner * bricks_dev + b).astype(jnp.float32)
            total = jnp.zeros((ROWS, LANES), jnp.float32)
            for n in range(slots):
                dens = in_ref[n * SLOT_ROWS : n * SLOT_ROWS + ROWS, :]
                total = total + jnp.where(tags[n] == brick, dens, 0.0)
            out[b * ROWS : (b + 1) * ROWS, :] = total
    table_rows = outs[0].shape[0] - bricks_dev * ROWS
    shape = (TILE, LANES)
    lane = iota(shape, 1)
    lines = [jnp.zeros(shape, jnp.float32) for _ in range(table_rows)]
    for first in range(0, slots, TILE):
        block = jnp.concatenate(meta[first : first + TILE], axis=0)
        for k in range(items):
            values = lane_pick(block, 8 * k + (lane & 7))
            brick = lane_pick(block, jnp.full(shape, 8 * items + k, jnp.int32)).astype(jnp.int32)
            values = jnp.where((brick & 15) == lane >> 3, values, 0.0)
            for r in range(table_rows):
                lines[r] = lines[r] + jnp.where(brick >> 4 == r, values, 0.0)
    table = jnp.concatenate([jnp.sum(line, axis=0, keepdims=True) for line in lines], axis=0)
    for out, owner in zip(outs, sends):
        out[bricks_dev * ROWS :, :] = jnp.where(owner < 0, 0.0, table)


def map_kernel(cells_ref, out_ref):
    bricks_dev, cells = cells_ref.shape
    cell = (iota((LANES, cells), 1) + 1).astype(jnp.float32)
    for b in range(bricks_dev):
        position = cells_ref[b : b + 1, :]
        high = position >> SHIFT == iota((ROWS, cells), 0)
        low = (position & (LANES - 1)) == iota((LANES, cells), 0)
        found = lax.dot_general(
            high.astype(jnp.float32).astype(jnp.bfloat16),
            jnp.where(low, cell, 0.0).astype(jnp.bfloat16),
            (((1,), (1,)), ((), ())),
            preferred_element_type=jnp.float32,
        )
        out_ref[b] = found.astype(jnp.int32) - 1


def cell_kernel(*refs):
    *ins, map_ref, refs_ref, out_ref = refs
    bricks_dev, _, cells = refs_ref.shape
    total = ins[0][...]
    for part in ins[1:]:
        total = total + part[...]
    table = total[bricks_dev * ROWS :]
    chunk = (TILE, LANES)
    tiles = cells // LANES
    refs = [
        [refs_ref[b, :, c * LANES : (c + 1) * LANES] for c in range(tiles)]
        for b in range(bricks_dev)
    ]
    picked = [[jnp.zeros(chunk, jnp.float32) for _ in row] for row in refs]
    for r in range(table.shape[0]):
        line = jnp.broadcast_to(table[r : r + 1, :], chunk)
        for b in range(bricks_dev):
            for c, index in enumerate(refs[b]):
                found = lane_pick(line, (index & (LANES - 1)))
                picked[b][c] = jnp.where(index >> SHIFT == r, found, picked[b][c])
    for b in range(bricks_dev):
        cell = map_ref[b]
        mean = jnp.zeros((ROWS, LANES), jnp.float32)
        for c in range(tiles):
            line = jnp.sum(picked[b][c], axis=0, keepdims=True) * (0.5 / 8.0)
            found = lane_pick(jnp.broadcast_to(line, (ROWS, LANES)), (cell & (LANES - 1)))
            mean = jnp.where(cell >> SHIFT == c, found, mean)
        own = total[b * ROWS : (b + 1) * ROWS]
        result = jnp.where(cell >= 0, 0.5 * own + mean, own)
        for row in range(ROWS):
            out_ref[b : b + 1, row * LANES : (row + 1) * LANES] = result[row : row + 1, :]


def moves_of(rows, owners):
    if owners == 4 and rows % 2 == 0:
        return [(1, 3, 2, 0), (2, 1, 0, 3), (3, 0, 1, 2), (0, 2, 3, 1)]
    return [tuple((i + d) % owners for i in range(owners)) for d in range(1, owners)]


def pairs_of(move, rows, cols):
    owners = len(move)
    pairs = []
    for row in range(rows):
        for col in range(cols):
            for z, to in enumerate(move):
                target = row ^ 1 if to == z else row
                source = (row * cols + col) * owners + z
                pairs.append((source, (target * cols + col) * owners + to))
    return pairs


def vmem():
    return pl.BlockSpec(memory_space=pltpu.VMEM)


def body(
    block_data, item_pairs, dest_slot, brick_tag, centres, exponents, levels, cell_pos, corner_refs
):
    groups = lax.axis_size("row") * lax.axis_size("col")
    owners = lax.axis_size("basis")
    items = block_data.shape[0]
    slot_depth = max(1, items // groups)
    slots = groups * slot_depth
    bricks = levels.shape[0]
    bricks_group = bricks // groups
    bricks_dev = bricks_group // owners
    table_rows = -(-bricks * 8 // LANES)
    basis = block_data.shape[1]
    params = pltpu.CompilerParams(vmem_limit_bytes=32 * 1024 * 1024)

    outgoing = pl.pallas_call(
        functools.partial(pair_kernel, slot_depth, bricks_group),
        out_shape=jax.ShapeDtypeStruct((slots * SLOT_ROWS, LANES), jnp.float32),
        in_specs=[pl.BlockSpec(memory_space=pltpu.HBM)] * 7,
        out_specs=vmem(),
        scratch_shapes=[
            pltpu.SMEM((2, items), jnp.int32),
            pltpu.SMEM((items,), jnp.int32),
            pltpu.SMEM((items,), jnp.int32),
            pltpu.SMEM((bricks,), jnp.int32),
            pltpu.VMEM(block_data.shape, block_data.dtype),
            pltpu.VMEM((3, centres.shape[0], basis), jnp.float32),
            pltpu.VMEM(exponents.shape, jnp.float32),
            pltpu.VMEM((4, items, LANES), jnp.float32),
            pltpu.SemaphoreType.DMA((4,)),
            pltpu.SemaphoreType.DMA((5,)),
        ],
        compiler_params=params,
        name="pair_density",
    )(
        *(
            pltpu.with_memory_space_constraint(operand, pltpu.HBM)
            for operand in (
                item_pairs.T,
                dest_slot,
                brick_tag,
                levels,
                block_data,
                jnp.transpose(centres, (1, 0, 2)),
                exponents,
            )
        )
    )
    arrived = lax.all_to_all(
        outgoing.reshape(slots, 1, SLOT_ROWS * LANES),
        ("row", "col"),
        split_axis=0,
        concat_axis=0,
        tiled=True,
    ).reshape(outgoing.shape)
    rows, cols = lax.axis_size("row"), lax.axis_size("col")
    moves = moves_of(rows, owners)
    partial = pl.pallas_call(
        functools.partial(group_kernel, items, bricks_dev, moves),
        out_shape=[jax.ShapeDtypeStruct((bricks_dev * ROWS + table_rows, LANES), jnp.float32)]
        * (len(moves) + 1),
        in_specs=[vmem()],
        out_specs=[vmem()] * (len(moves) + 1),
        compiler_params=params,
        name="group_sum",
    )(arrived)
    parts = [partial[0]] + [
        lax.ppermute(piece, ("row", "col", "basis"), pairs_of(move, rows, cols))
        for piece, move in zip(partial[1:], moves)
    ]
    cell_map = pl.pallas_call(
        map_kernel,
        out_shape=jax.ShapeDtypeStruct((bricks_dev, ROWS, LANES), jnp.int32),
        in_specs=[vmem()],
        out_specs=vmem(),
        compiler_params=params,
        cost_estimate=pl.CostEstimate(flops=4_000_000, bytes_accessed=200_000, transcendentals=0),
        name="cell_map",
    )(cell_pos)
    return pl.pallas_call(
        cell_kernel,
        out_shape=jax.ShapeDtypeStruct((bricks_dev, EDGE * FACE), jnp.float32),
        in_specs=[vmem()] * (len(parts) + 2),
        out_specs=vmem(),
        compiler_params=params,
        name="cells",
    )(*parts, cell_map, jnp.transpose(corner_refs, (0, 2, 1)))


def solution(mesh):
    split = ("row", "col", "basis")
    return jax.shard_map(
        body,
        mesh=mesh,
        in_specs=(
            P(split, None, None),
            P(split, None),
            P(split),
            P(split),
            P(),
            P(),
            P(),
            P(split, None),
            P(split, None, None),
        ),
        out_specs=P(split, None),
        check_vma=False,
    )
```

```python
import functools

import jax
import jax.numpy as jnp
from jax import lax
from jax.experimental import pallas as pl
from jax.experimental.pallas import tpu as pltpu
from jax.sharding import PartitionSpec as P

EDGE = 16
FACE = EDGE * EDGE
LANES = 128
SHIFT = 7
ROWS = EDGE * FACE // LANES
COARSE = 0.2
SLOT_ROWS = ROWS + 1
TILE = 8


def lane_pick(values, index):
    return jnp.take_along_axis(values, index, axis=1, mode="promise_in_bounds")


def iota(shape, axis):
    return lax.broadcasted_iota(jnp.int32, shape, axis)


def axis_factors(coords, middle, decay):
    return jnp.exp(-decay * (coords - middle) ** 2)


def pair_kernel(
    slot_depth,
    bricks_group,
    pairs_hbm,
    dest_hbm,
    tag_hbm,
    levels_hbm,
    blocks_hbm,
    centres_hbm,
    exponents_hbm,
    out_ref,
    pairs_ref,
    dest_ref,
    tag_ref,
    levels_ref,
    blocks_ref,
    centres_ref,
    exponents_ref,
    corner_buf,
    list_sems,
    table_sems,
):
    items = blocks_ref.shape[0]
    slots = out_ref.shape[0] // SLOT_ROWS
    lists = [
        pltpu.make_async_copy(source, target, list_sems.at[n])
        for n, (source, target) in enumerate(
            (
                (pairs_hbm, pairs_ref),
                (dest_hbm, dest_ref),
                (tag_hbm, tag_ref),
                (levels_hbm, levels_ref),
            )
        )
    ]
    for copy in lists:
        copy.start()

    tables = [
        pltpu.make_async_copy(exponents_hbm, exponents_ref, table_sems.at[0]),
        pltpu.make_async_copy(blocks_hbm, blocks_ref, table_sems.at[1]),
    ]
    for copy in tables:
        copy.start()
    lists[0].wait()
    for k in range(items):
        for side in range(2):
            pltpu.make_async_copy(
                centres_hbm.at[:, pl.ds(pairs_ref[side, k], 1), :],
                centres_ref.at[2 * k + side],
                table_sems.at[2],
            ).start()
    for copy in lists[1:] + tables:
        copy.wait()
    pltpu.make_async_copy(centres_ref, centres_ref, table_sems.at[2]).wait()
    if slots != items:
        out_ref[...] = jnp.zeros_like(out_ref)
    steps = iota((EDGE, LANES), 0).astype(jnp.float32) - (EDGE - 1) / 2.0

    def one(k):
        target = dest_ref[k] // slot_depth * bricks_group + tag_ref[k]
        spacing = jnp.where(levels_ref[target] == 1, COARSE * 0.5, COARSE)
        coords = steps * spacing

        def factors(side):
            row = pl.ds(pairs_ref[side, k], 1)
            decay = exponents_ref[row, :]
            found = [axis_factors(coords, centres_ref[2 * k + side, d], decay) for d in range(3)]
            face = jnp.concatenate(
                [found[1][y : y + 1, :] * found[2] for y in range(EDGE)], axis=0
            )
            return found[0], face

        row_x, row_face = factors(0)
        col_x, col_face = factors(1)
        row_face = row_face.T
        block = blocks_ref[k]
        for x in range(EDGE):
            col = (col_x[x : x + 1, :] * col_face).astype(jnp.bfloat16)
            product = lax.dot_general(
                block, col, (((1,), (1,)), ((), ())), preferred_element_type=jnp.float32
            )
            weight = jnp.broadcast_to(row_x[x : x + 1, :], (LANES, block.shape[0])).T
            weight = jnp.concatenate([weight] * (FACE // LANES), axis=1)
            dens = jnp.sum(weight * row_face * product, axis=0, keepdims=True)
            for half in range(FACE // LANES):
                piece = dens[:, half * LANES : (half + 1) * LANES]
                out_ref[pl.ds(dest_ref[k] * SLOT_ROWS + 2 * x + half, 1), :] = piece
                if x in (0, EDGE - 1):
                    corner_buf[2 * (x // (EDGE - 1)) + half, pl.ds(k, 1), :] = piece

    for k in range(items):
        one(k)

    shape = (items, LANES)
    lane = iota(shape, 1)
    place = lane % 4
    low = jnp.where(place % 2 == 1, EDGE - 1, 0)
    high = (FACE - EDGE) % LANES + low
    source = jnp.where(place >= 2, high, low)
    found = [lane_pick(corner_buf[n], source) for n in range(4)]
    corner = lane % 8
    first = jnp.where(corner % 4 >= 2, found[1], found[0])
    last = jnp.where(corner % 4 >= 2, found[3], found[2])
    values = jnp.where(corner >= 4, last, first)
    row = iota(shape, 0)
    brick = jnp.zeros(shape, jnp.int32)
    for k in range(items):
        target = dest_ref[k] // slot_depth * bricks_group + tag_ref[k]
        brick = jnp.where(row == k, target, brick)
    placed = jnp.where(lane // 8 == row, values, 0.0)
    placed = jnp.where(lane == 8 * items + row, brick.astype(jnp.float32), placed)
    meta = jnp.sum(placed, axis=0, keepdims=True)
    last_lane = iota((1, LANES), 1) == LANES - 1
    if slots != items:

        @pl.loop(0, slots)
        def _(n):
            out_ref[pl.ds(n * SLOT_ROWS + ROWS, 1), :] = jnp.where(last_lane, -1.0, meta)

    for k in range(items):
        tagged = jnp.where(last_lane, tag_ref[k].astype(jnp.float32), meta)
        out_ref[pl.ds(dest_ref[k] * SLOT_ROWS + ROWS, 1), :] = tagged


def group_kernel(items, bricks_dev, moves, in_ref, *outs):
    me = lax.axis_index("basis")
    slots = in_ref.shape[0] // SLOT_ROWS
    meta = [in_ref[n * SLOT_ROWS + ROWS : (n + 1) * SLOT_ROWS, :] for n in range(slots)]
    tags = [jnp.broadcast_to(line[:, LANES - 1 :], (ROWS, LANES)) for line in meta]
    owned = sum(jnp.where(me == i, i, 0) for i in range(len(moves[0])))
    sends = []
    for out, move in zip(outs, [None, *moves]):
        owner = owned
        if move is not None:
            owner = sum(jnp.where(me == i, -1 if i == to else to, 0) for i, to in enumerate(move))
        sends.append(owner)
        for b in range(bricks_dev):
            brick = jnp.where(owner < 0, -2, owner * bricks_dev + b).astype(jnp.float32)
            total = jnp.zeros((ROWS, LANES), jnp.float32)
            for n in range(slots):
                dens = in_ref[n * SLOT_ROWS : n * SLOT_ROWS + ROWS, :]
                total = total + jnp.where(tags[n] == brick, dens, 0.0)
            out[b * ROWS : (b + 1) * ROWS, :] = total
    table_rows = outs[0].shape[0] - bricks_dev * ROWS
    shape = (TILE, LANES)
    lane = iota(shape, 1)
    lines = [jnp.zeros(shape, jnp.float32) for _ in range(table_rows)]
    for first in range(0, slots, TILE):
        block = jnp.concatenate(meta[first : first + TILE], axis=0)
        for k in range(items):
            values = lane_pick(block, 8 * k + (lane & 7))
            brick = lane_pick(block, jnp.full(shape, 8 * items + k, jnp.int32)).astype(jnp.int32)
            values = jnp.where((brick & 15) == lane >> 3, values, 0.0)
            for r in range(table_rows):
                lines[r] = lines[r] + jnp.where(brick >> 4 == r, values, 0.0)
    table = jnp.concatenate([jnp.sum(line, axis=0, keepdims=True) for line in lines], axis=0)
    for out, owner in zip(outs, sends):
        out[bricks_dev * ROWS :, :] = jnp.where(owner < 0, 0.0, table)


def map_kernel(cells_ref, out_ref):
    bricks_dev, cells = cells_ref.shape
    cell = (iota((LANES, cells), 1) + 1).astype(jnp.float32)
    for b in range(bricks_dev):
        position = cells_ref[b : b + 1, :]
        high = position >> SHIFT == iota((ROWS, cells), 0)
        low = (position & (LANES - 1)) == iota((LANES, cells), 0)
        found = lax.dot_general(
            high.astype(jnp.float32).astype(jnp.bfloat16),
            jnp.where(low, cell, 0.0).astype(jnp.bfloat16),
            (((1,), (1,)), ((), ())),
            preferred_element_type=jnp.float32,
        )
        out_ref[b] = found.astype(jnp.int32) - 1


def cell_kernel(*refs):
    *ins, map_ref, refs_ref, out_ref = refs
    bricks_dev, _, cells = refs_ref.shape
    total = ins[0][...]
    for part in ins[1:]:
        total = total + part[...]
    table = total[bricks_dev * ROWS :]
    chunk = (TILE, LANES)
    tiles = cells // LANES
    refs = [
        [refs_ref[b, :, c * LANES : (c + 1) * LANES] for c in range(tiles)]
        for b in range(bricks_dev)
    ]
    picked = [[jnp.zeros(chunk, jnp.float32) for _ in row] for row in refs]
    for r in range(table.shape[0]):
        line = jnp.broadcast_to(table[r : r + 1, :], chunk)
        for b in range(bricks_dev):
            for c, index in enumerate(refs[b]):
                found = lane_pick(line, (index & (LANES - 1)))
                picked[b][c] = jnp.where(index >> SHIFT == r, found, picked[b][c])
    for b in range(bricks_dev):
        cell = map_ref[b]
        mean = jnp.zeros((ROWS, LANES), jnp.float32)
        for c in range(tiles):
            line = jnp.sum(picked[b][c], axis=0, keepdims=True) * (0.5 / 8.0)
            found = lane_pick(jnp.broadcast_to(line, (ROWS, LANES)), (cell & (LANES - 1)))
            mean = jnp.where(cell >> SHIFT == c, found, mean)
        own = total[b * ROWS : (b + 1) * ROWS]
        result = jnp.where(cell >= 0, 0.5 * own + mean, own)
        for row in range(ROWS):
            out_ref[b : b + 1, row * LANES : (row + 1) * LANES] = result[row : row + 1, :]


def moves_of(rows, owners):
    if owners == 4 and rows % 2 == 0:
        return [(1, 3, 2, 0), (2, 1, 0, 3), (3, 0, 1, 2), (0, 2, 3, 1)]
    return [tuple((i + d) % owners for i in range(owners)) for d in range(1, owners)]


def pairs_of(move, rows, cols):
    owners = len(move)
    pairs = []
    for row in range(rows):
        for col in range(cols):
            for z, to in enumerate(move):
                target = row ^ 1 if to == z else row
                source = (row * cols + col) * owners + z
                pairs.append((source, (target * cols + col) * owners + to))
    return pairs


def vmem():
    return pl.BlockSpec(memory_space=pltpu.VMEM)


def body(
    block_data, item_pairs, dest_slot, brick_tag, centres, exponents, levels, cell_pos, corner_refs
):
    groups = lax.axis_size("row") * lax.axis_size("col")
    owners = lax.axis_size("basis")
    items = block_data.shape[0]
    slot_depth = max(1, items // groups)
    slots = groups * slot_depth
    bricks = levels.shape[0]
    bricks_group = bricks // groups
    bricks_dev = bricks_group // owners
    table_rows = -(-bricks * 8 // LANES)
    basis = block_data.shape[1]
    params = pltpu.CompilerParams(vmem_limit_bytes=32 * 1024 * 1024)

    outgoing = pl.pallas_call(
        functools.partial(pair_kernel, slot_depth, bricks_group),
        out_shape=jax.ShapeDtypeStruct((slots * SLOT_ROWS, LANES), jnp.float32),
        in_specs=[pl.BlockSpec(memory_space=pltpu.HBM)] * 7,
        out_specs=vmem(),
        scratch_shapes=[
            pltpu.SMEM((2, items), jnp.int32),
            pltpu.SMEM((items,), jnp.int32),
            pltpu.SMEM((items,), jnp.int32),
            pltpu.SMEM((bricks,), jnp.int32),
            pltpu.VMEM(block_data.shape, block_data.dtype),
            pltpu.VMEM((2 * items, 3, 1, basis), jnp.float32),
            pltpu.VMEM(exponents.shape, jnp.float32),
            pltpu.VMEM((4, items, LANES), jnp.float32),
            pltpu.SemaphoreType.DMA((4,)),
            pltpu.SemaphoreType.DMA((3,)),
        ],
        compiler_params=params,
        name="pair_density",
    )(
        *(
            pltpu.with_memory_space_constraint(operand, pltpu.HBM)
            for operand in (
                item_pairs.T,
                dest_slot,
                brick_tag,
                levels,
                block_data,
                jnp.transpose(centres, (1, 0, 2)),
                exponents,
            )
        )
    )
    arrived = lax.all_to_all(
        outgoing.reshape(slots, 1, SLOT_ROWS * LANES),
        ("row", "col"),
        split_axis=0,
        concat_axis=0,
        tiled=True,
    ).reshape(outgoing.shape)
    rows, cols = lax.axis_size("row"), lax.axis_size("col")
    moves = moves_of(rows, owners)
    partial = pl.pallas_call(
        functools.partial(group_kernel, items, bricks_dev, moves),
        out_shape=[jax.ShapeDtypeStruct((bricks_dev * ROWS + table_rows, LANES), jnp.float32)]
        * (len(moves) + 1),
        in_specs=[vmem()],
        out_specs=[vmem()] * (len(moves) + 1),
        compiler_params=params,
        name="group_sum",
    )(arrived)
    parts = [partial[0]] + [
        lax.ppermute(piece, ("row", "col", "basis"), pairs_of(move, rows, cols))
        for piece, move in zip(partial[1:], moves)
    ]
    cell_map = pl.pallas_call(
        map_kernel,
        out_shape=jax.ShapeDtypeStruct((bricks_dev, ROWS, LANES), jnp.int32),
        in_specs=[vmem()],
        out_specs=vmem(),
        compiler_params=params,
        cost_estimate=pl.CostEstimate(flops=4_000_000, bytes_accessed=200_000, transcendentals=0),
        name="cell_map",
    )(cell_pos)
    return pl.pallas_call(
        cell_kernel,
        out_shape=jax.ShapeDtypeStruct((bricks_dev, EDGE * FACE), jnp.float32),
        in_specs=[vmem()] * (len(parts) + 2),
        out_specs=vmem(),
        compiler_params=params,
        name="cells",
    )(*parts, cell_map, jnp.transpose(corner_refs, (0, 2, 1)))


def solution(mesh):
    split = ("row", "col", "basis")
    return jax.shard_map(
        body,
        mesh=mesh,
        in_specs=(
            P(split, None, None),
            P(split, None),
            P(split),
            P(split),
            P(),
            P(),
            P(),
            P(split, None),
            P(split, None, None),
        ),
        out_specs=P(split, None),
        check_vma=False,
    )
```

```python
import functools

import jax
import jax.numpy as jnp
from jax import lax
from jax.experimental import pallas as pl
from jax.experimental.pallas import tpu as pltpu
from jax.sharding import PartitionSpec as P

EDGE = 16
FACE = EDGE * EDGE
LANES = 128
SHIFT = 7
ROWS = EDGE * FACE // LANES
COARSE = 0.2
SLOT_ROWS = ROWS + 1
TILE = 8


def lane_pick(values, index):
    return jnp.take_along_axis(values, index, axis=1, mode="promise_in_bounds")


def iota(shape, axis):
    return lax.broadcasted_iota(jnp.int32, shape, axis)


def axis_factors(coords, middle, decay):
    return jnp.exp(-decay * (coords - middle) ** 2)


def pair_kernel(
    slot_depth,
    bricks_group,
    pairs_hbm,
    dest_hbm,
    tag_hbm,
    levels_hbm,
    blocks_hbm,
    centres_hbm,
    exponents_hbm,
    out_ref,
    pairs_ref,
    dest_ref,
    tag_ref,
    levels_ref,
    blocks_ref,
    centres_ref,
    exponents_ref,
    corner_buf,
    list_sems,
    table_sems,
):
    items = blocks_ref.shape[0]
    slots = out_ref.shape[0] // SLOT_ROWS
    lists = [
        pltpu.make_async_copy(source, target, list_sems.at[n])
        for n, (source, target) in enumerate(
            (
                (pairs_hbm, pairs_ref),
                (dest_hbm, dest_ref),
                (tag_hbm, tag_ref),
                (levels_hbm, levels_ref),
            )
        )
    ]
    for copy in lists:
        copy.start()

    table = pltpu.make_async_copy(exponents_hbm, exponents_ref, table_sems.at[0])
    blocks = pltpu.make_async_copy(blocks_hbm, blocks_ref, table_sems.at[1])
    table.start()
    lists[0].wait()
    for k in range(items):
        for side in range(2):
            pltpu.make_async_copy(
                centres_hbm.at[:, pl.ds(pairs_ref[side, k], 1), :],
                centres_ref.at[2 * k + side],
                table_sems.at[2],
            ).start()
    blocks.start()
    for copy in lists[1:] + [table]:
        copy.wait()
    pltpu.make_async_copy(centres_ref, centres_ref, table_sems.at[2]).wait()
    if slots != items:
        out_ref[...] = jnp.zeros_like(out_ref)
    steps = iota((EDGE, LANES), 0).astype(jnp.float32) - (EDGE - 1) / 2.0

    def one(k):
        target = dest_ref[k] // slot_depth * bricks_group + tag_ref[k]
        spacing = jnp.where(levels_ref[target] == 1, COARSE * 0.5, COARSE)
        coords = steps * spacing

        def factors(side):
            row = pl.ds(pairs_ref[side, k], 1)
            decay = exponents_ref[row, :]
            found = [axis_factors(coords, centres_ref[2 * k + side, d], decay) for d in range(3)]
            face = jnp.concatenate(
                [found[1][y : y + 1, :] * found[2] for y in range(EDGE)], axis=0
            )
            return found[0], face

        row_x, row_face = factors(0)
        col_x, col_face = factors(1)
        row_face = row_face.T
        if k == 0:
            blocks.wait()
        block = blocks_ref[k]
        for x in range(EDGE):
            col = (col_x[x : x + 1, :] * col_face).astype(jnp.bfloat16)
            product = lax.dot_general(
                block, col, (((1,), (1,)), ((), ())), preferred_element_type=jnp.float32
            )
            weight = jnp.broadcast_to(row_x[x : x + 1, :], (LANES, block.shape[0])).T
            weight = jnp.concatenate([weight] * (FACE // LANES), axis=1)
            dens = jnp.sum(weight * row_face * product, axis=0, keepdims=True)
            for half in range(FACE // LANES):
                piece = dens[:, half * LANES : (half + 1) * LANES]
                out_ref[pl.ds(dest_ref[k] * SLOT_ROWS + 2 * x + half, 1), :] = piece
                if x in (0, EDGE - 1):
                    corner_buf[2 * (x // (EDGE - 1)) + half, pl.ds(k, 1), :] = piece

    for k in range(items):
        one(k)

    shape = (items, LANES)
    lane = iota(shape, 1)
    place = lane % 4
    low = jnp.where(place % 2 == 1, EDGE - 1, 0)
    high = (FACE - EDGE) % LANES + low
    source = jnp.where(place >= 2, high, low)
    found = [lane_pick(corner_buf[n], source) for n in range(4)]
    corner = lane % 8
    first = jnp.where(corner % 4 >= 2, found[1], found[0])
    last = jnp.where(corner % 4 >= 2, found[3], found[2])
    values = jnp.where(corner >= 4, last, first)
    row = iota(shape, 0)
    brick = jnp.zeros(shape, jnp.int32)
    for k in range(items):
        target = dest_ref[k] // slot_depth * bricks_group + tag_ref[k]
        brick = jnp.where(row == k, target, brick)
    placed = jnp.where(lane // 8 == row, values, 0.0)
    placed = jnp.where(lane == 8 * items + row, brick.astype(jnp.float32), placed)
    meta = jnp.sum(placed, axis=0, keepdims=True)
    last_lane = iota((1, LANES), 1) == LANES - 1
    if slots != items:

        @pl.loop(0, slots)
        def _(n):
            out_ref[pl.ds(n * SLOT_ROWS + ROWS, 1), :] = jnp.where(last_lane, -1.0, meta)

    for k in range(items):
        tagged = jnp.where(last_lane, tag_ref[k].astype(jnp.float32), meta)
        out_ref[pl.ds(dest_ref[k] * SLOT_ROWS + ROWS, 1), :] = tagged


def group_kernel(items, bricks_dev, moves, in_ref, *outs):
    me = lax.axis_index("basis")
    slots = in_ref.shape[0] // SLOT_ROWS
    meta = [in_ref[n * SLOT_ROWS + ROWS : (n + 1) * SLOT_ROWS, :] for n in range(slots)]
    tags = [jnp.broadcast_to(line[:, LANES - 1 :], (ROWS, LANES)) for line in meta]
    owned = sum(jnp.where(me == i, i, 0) for i in range(len(moves[0])))
    sends = []
    for out, move in zip(outs, [None, *moves]):
        owner = owned
        if move is not None:
            owner = sum(jnp.where(me == i, -1 if i == to else to, 0) for i, to in enumerate(move))
        sends.append(owner)
        for b in range(bricks_dev):
            brick = jnp.where(owner < 0, -2, owner * bricks_dev + b).astype(jnp.float32)
            total = jnp.zeros((ROWS, LANES), jnp.float32)
            for n in range(slots):
                dens = in_ref[n * SLOT_ROWS : n * SLOT_ROWS + ROWS, :]
                total = total + jnp.where(tags[n] == brick, dens, 0.0)
            out[b * ROWS : (b + 1) * ROWS, :] = total
    table_rows = outs[0].shape[0] - bricks_dev * ROWS
    shape = (TILE, LANES)
    lane = iota(shape, 1)
    lines = [jnp.zeros(shape, jnp.float32) for _ in range(table_rows)]
    for first in range(0, slots, TILE):
        block = jnp.concatenate(meta[first : first + TILE], axis=0)
        for k in range(items):
            values = lane_pick(block, 8 * k + (lane & 7))
            brick = lane_pick(block, jnp.full(shape, 8 * items + k, jnp.int32)).astype(jnp.int32)
            values = jnp.where((brick & 15) == lane >> 3, values, 0.0)
            for r in range(table_rows):
                lines[r] = lines[r] + jnp.where(brick >> 4 == r, values, 0.0)
    table = jnp.concatenate([jnp.sum(line, axis=0, keepdims=True) for line in lines], axis=0)
    for out, owner in zip(outs, sends):
        out[bricks_dev * ROWS :, :] = jnp.where(owner < 0, 0.0, table)


def map_kernel(cells_ref, out_ref):
    bricks_dev, cells = cells_ref.shape
    cell = (iota((LANES, cells), 1) + 1).astype(jnp.float32)
    for b in range(bricks_dev):
        position = cells_ref[b : b + 1, :]
        high = position >> SHIFT == iota((ROWS, cells), 0)
        low = (position & (LANES - 1)) == iota((LANES, cells), 0)
        found = lax.dot_general(
            high.astype(jnp.float32).astype(jnp.bfloat16),
            jnp.where(low, cell, 0.0).astype(jnp.bfloat16),
            (((1,), (1,)), ((), ())),
            preferred_element_type=jnp.float32,
        )
        out_ref[b] = found.astype(jnp.int32) - 1


def cell_kernel(*refs):
    *ins, map_ref, refs_ref, out_ref = refs
    bricks_dev, _, cells = refs_ref.shape
    total = ins[0][...]
    for part in ins[1:]:
        total = total + part[...]
    table = total[bricks_dev * ROWS :]
    chunk = (TILE, LANES)
    tiles = cells // LANES
    refs = [
        [refs_ref[b, :, c * LANES : (c + 1) * LANES] for c in range(tiles)]
        for b in range(bricks_dev)
    ]
    picked = [[jnp.zeros(chunk, jnp.float32) for _ in row] for row in refs]
    for r in range(table.shape[0]):
        line = jnp.broadcast_to(table[r : r + 1, :], chunk)
        for b in range(bricks_dev):
            for c, index in enumerate(refs[b]):
                found = lane_pick(line, (index & (LANES - 1)))
                picked[b][c] = jnp.where(index >> SHIFT == r, found, picked[b][c])
    for b in range(bricks_dev):
        cell = map_ref[b]
        mean = jnp.zeros((ROWS, LANES), jnp.float32)
        for c in range(tiles):
            line = jnp.sum(picked[b][c], axis=0, keepdims=True) * (0.5 / 8.0)
            found = lane_pick(jnp.broadcast_to(line, (ROWS, LANES)), (cell & (LANES - 1)))
            mean = jnp.where(cell >> SHIFT == c, found, mean)
        own = total[b * ROWS : (b + 1) * ROWS]
        result = jnp.where(cell >= 0, 0.5 * own + mean, own)
        for row in range(ROWS):
            out_ref[b : b + 1, row * LANES : (row + 1) * LANES] = result[row : row + 1, :]


def moves_of(rows, owners):
    if owners == 4 and rows % 2 == 0:
        return [(1, 3, 2, 0), (2, 1, 0, 3), (3, 0, 1, 2), (0, 2, 3, 1)]
    return [tuple((i + d) % owners for i in range(owners)) for d in range(1, owners)]


def pairs_of(move, rows, cols):
    owners = len(move)
    pairs = []
    for row in range(rows):
        for col in range(cols):
            for z, to in enumerate(move):
                target = row ^ 1 if to == z else row
                source = (row * cols + col) * owners + z
                pairs.append((source, (target * cols + col) * owners + to))
    return pairs


def vmem():
    return pl.BlockSpec(memory_space=pltpu.VMEM)


def body(
    block_data, item_pairs, dest_slot, brick_tag, centres, exponents, levels, cell_pos, corner_refs
):
    groups = lax.axis_size("row") * lax.axis_size("col")
    owners = lax.axis_size("basis")
    items = block_data.shape[0]
    slot_depth = max(1, items // groups)
    slots = groups * slot_depth
    bricks = levels.shape[0]
    bricks_group = bricks // groups
    bricks_dev = bricks_group // owners
    table_rows = -(-bricks * 8 // LANES)
    basis = block_data.shape[1]
    params = pltpu.CompilerParams(vmem_limit_bytes=32 * 1024 * 1024)

    outgoing = pl.pallas_call(
        functools.partial(pair_kernel, slot_depth, bricks_group),
        out_shape=jax.ShapeDtypeStruct((slots * SLOT_ROWS, LANES), jnp.float32),
        in_specs=[pl.BlockSpec(memory_space=pltpu.HBM)] * 7,
        out_specs=vmem(),
        scratch_shapes=[
            pltpu.SMEM((2, items), jnp.int32),
            pltpu.SMEM((items,), jnp.int32),
            pltpu.SMEM((items,), jnp.int32),
            pltpu.SMEM((bricks,), jnp.int32),
            pltpu.VMEM(block_data.shape, block_data.dtype),
            pltpu.VMEM((2 * items, 3, 1, basis), jnp.float32),
            pltpu.VMEM(exponents.shape, jnp.float32),
            pltpu.VMEM((4, items, LANES), jnp.float32),
            pltpu.SemaphoreType.DMA((4,)),
            pltpu.SemaphoreType.DMA((3,)),
        ],
        compiler_params=params,
        name="pair_density",
    )(
        *(
            pltpu.with_memory_space_constraint(operand, pltpu.HBM)
            for operand in (
                item_pairs.T,
                dest_slot,
                brick_tag,
                levels,
                block_data,
                jnp.transpose(centres, (1, 0, 2)),
                exponents,
            )
        )
    )
    arrived = lax.all_to_all(
        outgoing.reshape(slots, 1, SLOT_ROWS * LANES),
        ("row", "col"),
        split_axis=0,
        concat_axis=0,
        tiled=True,
    ).reshape(outgoing.shape)
    rows, cols = lax.axis_size("row"), lax.axis_size("col")
    moves = moves_of(rows, owners)
    partial = pl.pallas_call(
        functools.partial(group_kernel, items, bricks_dev, moves),
        out_shape=[jax.ShapeDtypeStruct((bricks_dev * ROWS + table_rows, LANES), jnp.float32)]
        * (len(moves) + 1),
        in_specs=[vmem()],
        out_specs=[vmem()] * (len(moves) + 1),
        compiler_params=params,
        name="group_sum",
    )(arrived)
    parts = [partial[0]] + [
        lax.ppermute(piece, ("row", "col", "basis"), pairs_of(move, rows, cols))
        for piece, move in zip(partial[1:], moves)
    ]
    cell_map = pl.pallas_call(
        map_kernel,
        out_shape=jax.ShapeDtypeStruct((bricks_dev, ROWS, LANES), jnp.int32),
        in_specs=[vmem()],
        out_specs=vmem(),
        compiler_params=params,
        cost_estimate=pl.CostEstimate(flops=4_000_000, bytes_accessed=200_000, transcendentals=0),
        name="cell_map",
    )(cell_pos)
    return pl.pallas_call(
        cell_kernel,
        out_shape=jax.ShapeDtypeStruct((bricks_dev, EDGE * FACE), jnp.float32),
        in_specs=[vmem()] * (len(parts) + 2),
        out_specs=vmem(),
        compiler_params=params,
        name="cells",
    )(*parts, cell_map, jnp.transpose(corner_refs, (0, 2, 1)))


def solution(mesh):
    split = ("row", "col", "basis")
    return jax.shard_map(
        body,
        mesh=mesh,
        in_specs=(
            P(split, None, None),
            P(split, None),
            P(split),
            P(split),
            P(),
            P(),
            P(),
            P(split, None),
            P(split, None, None),
        ),
        out_specs=P(split, None),
        check_vma=False,
    )
```

```python
import functools

import jax
import jax.numpy as jnp
from jax import lax
from jax.experimental import pallas as pl
from jax.experimental.pallas import tpu as pltpu
from jax.sharding import PartitionSpec as P

EDGE = 16
FACE = EDGE * EDGE
LANES = 128
SHIFT = 7
ROWS = EDGE * FACE // LANES
COARSE = 0.2
SLOT_ROWS = ROWS + 1
TILE = 8


def lane_pick(values, index):
    return jnp.take_along_axis(values, index, axis=1, mode="promise_in_bounds")


def iota(shape, axis):
    return lax.broadcasted_iota(jnp.int32, shape, axis)


def fold(tiles):
    row = iota((TILE, LANES), 0)
    step = 1
    while len(tiles) > 1:
        odd = (row & step) != 0
        tiles = [
            jnp.where(odd, b, a)
            + jnp.where(odd, pltpu.roll(b, step, 0), pltpu.roll(a, TILE - step, 0))
            for a, b in zip(tiles[::2], tiles[1::2])
        ]
        step *= 2
    return tiles[0]


def axis_factors(coords, middle, decay):
    return jnp.exp(-decay * (coords - middle) ** 2)


def pair_kernel(
    slot_depth,
    bricks_group,
    pairs_hbm,
    dest_hbm,
    tag_hbm,
    levels_hbm,
    blocks_hbm,
    centres_hbm,
    exponents_hbm,
    out_ref,
    pairs_ref,
    dest_ref,
    tag_ref,
    levels_ref,
    order_ref,
    blocks_ref,
    centres_ref,
    exponents_ref,
    corner_buf,
    list_sems,
    table_sems,
):
    items = blocks_ref.shape[0]
    slots = out_ref.shape[0] // SLOT_ROWS
    lists = [
        pltpu.make_async_copy(source, target, list_sems.at[n])
        for n, (source, target) in enumerate(
            (
                (pairs_hbm, pairs_ref),
                (dest_hbm, dest_ref),
                (tag_hbm, tag_ref),
                (levels_hbm, levels_ref),
            )
        )
    ]
    for copy in lists:
        copy.start()

    tables = [
        pltpu.make_async_copy(exponents_hbm, exponents_ref, table_sems.at[0]),
        pltpu.make_async_copy(centres_hbm, centres_ref, table_sems.at[1]),
        pltpu.make_async_copy(blocks_hbm, blocks_ref, table_sems.at[2]),
    ]
    for copy in tables:
        copy.start()
    for copy in lists + tables:
        copy.wait()
    if slots != items:
        out_ref[...] = jnp.zeros_like(out_ref)
    steps = iota((EDGE, LANES), 0).astype(jnp.float32) - (EDGE - 1) / 2.0

    if slots == items:
        for k in range(items):
            order_ref[dest_ref[k]] = k
        work = [(order_ref[slot], slot) for slot in range(slots)]
    else:
        work = [(k, dest_ref[k]) for k in range(items)]

    def one(n, k, slot):
        target = slot // slot_depth * bricks_group + tag_ref[k]
        spacing = jnp.where(levels_ref[target] == 1, COARSE * 0.5, COARSE)
        coords = steps * spacing

        def factors(side):
            row = pl.ds(pairs_ref[side, k], 1)
            decay = exponents_ref[row, :]
            found = [axis_factors(coords, centres_ref[d, row, :], decay) for d in range(3)]
            face = jnp.concatenate(
                [found[1][y : y + 1, :] * found[2] for y in range(EDGE)], axis=0
            )
            return found[0], face

        row_x, row_face = factors(0)
        col_x, col_face = factors(1)
        row_face = row_face.T
        block = blocks_ref[k]
        sums = []
        for x in range(EDGE):
            col = (col_x[x : x + 1, :] * col_face).astype(jnp.bfloat16)
            product = lax.dot_general(
                block, col, (((1,), (1,)), ((), ())), preferred_element_type=jnp.float32
            )
            weight = jnp.broadcast_to(row_x[x : x + 1, :], (LANES, block.shape[0])).T
            weight = jnp.concatenate([weight] * (FACE // LANES), axis=1)
            parts = (weight * row_face * product).reshape(-1, TILE, FACE).sum(axis=0)
            sums.extend(parts[:, c : c + LANES] for c in range(0, FACE, LANES))
            if len(sums) == TILE:
                tile = fold(sums)
                sums = []
                first = 2 * (x + 1) - TILE
                out_ref[pl.ds(slot * SLOT_ROWS + first, TILE), :] = tile
                if first == 0:
                    corner_buf[:2, n] = tile[:2]
                if first == ROWS - TILE:
                    corner_buf[2:, n] = tile[TILE - 2 :]

    for n, (k, slot) in enumerate(work):
        one(n, k, slot)

    shape = (items, LANES)
    lane = iota(shape, 1)
    place = lane % 4
    low = jnp.where(place % 2 == 1, EDGE - 1, 0)
    high = (FACE - EDGE) % LANES + low
    source = jnp.where(place >= 2, high, low)
    found = [lane_pick(corner_buf[n], source) for n in range(4)]
    corner = lane % 8
    first = jnp.where(corner % 4 >= 2, found[1], found[0])
    last = jnp.where(corner % 4 >= 2, found[3], found[2])
    values = jnp.where(corner >= 4, last, first)
    row = iota(shape, 0)
    brick = jnp.zeros(shape, jnp.int32)
    for n, (k, slot) in enumerate(work):
        target = slot // slot_depth * bricks_group + tag_ref[k]
        brick = jnp.where(row == n, target, brick)
    placed = jnp.where(lane // 8 == row, values, 0.0)
    placed = jnp.where(lane == 8 * items + row, brick.astype(jnp.float32), placed)
    meta = jnp.sum(placed, axis=0, keepdims=True)
    last_lane = iota((1, LANES), 1) == LANES - 1
    if slots != items:

        @pl.loop(0, slots)
        def _(n):
            out_ref[pl.ds(n * SLOT_ROWS + ROWS, 1), :] = jnp.where(last_lane, -1.0, meta)

    for k, slot in work:
        tagged = jnp.where(last_lane, tag_ref[k].astype(jnp.float32), meta)
        out_ref[pl.ds(slot * SLOT_ROWS + ROWS, 1), :] = tagged


def group_kernel(items, bricks_dev, moves, in_ref, *outs):
    me = lax.axis_index("basis")
    slots = in_ref.shape[0] // SLOT_ROWS
    meta = [in_ref[n * SLOT_ROWS + ROWS : (n + 1) * SLOT_ROWS, :] for n in range(slots)]
    tags = [jnp.broadcast_to(line[:, LANES - 1 :], (ROWS, LANES)) for line in meta]
    owned = sum(jnp.where(me == i, i, 0) for i in range(len(moves[0])))
    sends = []
    for out, move in zip(outs, [None, *moves]):
        owner = owned
        if move is not None:
            owner = sum(jnp.where(me == i, -1 if i == to else to, 0) for i, to in enumerate(move))
        sends.append(owner)
        for b in range(bricks_dev):
            brick = jnp.where(owner < 0, -2, owner * bricks_dev + b).astype(jnp.float32)
            total = jnp.zeros((ROWS, LANES), jnp.float32)
            for n in range(slots):
                dens = in_ref[n * SLOT_ROWS : n * SLOT_ROWS + ROWS, :]
                total = total + jnp.where(tags[n] == brick, dens, 0.0)
            out[b * ROWS : (b + 1) * ROWS, :] = total
    table_rows = outs[0].shape[0] - bricks_dev * ROWS
    shape = (TILE, LANES)
    lane = iota(shape, 1)
    lines = [jnp.zeros(shape, jnp.float32) for _ in range(table_rows)]
    for first in range(0, slots, TILE):
        block = jnp.concatenate(meta[first : first + TILE], axis=0)
        for k in range(items):
            values = lane_pick(block, 8 * k + (lane & 7))
            brick = lane_pick(block, jnp.full(shape, 8 * items + k, jnp.int32)).astype(jnp.int32)
            values = jnp.where((brick & 15) == lane >> 3, values, 0.0)
            for r in range(table_rows):
                lines[r] = lines[r] + jnp.where(brick >> 4 == r, values, 0.0)
    table = jnp.concatenate([jnp.sum(line, axis=0, keepdims=True) for line in lines], axis=0)
    for out, owner in zip(outs, sends):
        out[bricks_dev * ROWS :, :] = jnp.where(owner < 0, 0.0, table)


def map_kernel(cells_ref, out_ref):
    bricks_dev, cells = cells_ref.shape
    cell = (iota((LANES, cells), 1) + 1).astype(jnp.float32)
    for b in range(bricks_dev):
        position = cells_ref[b : b + 1, :]
        high = position >> SHIFT == iota((ROWS, cells), 0)
        low = (position & (LANES - 1)) == iota((LANES, cells), 0)
        found = lax.dot_general(
            high.astype(jnp.float32).astype(jnp.bfloat16),
            jnp.where(low, cell, 0.0).astype(jnp.bfloat16),
            (((1,), (1,)), ((), ())),
            preferred_element_type=jnp.float32,
        )
        out_ref[b] = found.astype(jnp.int32) - 1


def cell_kernel(*refs):
    *ins, map_ref, refs_ref, out_ref = refs
    bricks_dev, _, cells = refs_ref.shape
    total = ins[0][...]
    for part in ins[1:]:
        total = total + part[...]
    table = total[bricks_dev * ROWS :]
    chunk = (TILE, LANES)
    tiles = cells // LANES
    refs = [
        [refs_ref[b, :, c * LANES : (c + 1) * LANES] for c in range(tiles)]
        for b in range(bricks_dev)
    ]
    picked = [[jnp.zeros(chunk, jnp.float32) for _ in row] for row in refs]
    for r in range(table.shape[0]):
        line = jnp.broadcast_to(table[r : r + 1, :], chunk)
        for b in range(bricks_dev):
            for c, index in enumerate(refs[b]):
                found = lane_pick(line, (index & (LANES - 1)))
                picked[b][c] = jnp.where(index >> SHIFT == r, found, picked[b][c])
    for b in range(bricks_dev):
        cell = map_ref[b]
        mean = jnp.zeros((ROWS, LANES), jnp.float32)
        for c in range(tiles):
            line = jnp.sum(picked[b][c], axis=0, keepdims=True) * (0.5 / 8.0)
            found = lane_pick(jnp.broadcast_to(line, (ROWS, LANES)), (cell & (LANES - 1)))
            mean = jnp.where(cell >> SHIFT == c, found, mean)
        own = total[b * ROWS : (b + 1) * ROWS]
        result = jnp.where(cell >= 0, 0.5 * own + mean, own)
        for row in range(ROWS):
            out_ref[b : b + 1, row * LANES : (row + 1) * LANES] = result[row : row + 1, :]


def moves_of(rows, owners):
    if owners == 4 and rows % 2 == 0:
        return [(1, 3, 2, 0), (2, 1, 0, 3), (3, 0, 1, 2), (0, 2, 3, 1)]
    return [tuple((i + d) % owners for i in range(owners)) for d in range(1, owners)]


def pairs_of(move, rows, cols):
    owners = len(move)
    pairs = []
    for row in range(rows):
        for col in range(cols):
            for z, to in enumerate(move):
                target = row ^ 1 if to == z else row
                source = (row * cols + col) * owners + z
                pairs.append((source, (target * cols + col) * owners + to))
    return pairs


def vmem():
    return pl.BlockSpec(memory_space=pltpu.VMEM)


def body(
    block_data, item_pairs, dest_slot, brick_tag, centres, exponents, levels, cell_pos, corner_refs
):
    groups = lax.axis_size("row") * lax.axis_size("col")
    owners = lax.axis_size("basis")
    items = block_data.shape[0]
    slot_depth = max(1, items // groups)
    slots = groups * slot_depth
    bricks = levels.shape[0]
    bricks_group = bricks // groups
    bricks_dev = bricks_group // owners
    table_rows = -(-bricks * 8 // LANES)
    basis = block_data.shape[1]
    params = pltpu.CompilerParams(vmem_limit_bytes=32 * 1024 * 1024)

    outgoing = pl.pallas_call(
        functools.partial(pair_kernel, slot_depth, bricks_group),
        out_shape=jax.ShapeDtypeStruct((slots * SLOT_ROWS, LANES), jnp.float32),
        in_specs=[pl.BlockSpec(memory_space=pltpu.HBM)] * 7,
        out_specs=vmem(),
        scratch_shapes=[
            pltpu.SMEM((2, items), jnp.int32),
            pltpu.SMEM((items,), jnp.int32),
            pltpu.SMEM((items,), jnp.int32),
            pltpu.SMEM((bricks,), jnp.int32),
            pltpu.SMEM((items,), jnp.int32),
            pltpu.VMEM(block_data.shape, block_data.dtype),
            pltpu.VMEM((3, centres.shape[0], basis), jnp.float32),
            pltpu.VMEM(exponents.shape, jnp.float32),
            pltpu.VMEM((4, items, LANES), jnp.float32),
            pltpu.SemaphoreType.DMA((4,)),
            pltpu.SemaphoreType.DMA((3,)),
        ],
        compiler_params=params,
        name="pair_density",
    )(
        *(
            pltpu.with_memory_space_constraint(operand, pltpu.HBM)
            for operand in (
                item_pairs.T,
                dest_slot,
                brick_tag,
                levels,
                block_data,
                jnp.transpose(centres, (1, 0, 2)),
                exponents,
            )
        )
    )
    arrived = lax.all_to_all(
        outgoing.reshape(slots, 1, SLOT_ROWS * LANES),
        ("row", "col"),
        split_axis=0,
        concat_axis=0,
        tiled=True,
    ).reshape(outgoing.shape)
    rows, cols = lax.axis_size("row"), lax.axis_size("col")
    moves = moves_of(rows, owners)
    partial = pl.pallas_call(
        functools.partial(group_kernel, items, bricks_dev, moves),
        out_shape=[jax.ShapeDtypeStruct((bricks_dev * ROWS + table_rows, LANES), jnp.float32)]
        * (len(moves) + 1),
        in_specs=[vmem()],
        out_specs=[vmem()] * (len(moves) + 1),
        compiler_params=params,
        name="group_sum",
    )(arrived)
    parts = [partial[0]] + [
        lax.ppermute(piece, ("row", "col", "basis"), pairs_of(move, rows, cols))
        for piece, move in zip(partial[1:], moves)
    ]
    cell_map = pl.pallas_call(
        map_kernel,
        out_shape=jax.ShapeDtypeStruct((bricks_dev, ROWS, LANES), jnp.int32),
        in_specs=[vmem()],
        out_specs=vmem(),
        compiler_params=params,
        cost_estimate=pl.CostEstimate(flops=4_000_000, bytes_accessed=200_000, transcendentals=0),
        name="cell_map",
    )(cell_pos)
    return pl.pallas_call(
        cell_kernel,
        out_shape=jax.ShapeDtypeStruct((bricks_dev, EDGE * FACE), jnp.float32),
        in_specs=[vmem()] * (len(parts) + 2),
        out_specs=vmem(),
        compiler_params=params,
        name="cells",
    )(*parts, cell_map, jnp.transpose(corner_refs, (0, 2, 1)))


def solution(mesh):
    split = ("row", "col", "basis")
    return jax.shard_map(
        body,
        mesh=mesh,
        in_specs=(
            P(split, None, None),
            P(split, None),
            P(split),
            P(split),
            P(),
            P(),
            P(),
            P(split, None),
            P(split, None, None),
        ),
        out_specs=P(split, None),
        check_vma=False,
    )
```

```python
import functools

import jax
import jax.numpy as jnp
from jax import lax
from jax.experimental import pallas as pl
from jax.experimental.pallas import tpu as pltpu
from jax.sharding import PartitionSpec as P

EDGE = 16
FACE = EDGE * EDGE
LANES = 128
SHIFT = 7
ROWS = EDGE * FACE // LANES
COARSE = 0.2
SLOT_ROWS = ROWS + 1
TILE = 8


def lane_pick(values, index):
    return jnp.take_along_axis(values, index, axis=1, mode="promise_in_bounds")


def iota(shape, axis):
    return lax.broadcasted_iota(jnp.int32, shape, axis)


def fold(tiles):
    row = iota((TILE, LANES), 0)
    step = 1
    while len(tiles) > 1:
        odd = (row & step) != 0
        tiles = [
            jnp.where(odd, b, a)
            + jnp.where(odd, pltpu.roll(b, step, 0), pltpu.roll(a, TILE - step, 0))
            for a, b in zip(tiles[::2], tiles[1::2])
        ]
        step *= 2
    return tiles[0]


def axis_factors(coords, middle, decay):
    return jnp.exp(-decay * (coords - middle) ** 2)


def pair_kernel(
    slot_depth,
    bricks_group,
    pairs_hbm,
    dest_hbm,
    tag_hbm,
    levels_hbm,
    blocks_hbm,
    centres_hbm,
    exponents_hbm,
    out_ref,
    pairs_ref,
    dest_ref,
    tag_ref,
    levels_ref,
    order_ref,
    blocks_ref,
    centres_ref,
    exponents_ref,
    corner_buf,
    list_sems,
    table_sems,
):
    items = blocks_ref.shape[0]
    slots = out_ref.shape[0] // SLOT_ROWS
    lists = [
        pltpu.make_async_copy(source, target, list_sems.at[n])
        for n, (source, target) in enumerate(
            (
                (pairs_hbm, pairs_ref),
                (dest_hbm, dest_ref),
                (tag_hbm, tag_ref),
                (levels_hbm, levels_ref),
            )
        )
    ]
    for copy in lists:
        copy.start()

    lists[0].wait()
    for k in range(items):
        for side in range(2):
            row = pl.ds(pairs_ref[side, k], 1)
            at = 2 * k + side
            pltpu.make_async_copy(
                centres_hbm.at[:, row, :], centres_ref.at[at], table_sems.at[0]
            ).start()
            pltpu.make_async_copy(
                exponents_hbm.at[row, :], exponents_ref.at[at], table_sems.at[1]
            ).start()
    blocks = pltpu.make_async_copy(blocks_hbm, blocks_ref, table_sems.at[2])
    blocks.start()
    for copy in lists[1:]:
        copy.wait()
    pltpu.make_async_copy(centres_ref, centres_ref, table_sems.at[0]).wait()
    pltpu.make_async_copy(exponents_ref, exponents_ref, table_sems.at[1]).wait()
    blocks.wait()
    if slots != items:
        out_ref[...] = jnp.zeros_like(out_ref)
    steps = iota((EDGE, LANES), 0).astype(jnp.float32) - (EDGE - 1) / 2.0

    if slots == items:
        for k in range(items):
            order_ref[dest_ref[k]] = k
        work = [(order_ref[slot], slot) for slot in range(slots)]
    else:
        work = [(k, dest_ref[k]) for k in range(items)]

    def one(n, k, slot):
        target = slot // slot_depth * bricks_group + tag_ref[k]
        spacing = jnp.where(levels_ref[target] == 1, COARSE * 0.5, COARSE)
        coords = steps * spacing

        def factors(side):
            at = 2 * k + side
            decay = exponents_ref[at]
            found = [axis_factors(coords, centres_ref[at, d], decay) for d in range(3)]
            face = jnp.concatenate(
                [found[1][y : y + 1, :] * found[2] for y in range(EDGE)], axis=0
            )
            return found[0], face

        row_x, row_face = factors(0)
        col_x, col_face = factors(1)
        row_face = row_face.T
        block = blocks_ref[k]
        sums = []
        for x in range(EDGE):
            col = (col_x[x : x + 1, :] * col_face).astype(jnp.bfloat16)
            product = lax.dot_general(
                block, col, (((1,), (1,)), ((), ())), preferred_element_type=jnp.float32
            )
            weight = jnp.broadcast_to(row_x[x : x + 1, :], (LANES, block.shape[0])).T
            weight = jnp.concatenate([weight] * (FACE // LANES), axis=1)
            parts = (weight * row_face * product).reshape(-1, TILE, FACE).sum(axis=0)
            sums.extend(parts[:, c : c + LANES] for c in range(0, FACE, LANES))
            if len(sums) == TILE:
                tile = fold(sums)
                sums = []
                first = 2 * (x + 1) - TILE
                out_ref[pl.ds(slot * SLOT_ROWS + first, TILE), :] = tile
                if first == 0:
                    corner_buf[:2, n] = tile[:2]
                if first == ROWS - TILE:
                    corner_buf[2:, n] = tile[TILE - 2 :]

    for n, (k, slot) in enumerate(work):
        one(n, k, slot)

    shape = (items, LANES)
    lane = iota(shape, 1)
    place = lane % 4
    low = jnp.where(place % 2 == 1, EDGE - 1, 0)
    high = (FACE - EDGE) % LANES + low
    source = jnp.where(place >= 2, high, low)
    found = [lane_pick(corner_buf[n], source) for n in range(4)]
    corner = lane % 8
    first = jnp.where(corner % 4 >= 2, found[1], found[0])
    last = jnp.where(corner % 4 >= 2, found[3], found[2])
    values = jnp.where(corner >= 4, last, first)
    row = iota(shape, 0)
    brick = jnp.zeros(shape, jnp.int32)
    for n, (k, slot) in enumerate(work):
        target = slot // slot_depth * bricks_group + tag_ref[k]
        brick = jnp.where(row == n, target, brick)
    placed = jnp.where(lane // 8 == row, values, 0.0)
    placed = jnp.where(lane == 8 * items + row, brick.astype(jnp.float32), placed)
    meta = jnp.sum(placed, axis=0, keepdims=True)
    last_lane = iota((1, LANES), 1) == LANES - 1
    if slots != items:

        @pl.loop(0, slots)
        def _(n):
            out_ref[pl.ds(n * SLOT_ROWS + ROWS, 1), :] = jnp.where(last_lane, -1.0, meta)

    for k, slot in work:
        tagged = jnp.where(last_lane, tag_ref[k].astype(jnp.float32), meta)
        out_ref[pl.ds(slot * SLOT_ROWS + ROWS, 1), :] = tagged


def group_kernel(items, bricks_dev, moves, in_ref, *outs):
    me = lax.axis_index("basis")
    slots = in_ref.shape[0] // SLOT_ROWS
    meta = [in_ref[n * SLOT_ROWS + ROWS : (n + 1) * SLOT_ROWS, :] for n in range(slots)]
    tags = [jnp.broadcast_to(line[:, LANES - 1 :], (ROWS, LANES)) for line in meta]
    owned = sum(jnp.where(me == i, i, 0) for i in range(len(moves[0])))
    sends = []
    for out, move in zip(outs, [None, *moves]):
        owner = owned
        if move is not None:
            owner = sum(jnp.where(me == i, -1 if i == to else to, 0) for i, to in enumerate(move))
        sends.append(owner)
        for b in range(bricks_dev):
            brick = jnp.where(owner < 0, -2, owner * bricks_dev + b).astype(jnp.float32)
            total = jnp.zeros((ROWS, LANES), jnp.float32)
            for n in range(slots):
                dens = in_ref[n * SLOT_ROWS : n * SLOT_ROWS + ROWS, :]
                total = total + jnp.where(tags[n] == brick, dens, 0.0)
            out[b * ROWS : (b + 1) * ROWS, :] = total
    table_rows = outs[0].shape[0] - bricks_dev * ROWS
    shape = (TILE, LANES)
    lane = iota(shape, 1)
    lines = [jnp.zeros(shape, jnp.float32) for _ in range(table_rows)]
    for first in range(0, slots, TILE):
        block = jnp.concatenate(meta[first : first + TILE], axis=0)
        for k in range(items):
            values = lane_pick(block, 8 * k + (lane & 7))
            brick = lane_pick(block, jnp.full(shape, 8 * items + k, jnp.int32)).astype(jnp.int32)
            values = jnp.where((brick & 15) == lane >> 3, values, 0.0)
            for r in range(table_rows):
                lines[r] = lines[r] + jnp.where(brick >> 4 == r, values, 0.0)
    table = jnp.concatenate([jnp.sum(line, axis=0, keepdims=True) for line in lines], axis=0)
    for out, owner in zip(outs, sends):
        out[bricks_dev * ROWS :, :] = jnp.where(owner < 0, 0.0, table)


def map_kernel(cells_ref, out_ref):
    bricks_dev, cells = cells_ref.shape
    cell = (iota((LANES, cells), 1) + 1).astype(jnp.float32)
    for b in range(bricks_dev):
        position = cells_ref[b : b + 1, :]
        high = position >> SHIFT == iota((ROWS, cells), 0)
        low = (position & (LANES - 1)) == iota((LANES, cells), 0)
        found = lax.dot_general(
            high.astype(jnp.float32).astype(jnp.bfloat16),
            jnp.where(low, cell, 0.0).astype(jnp.bfloat16),
            (((1,), (1,)), ((), ())),
            preferred_element_type=jnp.float32,
        )
        out_ref[b] = found.astype(jnp.int32) - 1


def cell_kernel(*refs):
    *ins, map_ref, refs_ref, out_ref = refs
    bricks_dev, _, cells = refs_ref.shape
    total = ins[0][...]
    for part in ins[1:]:
        total = total + part[...]
    table = total[bricks_dev * ROWS :]
    chunk = (TILE, LANES)
    tiles = cells // LANES
    refs = [
        [refs_ref[b, :, c * LANES : (c + 1) * LANES] for c in range(tiles)]
        for b in range(bricks_dev)
    ]
    picked = [[jnp.zeros(chunk, jnp.float32) for _ in row] for row in refs]
    for r in range(table.shape[0]):
        line = jnp.broadcast_to(table[r : r + 1, :], chunk)
        for b in range(bricks_dev):
            for c, index in enumerate(refs[b]):
                found = lane_pick(line, (index & (LANES - 1)))
                picked[b][c] = jnp.where(index >> SHIFT == r, found, picked[b][c])
    for b in range(bricks_dev):
        cell = map_ref[b]
        mean = jnp.zeros((ROWS, LANES), jnp.float32)
        for c in range(tiles):
            line = jnp.sum(picked[b][c], axis=0, keepdims=True) * (0.5 / 8.0)
            found = lane_pick(jnp.broadcast_to(line, (ROWS, LANES)), (cell & (LANES - 1)))
            mean = jnp.where(cell >> SHIFT == c, found, mean)
        own = total[b * ROWS : (b + 1) * ROWS]
        result = jnp.where(cell >= 0, 0.5 * own + mean, own)
        for row in range(ROWS):
            out_ref[b : b + 1, row * LANES : (row + 1) * LANES] = result[row : row + 1, :]


def moves_of(rows, owners):
    if owners == 4 and rows % 2 == 0:
        return [(1, 3, 2, 0), (2, 1, 0, 3), (3, 0, 1, 2), (0, 2, 3, 1)]
    return [tuple((i + d) % owners for i in range(owners)) for d in range(1, owners)]


def pairs_of(move, rows, cols):
    owners = len(move)
    pairs = []
    for row in range(rows):
        for col in range(cols):
            for z, to in enumerate(move):
                target = row ^ 1 if to == z else row
                source = (row * cols + col) * owners + z
                pairs.append((source, (target * cols + col) * owners + to))
    return pairs


def vmem():
    return pl.BlockSpec(memory_space=pltpu.VMEM)


def body(
    block_data, item_pairs, dest_slot, brick_tag, centres, exponents, levels, cell_pos, corner_refs
):
    groups = lax.axis_size("row") * lax.axis_size("col")
    owners = lax.axis_size("basis")
    items = block_data.shape[0]
    slot_depth = max(1, items // groups)
    slots = groups * slot_depth
    bricks = levels.shape[0]
    bricks_group = bricks // groups
    bricks_dev = bricks_group // owners
    table_rows = -(-bricks * 8 // LANES)
    basis = block_data.shape[1]
    params = pltpu.CompilerParams(vmem_limit_bytes=32 * 1024 * 1024)

    outgoing = pl.pallas_call(
        functools.partial(pair_kernel, slot_depth, bricks_group),
        out_shape=jax.ShapeDtypeStruct((slots * SLOT_ROWS, LANES), jnp.float32),
        in_specs=[pl.BlockSpec(memory_space=pltpu.HBM)] * 7,
        out_specs=vmem(),
        scratch_shapes=[
            pltpu.SMEM((2, items), jnp.int32),
            pltpu.SMEM((items,), jnp.int32),
            pltpu.SMEM((items,), jnp.int32),
            pltpu.SMEM((bricks,), jnp.int32),
            pltpu.SMEM((items,), jnp.int32),
            pltpu.VMEM(block_data.shape, block_data.dtype),
            pltpu.VMEM((2 * items, 3, 1, basis), jnp.float32),
            pltpu.VMEM((2 * items, 1, basis), jnp.float32),
            pltpu.VMEM((4, items, LANES), jnp.float32),
            pltpu.SemaphoreType.DMA((4,)),
            pltpu.SemaphoreType.DMA((3,)),
        ],
        compiler_params=params,
        name="pair_density",
    )(
        *(
            pltpu.with_memory_space_constraint(operand, pltpu.HBM)
            for operand in (
                item_pairs.T,
                dest_slot,
                brick_tag,
                levels,
                block_data,
                jnp.transpose(centres, (1, 0, 2)),
                exponents,
            )
        )
    )
    arrived = lax.all_to_all(
        outgoing.reshape(slots, 1, SLOT_ROWS * LANES),
        ("row", "col"),
        split_axis=0,
        concat_axis=0,
        tiled=True,
    ).reshape(outgoing.shape)
    rows, cols = lax.axis_size("row"), lax.axis_size("col")
    moves = moves_of(rows, owners)
    partial = pl.pallas_call(
        functools.partial(group_kernel, items, bricks_dev, moves),
        out_shape=[jax.ShapeDtypeStruct((bricks_dev * ROWS + table_rows, LANES), jnp.float32)]
        * (len(moves) + 1),
        in_specs=[vmem()],
        out_specs=[vmem()] * (len(moves) + 1),
        compiler_params=params,
        name="group_sum",
    )(arrived)
    parts = [partial[0]] + [
        lax.ppermute(piece, ("row", "col", "basis"), pairs_of(move, rows, cols))
        for piece, move in zip(partial[1:], moves)
    ]
    cell_map = pl.pallas_call(
        map_kernel,
        out_shape=jax.ShapeDtypeStruct((bricks_dev, ROWS, LANES), jnp.int32),
        in_specs=[vmem()],
        out_specs=vmem(),
        compiler_params=params,
        cost_estimate=pl.CostEstimate(flops=4_000_000, bytes_accessed=200_000, transcendentals=0),
        name="cell_map",
    )(cell_pos)
    return pl.pallas_call(
        cell_kernel,
        out_shape=jax.ShapeDtypeStruct((bricks_dev, EDGE * FACE), jnp.float32),
        in_specs=[vmem()] * (len(parts) + 2),
        out_specs=vmem(),
        compiler_params=params,
        name="cells",
    )(*parts, cell_map, jnp.transpose(corner_refs, (0, 2, 1)))


def solution(mesh):
    split = ("row", "col", "basis")
    return jax.shard_map(
        body,
        mesh=mesh,
        in_specs=(
            P(split, None, None),
            P(split, None),
            P(split),
            P(split),
            P(),
            P(),
            P(),
            P(split, None),
            P(split, None, None),
        ),
        out_specs=P(split, None),
        check_vma=False,
    )
```

```python
import functools

import jax
import jax.numpy as jnp
from jax import lax
from jax.experimental import pallas as pl
from jax.experimental.pallas import tpu as pltpu
from jax.sharding import PartitionSpec as P

EDGE = 16
FACE = EDGE * EDGE
LANES = 128
SHIFT = 7
ROWS = EDGE * FACE // LANES
COARSE = 0.2
SLOT_ROWS = ROWS + 1
TILE = 8


def lane_pick(values, index):
    return jnp.take_along_axis(values, index, axis=1, mode="promise_in_bounds")


def iota(shape, axis):
    return lax.broadcasted_iota(jnp.int32, shape, axis)


def fold(tiles):
    row = iota((TILE, LANES), 0)
    step = 1
    while len(tiles) > 1:
        odd = (row & step) != 0
        tiles = [
            jnp.where(odd, b, a)
            + jnp.where(odd, pltpu.roll(b, step, 0), pltpu.roll(a, TILE - step, 0))
            for a, b in zip(tiles[::2], tiles[1::2])
        ]
        step *= 2
    return tiles[0]


def axis_factors(coords, middle, decay):
    return jnp.exp(-decay * (coords - middle) ** 2)


def pair_kernel(
    slot_depth,
    bricks_group,
    pairs_hbm,
    dest_hbm,
    tag_hbm,
    levels_hbm,
    blocks_hbm,
    centres_hbm,
    exponents_hbm,
    out_ref,
    pairs_ref,
    dest_ref,
    tag_ref,
    levels_ref,
    order_ref,
    blocks_ref,
    centres_ref,
    exponents_ref,
    corner_buf,
    list_sems,
    table_sems,
):
    items = blocks_ref.shape[0]
    slots = out_ref.shape[0] // SLOT_ROWS
    lists = [
        pltpu.make_async_copy(source, target, list_sems.at[n])
        for n, (source, target) in enumerate(
            (
                (pairs_hbm, pairs_ref),
                (dest_hbm, dest_ref),
                (tag_hbm, tag_ref),
                (levels_hbm, levels_ref),
            )
        )
    ]
    for copy in lists:
        copy.start()

    tables = [
        pltpu.make_async_copy(exponents_hbm, exponents_ref, table_sems.at[0]),
        pltpu.make_async_copy(centres_hbm, centres_ref, table_sems.at[1]),
        pltpu.make_async_copy(blocks_hbm, blocks_ref, table_sems.at[2]),
    ]
    for copy in tables:
        copy.start()
    for copy in lists + tables:
        copy.wait()
    if slots != items:
        out_ref[...] = jnp.zeros_like(out_ref)
    steps = iota((EDGE, LANES), 0).astype(jnp.float32) - (EDGE - 1) / 2.0

    if slots == items:
        for k in range(items):
            order_ref[dest_ref[k]] = k
        work = [(order_ref[slot], slot) for slot in range(slots)]
    else:
        work = [(k, dest_ref[k]) for k in range(items)]

    def prepare(k, slot):
        target = slot // slot_depth * bricks_group + tag_ref[k]
        spacing = jnp.where(levels_ref[target] == 1, COARSE * 0.5, COARSE)
        coords = steps * spacing

        def factors(side):
            row = pl.ds(pairs_ref[side, k], 1)
            decay = exponents_ref[row, :]
            found = [axis_factors(coords, centres_ref[d, row, :], decay) for d in range(3)]
            face = jnp.concatenate(
                [found[1][y : y + 1, :] * found[2] for y in range(EDGE)], axis=0
            )
            return found[0], face

        row_x, row_face = factors(0)
        return row_x, row_face.T, *factors(1), blocks_ref[k]

    def multiply(ready, x):
        _, _, col_x, col_face, block = ready
        col = (col_x[x : x + 1, :] * col_face).astype(jnp.bfloat16)
        return lax.dot_general(
            block, col, (((1,), (1,)), ((), ())), preferred_element_type=jnp.float32
        )

    def reduce(ready, x, product, sums):
        row_x, row_face = ready[:2]
        weight = jnp.broadcast_to(row_x[x : x + 1, :], (LANES, row_face.shape[0])).T
        weight = jnp.concatenate([weight] * (FACE // LANES), axis=1)
        parts = (weight * row_face * product).reshape(-1, TILE, FACE).sum(axis=0)
        sums.extend(parts[:, c : c + LANES] for c in range(0, FACE, LANES))

    def store(n, slot, x, sums):
        tile = fold(sums)
        sums.clear()
        first = 2 * (x + 1) - TILE
        out_ref[pl.ds(slot * SLOT_ROWS + first, TILE), :] = tile
        if first == 0:
            corner_buf[:2, n] = tile[:2]
        if first == ROWS - TILE:
            corner_buf[2:, n] = tile[TILE - 2 :]

    ahead, early = 1, 8
    flat = [(n, x) for n in range(items) for x in range(EDGE)]
    ready, products, sums = {0: prepare(*work[0])}, {}, []
    for at in range(-ahead, len(flat)):
        if at + ahead < len(flat):
            n, x = flat[at + ahead]
            products[n, x] = multiply(ready[n], x)
            if x == early and n + 1 < items:
                ready[n + 1] = prepare(*work[n + 1])
        if at >= 0:
            n, x = flat[at]
            reduce(ready[n], x, products.pop((n, x)), sums)
            if len(sums) == TILE:
                store(n, work[n][1], x, sums)

    shape = (items, LANES)
    lane = iota(shape, 1)
    place = lane % 4
    low = jnp.where(place % 2 == 1, EDGE - 1, 0)
    high = (FACE - EDGE) % LANES + low
    source = jnp.where(place >= 2, high, low)
    found = [lane_pick(corner_buf[n], source) for n in range(4)]
    corner = lane % 8
    first = jnp.where(corner % 4 >= 2, found[1], found[0])
    last = jnp.where(corner % 4 >= 2, found[3], found[2])
    values = jnp.where(corner >= 4, last, first)
    row = iota(shape, 0)
    brick = jnp.zeros(shape, jnp.int32)
    for n, (k, slot) in enumerate(work):
        target = slot // slot_depth * bricks_group + tag_ref[k]
        brick = jnp.where(row == n, target, brick)
    placed = jnp.where(lane // 8 == row, values, 0.0)
    placed = jnp.where(lane == 8 * items + row, brick.astype(jnp.float32), placed)
    meta = jnp.sum(placed, axis=0, keepdims=True)
    last_lane = iota((1, LANES), 1) == LANES - 1
    if slots != items:

        @pl.loop(0, slots)
        def _(n):
            out_ref[pl.ds(n * SLOT_ROWS + ROWS, 1), :] = jnp.where(last_lane, -1.0, meta)

    for k, slot in work:
        tagged = jnp.where(last_lane, tag_ref[k].astype(jnp.float32), meta)
        out_ref[pl.ds(slot * SLOT_ROWS + ROWS, 1), :] = tagged


def group_kernel(items, bricks_dev, moves, in_ref, *outs):
    me = lax.axis_index("basis")
    slots = in_ref.shape[0] // SLOT_ROWS
    meta = [in_ref[n * SLOT_ROWS + ROWS : (n + 1) * SLOT_ROWS, :] for n in range(slots)]
    tags = [jnp.broadcast_to(line[:, LANES - 1 :], (ROWS, LANES)) for line in meta]
    owned = sum(jnp.where(me == i, i, 0) for i in range(len(moves[0])))
    sends = []
    for out, move in zip(outs, [None, *moves]):
        owner = owned
        if move is not None:
            owner = sum(jnp.where(me == i, -1 if i == to else to, 0) for i, to in enumerate(move))
        sends.append(owner)
        for b in range(bricks_dev):
            brick = jnp.where(owner < 0, -2, owner * bricks_dev + b).astype(jnp.float32)
            total = jnp.zeros((ROWS, LANES), jnp.float32)
            for n in range(slots):
                dens = in_ref[n * SLOT_ROWS : n * SLOT_ROWS + ROWS, :]
                total = total + jnp.where(tags[n] == brick, dens, 0.0)
            out[b * ROWS : (b + 1) * ROWS, :] = total
    table_rows = outs[0].shape[0] - bricks_dev * ROWS
    shape = (TILE, LANES)
    lane = iota(shape, 1)
    lines = [jnp.zeros(shape, jnp.float32) for _ in range(table_rows)]
    for first in range(0, slots, TILE):
        block = jnp.concatenate(meta[first : first + TILE], axis=0)
        for k in range(items):
            values = lane_pick(block, 8 * k + (lane & 7))
            brick = lane_pick(block, jnp.full(shape, 8 * items + k, jnp.int32)).astype(jnp.int32)
            values = jnp.where((brick & 15) == lane >> 3, values, 0.0)
            for r in range(table_rows):
                lines[r] = lines[r] + jnp.where(brick >> 4 == r, values, 0.0)
    table = jnp.concatenate([jnp.sum(line, axis=0, keepdims=True) for line in lines], axis=0)
    for out, owner in zip(outs, sends):
        out[bricks_dev * ROWS :, :] = jnp.where(owner < 0, 0.0, table)


def map_kernel(cells_ref, out_ref):
    bricks_dev, cells = cells_ref.shape
    cell = (iota((LANES, cells), 1) + 1).astype(jnp.float32)
    for b in range(bricks_dev):
        position = cells_ref[b : b + 1, :]
        high = position >> SHIFT == iota((ROWS, cells), 0)
        low = (position & (LANES - 1)) == iota((LANES, cells), 0)
        found = lax.dot_general(
            high.astype(jnp.float32).astype(jnp.bfloat16),
            jnp.where(low, cell, 0.0).astype(jnp.bfloat16),
            (((1,), (1,)), ((), ())),
            preferred_element_type=jnp.float32,
        )
        out_ref[b] = found.astype(jnp.int32) - 1


def cell_kernel(*refs):
    *ins, map_ref, refs_ref, out_ref = refs
    bricks_dev, _, cells = refs_ref.shape
    total = ins[0][...]
    for part in ins[1:]:
        total = total + part[...]
    table = total[bricks_dev * ROWS :]
    chunk = (TILE, LANES)
    tiles = cells // LANES
    refs = [
        [refs_ref[b, :, c * LANES : (c + 1) * LANES] for c in range(tiles)]
        for b in range(bricks_dev)
    ]
    picked = [[jnp.zeros(chunk, jnp.float32) for _ in row] for row in refs]
    for r in range(table.shape[0]):
        line = jnp.broadcast_to(table[r : r + 1, :], chunk)
        for b in range(bricks_dev):
            for c, index in enumerate(refs[b]):
                found = lane_pick(line, (index & (LANES - 1)))
                picked[b][c] = jnp.where(index >> SHIFT == r, found, picked[b][c])
    for b in range(bricks_dev):
        cell = map_ref[b]
        mean = jnp.zeros((ROWS, LANES), jnp.float32)
        for c in range(tiles):
            line = jnp.sum(picked[b][c], axis=0, keepdims=True) * (0.5 / 8.0)
            found = lane_pick(jnp.broadcast_to(line, (ROWS, LANES)), (cell & (LANES - 1)))
            mean = jnp.where(cell >> SHIFT == c, found, mean)
        own = total[b * ROWS : (b + 1) * ROWS]
        result = jnp.where(cell >= 0, 0.5 * own + mean, own)
        for row in range(ROWS):
            out_ref[b : b + 1, row * LANES : (row + 1) * LANES] = result[row : row + 1, :]


def moves_of(rows, owners):
    if owners == 4 and rows % 2 == 0:
        return [(1, 3, 2, 0), (2, 1, 0, 3), (3, 0, 1, 2), (0, 2, 3, 1)]
    return [tuple((i + d) % owners for i in range(owners)) for d in range(1, owners)]


def pairs_of(move, rows, cols):
    owners = len(move)
    pairs = []
    for row in range(rows):
        for col in range(cols):
            for z, to in enumerate(move):
                target = row ^ 1 if to == z else row
                source = (row * cols + col) * owners + z
                pairs.append((source, (target * cols + col) * owners + to))
    return pairs


def vmem():
    return pl.BlockSpec(memory_space=pltpu.VMEM)


def body(
    block_data, item_pairs, dest_slot, brick_tag, centres, exponents, levels, cell_pos, corner_refs
):
    groups = lax.axis_size("row") * lax.axis_size("col")
    owners = lax.axis_size("basis")
    items = block_data.shape[0]
    slot_depth = max(1, items // groups)
    slots = groups * slot_depth
    bricks = levels.shape[0]
    bricks_group = bricks // groups
    bricks_dev = bricks_group // owners
    table_rows = -(-bricks * 8 // LANES)
    basis = block_data.shape[1]
    params = pltpu.CompilerParams(vmem_limit_bytes=32 * 1024 * 1024)

    outgoing = pl.pallas_call(
        functools.partial(pair_kernel, slot_depth, bricks_group),
        out_shape=jax.ShapeDtypeStruct((slots * SLOT_ROWS, LANES), jnp.float32),
        in_specs=[pl.BlockSpec(memory_space=pltpu.HBM)] * 7,
        out_specs=vmem(),
        scratch_shapes=[
            pltpu.SMEM((2, items), jnp.int32),
            pltpu.SMEM((items,), jnp.int32),
            pltpu.SMEM((items,), jnp.int32),
            pltpu.SMEM((bricks,), jnp.int32),
            pltpu.SMEM((items,), jnp.int32),
            pltpu.VMEM(block_data.shape, block_data.dtype),
            pltpu.VMEM((3, centres.shape[0], basis), jnp.float32),
            pltpu.VMEM(exponents.shape, jnp.float32),
            pltpu.VMEM((4, items, LANES), jnp.float32),
            pltpu.SemaphoreType.DMA((4,)),
            pltpu.SemaphoreType.DMA((3,)),
        ],
        compiler_params=params,
        name="pair_density",
    )(
        *(
            pltpu.with_memory_space_constraint(operand, pltpu.HBM)
            for operand in (
                item_pairs.T,
                dest_slot,
                brick_tag,
                levels,
                block_data,
                jnp.transpose(centres, (1, 0, 2)),
                exponents,
            )
        )
    )
    arrived = lax.all_to_all(
        outgoing.reshape(slots, 1, SLOT_ROWS * LANES),
        ("row", "col"),
        split_axis=0,
        concat_axis=0,
        tiled=True,
    ).reshape(outgoing.shape)
    rows, cols = lax.axis_size("row"), lax.axis_size("col")
    moves = moves_of(rows, owners)
    partial = pl.pallas_call(
        functools.partial(group_kernel, items, bricks_dev, moves),
        out_shape=[jax.ShapeDtypeStruct((bricks_dev * ROWS + table_rows, LANES), jnp.float32)]
        * (len(moves) + 1),
        in_specs=[vmem()],
        out_specs=[vmem()] * (len(moves) + 1),
        compiler_params=params,
        name="group_sum",
    )(arrived)
    parts = [partial[0]] + [
        lax.ppermute(piece, ("row", "col", "basis"), pairs_of(move, rows, cols))
        for piece, move in zip(partial[1:], moves)
    ]
    cell_map = pl.pallas_call(
        map_kernel,
        out_shape=jax.ShapeDtypeStruct((bricks_dev, ROWS, LANES), jnp.int32),
        in_specs=[vmem()],
        out_specs=vmem(),
        compiler_params=params,
        cost_estimate=pl.CostEstimate(flops=4_000_000, bytes_accessed=200_000, transcendentals=0),
        name="cell_map",
    )(cell_pos)
    return pl.pallas_call(
        cell_kernel,
        out_shape=jax.ShapeDtypeStruct((bricks_dev, EDGE * FACE), jnp.float32),
        in_specs=[vmem()] * (len(parts) + 2),
        out_specs=vmem(),
        compiler_params=params,
        name="cells",
    )(*parts, cell_map, jnp.transpose(corner_refs, (0, 2, 1)))


def solution(mesh):
    split = ("row", "col", "basis")
    return jax.shard_map(
        body,
        mesh=mesh,
        in_specs=(
            P(split, None, None),
            P(split, None),
            P(split),
            P(split),
            P(),
            P(),
            P(),
            P(split, None),
            P(split, None, None),
        ),
        out_specs=P(split, None),
        check_vma=False,
    )
```

```python
import functools

import jax
import jax.numpy as jnp
from jax import lax
from jax.experimental import pallas as pl
from jax.experimental.pallas import tpu as pltpu
from jax.sharding import PartitionSpec as P

EDGE = 16
FACE = EDGE * EDGE
LANES = 128
SHIFT = 7
ROWS = EDGE * FACE // LANES
COARSE = 0.2
SLOT_ROWS = ROWS + 1
TILE = 8


def lane_pick(values, index):
    return jnp.take_along_axis(values, index, axis=1, mode="promise_in_bounds")


def iota(shape, axis):
    return lax.broadcasted_iota(jnp.int32, shape, axis)


def fold(tiles):
    row = iota((TILE, LANES), 0)
    step = 1
    while len(tiles) > 1:
        odd = (row & step) != 0
        tiles = [
            jnp.where(odd, b, a)
            + jnp.where(odd, pltpu.roll(b, step, 0), pltpu.roll(a, TILE - step, 0))
            for a, b in zip(tiles[::2], tiles[1::2])
        ]
        step *= 2
    return tiles[0]


def axis_factors(coords, middle, decay):
    return jnp.exp(-decay * (coords - middle) ** 2)


def pair_kernel(
    slot_depth,
    bricks_group,
    pairs_hbm,
    dest_hbm,
    tag_hbm,
    levels_hbm,
    blocks_hbm,
    centres_hbm,
    exponents_hbm,
    out_ref,
    pairs_ref,
    dest_ref,
    tag_ref,
    levels_ref,
    order_ref,
    blocks_ref,
    centres_ref,
    exponents_ref,
    corner_buf,
    list_sems,
    table_sems,
):
    items = blocks_ref.shape[0]
    slots = out_ref.shape[0] // SLOT_ROWS
    lists = [
        pltpu.make_async_copy(source, target, list_sems.at[n])
        for n, (source, target) in enumerate(
            (
                (pairs_hbm, pairs_ref),
                (dest_hbm, dest_ref),
                (tag_hbm, tag_ref),
                (levels_hbm, levels_ref),
            )
        )
    ]
    tables = [
        pltpu.make_async_copy(centres_hbm, centres_ref, table_sems.at[0]),
        pltpu.make_async_copy(exponents_hbm, exponents_ref, table_sems.at[1]),
        pltpu.make_async_copy(blocks_hbm, blocks_ref, table_sems.at[2]),
    ]
    for copy in tables + lists:
        copy.start()
    for copy in lists + tables:
        copy.wait()
    if slots != items:
        out_ref[...] = jnp.zeros_like(out_ref)
    steps = iota((EDGE, LANES), 0).astype(jnp.float32) - (EDGE - 1) / 2.0

    if slots == items:
        for k in range(items):
            order_ref[dest_ref[k]] = k
        work = [(order_ref[slot], slot) for slot in range(slots)]
    else:
        work = [(k, dest_ref[k]) for k in range(items)]

    def prepare(k, slot):
        target = slot // slot_depth * bricks_group + tag_ref[k]
        spacing = jnp.where(levels_ref[target] == 1, COARSE * 0.5, COARSE)
        coords = steps * spacing

        def factors(side):
            row = pl.ds(pairs_ref[side, k], 1)
            decay = exponents_ref[row, :]
            found = [axis_factors(coords, centres_ref[d, row, :], decay) for d in range(3)]
            face = jnp.concatenate(
                [found[1][y : y + 1, :] * found[2] for y in range(EDGE)], axis=0
            )
            return found[0], face

        row_x, row_face = factors(0)
        return row_x, row_face.T, *factors(1), blocks_ref[k]

    def multiply(ready, x):
        _, _, col_x, col_face, block = ready
        col = (col_x[x : x + 1, :] * col_face).astype(jnp.bfloat16)
        return lax.dot_general(
            block, col, (((1,), (1,)), ((), ())), preferred_element_type=jnp.float32
        )

    def reduce(ready, x, product, sums):
        row_x, row_face = ready[:2]
        weight = jnp.broadcast_to(row_x[x : x + 1, :], (LANES, row_face.shape[0])).T
        weight = jnp.concatenate([weight] * (FACE // LANES), axis=1)
        parts = (weight * row_face * product).reshape(-1, TILE, FACE).sum(axis=0)
        sums.extend(parts[:, c : c + LANES] for c in range(0, FACE, LANES))

    def store(n, slot, x, sums):
        tile = fold(sums)
        sums.clear()
        first = 2 * (x + 1) - TILE
        out_ref[pl.ds(slot * SLOT_ROWS + first, TILE), :] = tile
        if first == 0:
            corner_buf[:2, n] = tile[:2]
        if first == ROWS - TILE:
            corner_buf[2:, n] = tile[TILE - 2 :]

    ahead, early = 1, 8
    flat = [(n, x) for n in range(items) for x in range(EDGE)]
    ready, products, sums = {0: prepare(*work[0])}, {}, []
    for at in range(-ahead, len(flat)):
        if at + ahead < len(flat):
            n, x = flat[at + ahead]
            products[n, x] = multiply(ready[n], x)
            if x == early and n + 1 < items:
                ready[n + 1] = prepare(*work[n + 1])
        if at >= 0:
            n, x = flat[at]
            reduce(ready[n], x, products.pop((n, x)), sums)
            if len(sums) == TILE:
                store(n, work[n][1], x, sums)

    shape = (items, LANES)
    lane = iota(shape, 1)
    place = lane % 4
    low = jnp.where(place % 2 == 1, EDGE - 1, 0)
    high = (FACE - EDGE) % LANES + low
    source = jnp.where(place >= 2, high, low)
    found = [lane_pick(corner_buf[n], source) for n in range(4)]
    corner = lane % 8
    first = jnp.where(corner % 4 >= 2, found[1], found[0])
    last = jnp.where(corner % 4 >= 2, found[3], found[2])
    values = jnp.where(corner >= 4, last, first)
    row = iota(shape, 0)
    brick = jnp.zeros(shape, jnp.int32)
    for n, (k, slot) in enumerate(work):
        target = slot // slot_depth * bricks_group + tag_ref[k]
        brick = jnp.where(row == n, target, brick)
    placed = jnp.where(lane // 8 == row, values, 0.0)
    placed = jnp.where(lane == 8 * items + row, brick.astype(jnp.float32), placed)
    meta = jnp.sum(placed, axis=0, keepdims=True)
    last_lane = iota((1, LANES), 1) == LANES - 1
    if slots != items:

        @pl.loop(0, slots)
        def _(n):
            out_ref[pl.ds(n * SLOT_ROWS + ROWS, 1), :] = jnp.where(last_lane, -1.0, meta)

    for k, slot in work:
        tagged = jnp.where(last_lane, tag_ref[k].astype(jnp.float32), meta)
        out_ref[pl.ds(slot * SLOT_ROWS + ROWS, 1), :] = tagged


def group_kernel(items, bricks_dev, moves, in_ref, *refs):
    *outs, sums_ref = refs
    me = lax.axis_index("basis")
    slots = in_ref.shape[0] // SLOT_ROWS
    meta = [in_ref[n * SLOT_ROWS + ROWS : (n + 1) * SLOT_ROWS, :] for n in range(slots)]
    tags = [jnp.broadcast_to(line[:, LANES - 1 :], (ROWS, LANES)) for line in meta]
    owners = len(moves[0])
    for brick in range(owners * bricks_dev):
        total = jnp.zeros((ROWS, LANES), jnp.float32)
        for n in range(slots):
            dens = in_ref[n * SLOT_ROWS : n * SLOT_ROWS + ROWS, :]
            total = total + jnp.where(tags[n] == float(brick), dens, 0.0)
        first = brick % bricks_dev * ROWS
        sums_ref[brick // bricks_dev, first : first + ROWS, :] = total
    sums_ref[owners] = jnp.zeros(sums_ref.shape[1:], jnp.float32)
    table_rows = outs[0].shape[0] - bricks_dev * ROWS
    shape = (TILE, LANES)
    lane = iota(shape, 1)
    lines = [jnp.zeros(shape, jnp.float32) for _ in range(table_rows)]
    for first in range(0, slots, TILE):
        block = jnp.concatenate(meta[first : first + TILE], axis=0)
        for k in range(items):
            values = lane_pick(block, 8 * k + (lane & 7))
            brick = lane_pick(block, jnp.full(shape, 8 * items + k, jnp.int32)).astype(jnp.int32)
            values = jnp.where((brick & 15) == lane >> 3, values, 0.0)
            for r in range(table_rows):
                lines[r] = lines[r] + jnp.where(brick >> 4 == r, values, 0.0)
    table = jnp.concatenate([jnp.sum(line, axis=0, keepdims=True) for line in lines], axis=0)
    for owner in range(owners):
        sums_ref[owner, bricks_dev * ROWS :, :] = table
    for out, move in zip(outs, [range(owners), *moves]):
        stays = out is not outs[0]
        to = sum(
            jnp.where(me == i, owners if stays and i == owner else owner, 0)
            for i, owner in enumerate(move)
        )
        out[...] = sums_ref[to]


def map_kernel(cells_ref, out_ref):
    bricks_dev, cells = cells_ref.shape
    cell = (iota((LANES, cells), 1) + 1).astype(jnp.float32)
    for b in range(bricks_dev):
        position = cells_ref[b : b + 1, :]
        high = position >> SHIFT == iota((ROWS, cells), 0)
        low = (position & (LANES - 1)) == iota((LANES, cells), 0)
        found = lax.dot_general(
            high.astype(jnp.float32).astype(jnp.bfloat16),
            jnp.where(low, cell, 0.0).astype(jnp.bfloat16),
            (((1,), (1,)), ((), ())),
            preferred_element_type=jnp.float32,
        )
        out_ref[b] = found.astype(jnp.int32) - 1


def cell_kernel(*refs):
    *ins, map_ref, refs_ref, out_ref = refs
    bricks_dev, _, cells = refs_ref.shape
    total = ins[0][...]
    for part in ins[1:]:
        total = total + part[...]
    table = total[bricks_dev * ROWS :]
    chunk = (TILE, LANES)
    tiles = cells // LANES
    refs = [
        [refs_ref[b, :, c * LANES : (c + 1) * LANES] for c in range(tiles)]
        for b in range(bricks_dev)
    ]
    picked = [[jnp.zeros(chunk, jnp.float32) for _ in row] for row in refs]
    for r in range(table.shape[0]):
        line = jnp.broadcast_to(table[r : r + 1, :], chunk)
        for b in range(bricks_dev):
            for c, index in enumerate(refs[b]):
                found = lane_pick(line, (index & (LANES - 1)))
                picked[b][c] = jnp.where(index >> SHIFT == r, found, picked[b][c])
    for b in range(bricks_dev):
        cell = map_ref[b]
        mean = jnp.zeros((ROWS, LANES), jnp.float32)
        for c in range(tiles):
            line = jnp.sum(picked[b][c], axis=0, keepdims=True) * (0.5 / 8.0)
            found = lane_pick(jnp.broadcast_to(line, (ROWS, LANES)), (cell & (LANES - 1)))
            mean = jnp.where(cell >> SHIFT == c, found, mean)
        own = total[b * ROWS : (b + 1) * ROWS]
        result = jnp.where(cell >= 0, 0.5 * own + mean, own)
        for row in range(ROWS):
            out_ref[b : b + 1, row * LANES : (row + 1) * LANES] = result[row : row + 1, :]


def moves_of(rows, owners):
    if owners == 4 and rows % 2 == 0:
        return [(1, 3, 2, 0), (2, 1, 0, 3), (3, 0, 1, 2), (0, 2, 3, 1)]
    return [tuple((i + d) % owners for i in range(owners)) for d in range(1, owners)]


def pairs_of(move, rows, cols):
    owners = len(move)
    pairs = []
    for row in range(rows):
        for col in range(cols):
            for z, to in enumerate(move):
                target = row ^ 1 if to == z else row
                source = (row * cols + col) * owners + z
                pairs.append((source, (target * cols + col) * owners + to))
    return pairs


def vmem():
    return pl.BlockSpec(memory_space=pltpu.VMEM)


def body(
    block_data, item_pairs, dest_slot, brick_tag, centres, exponents, levels, cell_pos, corner_refs
):
    groups = lax.axis_size("row") * lax.axis_size("col")
    owners = lax.axis_size("basis")
    items = block_data.shape[0]
    slot_depth = max(1, items // groups)
    slots = groups * slot_depth
    bricks = levels.shape[0]
    bricks_group = bricks // groups
    bricks_dev = bricks_group // owners
    table_rows = -(-bricks * 8 // LANES)
    basis = block_data.shape[1]
    params = pltpu.CompilerParams(vmem_limit_bytes=32 * 1024 * 1024)

    outgoing = pl.pallas_call(
        functools.partial(pair_kernel, slot_depth, bricks_group),
        out_shape=jax.ShapeDtypeStruct((slots * SLOT_ROWS, LANES), jnp.float32),
        in_specs=[pl.BlockSpec(memory_space=pltpu.HBM)] * 7,
        out_specs=vmem(),
        scratch_shapes=[
            pltpu.SMEM((2, items), jnp.int32),
            pltpu.SMEM((items,), jnp.int32),
            pltpu.SMEM((items,), jnp.int32),
            pltpu.SMEM((bricks,), jnp.int32),
            pltpu.SMEM((items,), jnp.int32),
            pltpu.VMEM(block_data.shape, block_data.dtype),
            pltpu.VMEM((3, centres.shape[0], basis), jnp.float32),
            pltpu.VMEM(exponents.shape, jnp.float32),
            pltpu.VMEM((4, items, LANES), jnp.float32),
            pltpu.SemaphoreType.DMA((4,)),
            pltpu.SemaphoreType.DMA((3,)),
        ],
        compiler_params=params,
        name="pair_density",
    )(
        *(
            pltpu.with_memory_space_constraint(operand, pltpu.HBM)
            for operand in (
                item_pairs.T,
                dest_slot,
                brick_tag,
                levels,
                block_data,
                jnp.transpose(centres, (1, 0, 2)),
                exponents,
            )
        )
    )
    arrived = lax.all_to_all(
        outgoing.reshape(slots, 1, SLOT_ROWS * LANES),
        ("row", "col"),
        split_axis=0,
        concat_axis=0,
        tiled=True,
    ).reshape(outgoing.shape)
    rows, cols = lax.axis_size("row"), lax.axis_size("col")
    moves = moves_of(rows, owners)
    partial = pl.pallas_call(
        functools.partial(group_kernel, items, bricks_dev, moves),
        out_shape=[jax.ShapeDtypeStruct((bricks_dev * ROWS + table_rows, LANES), jnp.float32)]
        * (len(moves) + 1),
        in_specs=[vmem()],
        out_specs=[vmem()] * (len(moves) + 1),
        scratch_shapes=[
            pltpu.VMEM((owners + 1, bricks_dev * ROWS + table_rows, LANES), jnp.float32)
        ],
        compiler_params=params,
        name="group_sum",
    )(arrived)
    parts = [partial[0]] + [
        lax.ppermute(piece, ("row", "col", "basis"), pairs_of(move, rows, cols))
        for piece, move in zip(partial[1:], moves)
    ]
    cell_map = pl.pallas_call(
        map_kernel,
        out_shape=jax.ShapeDtypeStruct((bricks_dev, ROWS, LANES), jnp.int32),
        in_specs=[vmem()],
        out_specs=vmem(),
        compiler_params=params,
        cost_estimate=pl.CostEstimate(flops=4_000_000, bytes_accessed=200_000, transcendentals=0),
        name="cell_map",
    )(cell_pos)
    return pl.pallas_call(
        cell_kernel,
        out_shape=jax.ShapeDtypeStruct((bricks_dev, EDGE * FACE), jnp.float32),
        in_specs=[vmem()] * (len(parts) + 2),
        out_specs=vmem(),
        compiler_params=params,
        name="cells",
    )(*parts, cell_map, jnp.transpose(corner_refs, (0, 2, 1)))


def solution(mesh):
    split = ("row", "col", "basis")
    return jax.shard_map(
        body,
        mesh=mesh,
        in_specs=(
            P(split, None, None),
            P(split, None),
            P(split),
            P(split),
            P(),
            P(),
            P(),
            P(split, None),
            P(split, None, None),
        ),
        out_specs=P(split, None),
        check_vma=False,
    )
```

```python
import functools

import jax
import jax.numpy as jnp
from jax import lax
from jax.experimental import pallas as pl
from jax.experimental.pallas import tpu as pltpu
from jax.sharding import PartitionSpec as P

EDGE = 16
FACE = EDGE * EDGE
LANES = 128
SHIFT = 7
ROWS = EDGE * FACE // LANES
COARSE = 0.2
SLOT_ROWS = ROWS + 1
TILE = 8


def lane_pick(values, index):
    return jnp.take_along_axis(values, index, axis=1, mode="promise_in_bounds")


def iota(shape, axis):
    return lax.broadcasted_iota(jnp.int32, shape, axis)


def fold(tiles):
    row = iota((TILE, LANES), 0)
    step = 1
    while len(tiles) > 1:
        odd = (row & step) != 0
        tiles = [
            jnp.where(odd, b, a)
            + jnp.where(odd, pltpu.roll(b, step, 0), pltpu.roll(a, TILE - step, 0))
            for a, b in zip(tiles[::2], tiles[1::2])
        ]
        step *= 2
    return tiles[0]


def axis_factors(coords, middle, decay):
    return jnp.exp(-decay * (coords - middle) ** 2)


def pair_kernel(
    slot_depth,
    bricks_group,
    pairs_hbm,
    dest_hbm,
    tag_hbm,
    levels_hbm,
    blocks_hbm,
    centres_hbm,
    exponents_hbm,
    out_ref,
    pairs_ref,
    dest_ref,
    tag_ref,
    levels_ref,
    order_ref,
    blocks_ref,
    centres_ref,
    exponents_ref,
    corner_buf,
    list_sems,
    table_sems,
):
    items = blocks_ref.shape[0]
    slots = out_ref.shape[0] // SLOT_ROWS
    lists = [
        pltpu.make_async_copy(source, target, list_sems.at[n])
        for n, (source, target) in enumerate(
            (
                (pairs_hbm, pairs_ref),
                (dest_hbm, dest_ref),
                (tag_hbm, tag_ref),
                (levels_hbm, levels_ref),
            )
        )
    ]
    tables = [
        pltpu.make_async_copy(centres_hbm, centres_ref, table_sems.at[0]),
        pltpu.make_async_copy(exponents_hbm, exponents_ref, table_sems.at[1]),
        pltpu.make_async_copy(blocks_hbm, blocks_ref, table_sems.at[2]),
    ]
    for copy in tables + lists:
        copy.start()
    for copy in lists + tables:
        copy.wait()
    if slots != items:
        out_ref[...] = jnp.zeros_like(out_ref)
    steps = iota((EDGE, LANES), 0).astype(jnp.float32) - (EDGE - 1) / 2.0

    if slots == items:
        for k in range(items):
            order_ref[dest_ref[k]] = k
        work = [(order_ref[slot], slot) for slot in range(slots)]
    else:
        work = [(k, dest_ref[k]) for k in range(items)]

    def prepare(k, slot):
        target = slot // slot_depth * bricks_group + tag_ref[k]
        spacing = jnp.where(levels_ref[target] == 1, COARSE * 0.5, COARSE)
        coords = steps * spacing

        def factors(side):
            row = pl.ds(pairs_ref[side, k], 1)
            decay = exponents_ref[row, :]
            found = [axis_factors(coords, centres_ref[d, row, :], decay) for d in range(3)]
            face = jnp.concatenate(
                [found[1][y : y + 1, :] * found[2] for y in range(EDGE)], axis=0
            )
            return found[0], face

        row_x, row_face = factors(0)
        return row_x, row_face.T, *factors(1), blocks_ref[k]

    def multiply(ready, x):
        _, _, col_x, col_face, block = ready
        col = (col_x[x : x + 1, :] * col_face).astype(jnp.bfloat16)
        return lax.dot_general(
            block, col, (((1,), (1,)), ((), ())), preferred_element_type=jnp.float32
        )

    def reduce(ready, x, product, sums):
        row_x, row_face = ready[:2]
        weight = jnp.broadcast_to(row_x[x : x + 1, :], (LANES, row_face.shape[0])).T
        weight = jnp.concatenate([weight] * (FACE // LANES), axis=1)
        parts = (weight * row_face * product).reshape(-1, TILE, FACE).sum(axis=0)
        sums.extend(parts[:, c : c + LANES] for c in range(0, FACE, LANES))

    def store(n, slot, x, sums):
        tile = fold(sums)
        sums.clear()
        first = 2 * (x + 1) - TILE
        out_ref[pl.ds(slot * SLOT_ROWS + first, TILE), :] = tile
        if first == 0:
            corner_buf[:2, n] = tile[:2]
        if first == ROWS - TILE:
            corner_buf[2:, n] = tile[TILE - 2 :]

    ahead, early = 1, 8
    flat = [(n, x) for n in range(items) for x in range(EDGE)]
    ready, products, sums = {0: prepare(*work[0])}, {}, []
    for at in range(-ahead, len(flat)):
        if at + ahead < len(flat):
            n, x = flat[at + ahead]
            products[n, x] = multiply(ready[n], x)
            if x == early and n + 1 < items:
                ready[n + 1] = prepare(*work[n + 1])
        if at >= 0:
            n, x = flat[at]
            reduce(ready[n], x, products.pop((n, x)), sums)
            if len(sums) == TILE:
                store(n, work[n][1], x, sums)

    shape = (items, LANES)
    lane = iota(shape, 1)
    place = lane % 4
    low = jnp.where(place % 2 == 1, EDGE - 1, 0)
    high = (FACE - EDGE) % LANES + low
    source = jnp.where(place >= 2, high, low)
    found = [lane_pick(corner_buf[n], source) for n in range(4)]
    corner = lane % 8
    first = jnp.where(corner % 4 >= 2, found[1], found[0])
    last = jnp.where(corner % 4 >= 2, found[3], found[2])
    values = jnp.where(corner >= 4, last, first)
    row = iota(shape, 0)
    brick = jnp.zeros(shape, jnp.int32)
    for n, (k, slot) in enumerate(work):
        target = slot // slot_depth * bricks_group + tag_ref[k]
        brick = jnp.where(row == n, target, brick)
    placed = jnp.where(lane // 8 == row, values, 0.0)
    placed = jnp.where(lane == 8 * items + row, brick.astype(jnp.float32), placed)
    meta = jnp.sum(placed, axis=0, keepdims=True)
    last_lane = iota((1, LANES), 1) == LANES - 1
    if slots != items:

        @pl.loop(0, slots)
        def _(n):
            out_ref[pl.ds(n * SLOT_ROWS + ROWS, 1), :] = jnp.where(last_lane, -1.0, meta)

    for k, slot in work:
        tagged = jnp.where(last_lane, tag_ref[k].astype(jnp.float32), meta)
        out_ref[pl.ds(slot * SLOT_ROWS + ROWS, 1), :] = tagged


def group_kernel(items, bricks_dev, moves, in_ref, *refs):
    *outs, sums_ref = refs
    me = lax.axis_index("basis")
    slots = in_ref.shape[0] // SLOT_ROWS
    meta = [in_ref[n * SLOT_ROWS + ROWS : (n + 1) * SLOT_ROWS, :] for n in range(slots)]
    tags = [jnp.broadcast_to(line[:, LANES - 1 :], (ROWS, LANES)) for line in meta]
    owners = len(moves[0])
    for brick in range(owners * bricks_dev):
        total = jnp.zeros((ROWS, LANES), jnp.float32)
        for n in range(slots):
            dens = in_ref[n * SLOT_ROWS : n * SLOT_ROWS + ROWS, :]
            total = total + jnp.where(tags[n] == float(brick), dens, 0.0)
        first = brick % bricks_dev * ROWS
        sums_ref[brick // bricks_dev, first : first + ROWS, :] = total
    sums_ref[owners] = jnp.zeros(sums_ref.shape[1:], jnp.float32)
    table_rows = outs[0].shape[0] - bricks_dev * ROWS
    shape = (TILE, LANES)
    lane = iota(shape, 1)
    lines = [jnp.zeros(shape, jnp.float32) for _ in range(table_rows)]
    for first in range(0, slots, TILE):
        block = jnp.concatenate(meta[first : first + TILE], axis=0)
        for k in range(items):
            values = lane_pick(block, 8 * k + (lane & 7))
            brick = lane_pick(block, jnp.full(shape, 8 * items + k, jnp.int32)).astype(jnp.int32)
            values = jnp.where((brick & 15) == lane >> 3, values, 0.0)
            for r in range(table_rows):
                lines[r] = lines[r] + jnp.where(brick >> 4 == r, values, 0.0)
    table = jnp.concatenate([jnp.sum(line, axis=0, keepdims=True) for line in lines], axis=0)
    for owner in range(owners):
        sums_ref[owner, bricks_dev * ROWS :, :] = table
    for out, move in zip(outs, [range(owners), *moves]):
        stays = out is not outs[0]
        to = sum(
            jnp.where(me == i, owners if stays and i == owner else owner, 0)
            for i, owner in enumerate(move)
        )
        out[...] = sums_ref[to]


def map_kernel(cells_ref, out_ref):
    bricks_dev, cells = cells_ref.shape
    cell = (iota((LANES, cells), 1) + 1).astype(jnp.float32)
    for b in range(bricks_dev):
        position = cells_ref[b : b + 1, :]
        high = position >> SHIFT == iota((ROWS, cells), 0)
        low = (position & (LANES - 1)) == iota((LANES, cells), 0)
        found = lax.dot_general(
            high.astype(jnp.float32).astype(jnp.bfloat16),
            jnp.where(low, cell, 0.0).astype(jnp.bfloat16),
            (((1,), (1,)), ((), ())),
            preferred_element_type=jnp.float32,
        )
        out_ref[b] = found.astype(jnp.int32) - 1


def cell_kernel(*refs):
    *ins, map_ref, refs_ref, out_hbm, out_ref, sems = refs
    bricks_dev, _, cells = refs_ref.shape
    total = ins[0][...]
    for part in ins[1:]:
        total = total + part[...]
    table = total[bricks_dev * ROWS :]
    chunk = (TILE, LANES)
    tiles = cells // LANES
    refs = [
        [refs_ref[b, :, c * LANES : (c + 1) * LANES] for c in range(tiles)]
        for b in range(bricks_dev)
    ]
    picked = [[jnp.zeros(chunk, jnp.float32) for _ in row] for row in refs]
    for r in range(table.shape[0]):
        line = jnp.broadcast_to(table[r : r + 1, :], chunk)
        for b in range(bricks_dev):
            for c, index in enumerate(refs[b]):
                found = lane_pick(line, (index & (LANES - 1)))
                picked[b][c] = jnp.where(index >> SHIFT == r, found, picked[b][c])
    results = []
    for b in range(bricks_dev):
        cell = map_ref[b]
        mean = jnp.zeros((ROWS, LANES), jnp.float32)
        for c in range(tiles):
            line = jnp.sum(picked[b][c], axis=0, keepdims=True) * (0.5 / 8.0)
            found = lane_pick(jnp.broadcast_to(line, (ROWS, LANES)), (cell & (LANES - 1)))
            mean = jnp.where(cell >> SHIFT == c, found, mean)
        own = total[b * ROWS : (b + 1) * ROWS]
        results.append(jnp.where(cell >= 0, 0.5 * own + mean, own))
    copies = []
    for part in range(2):
        span = ROWS // 2
        for b, result in enumerate(results):
            for row in range(part * span, (part + 1) * span):
                out_ref[b : b + 1, row * LANES : (row + 1) * LANES] = result[row : row + 1, :]
        lanes = pl.ds(part * span * LANES, span * LANES)
        copies.append(
            pltpu.make_async_copy(out_ref.at[:, lanes], out_hbm.at[:, lanes], sems.at[part])
        )
        copies[-1].start()
    for copy in copies:
        copy.wait()


def moves_of(rows, owners):
    if owners == 4 and rows % 2 == 0:
        return [(1, 3, 2, 0), (2, 1, 0, 3), (3, 0, 1, 2), (0, 2, 3, 1)]
    return [tuple((i + d) % owners for i in range(owners)) for d in range(1, owners)]


def pairs_of(move, rows, cols):
    owners = len(move)
    pairs = []
    for row in range(rows):
        for col in range(cols):
            for z, to in enumerate(move):
                target = row ^ 1 if to == z else row
                source = (row * cols + col) * owners + z
                pairs.append((source, (target * cols + col) * owners + to))
    return pairs


def vmem():
    return pl.BlockSpec(memory_space=pltpu.VMEM)


def body(
    block_data, item_pairs, dest_slot, brick_tag, centres, exponents, levels, cell_pos, corner_refs
):
    groups = lax.axis_size("row") * lax.axis_size("col")
    owners = lax.axis_size("basis")
    items = block_data.shape[0]
    slot_depth = max(1, items // groups)
    slots = groups * slot_depth
    bricks = levels.shape[0]
    bricks_group = bricks // groups
    bricks_dev = bricks_group // owners
    table_rows = -(-bricks * 8 // LANES)
    basis = block_data.shape[1]
    params = pltpu.CompilerParams(vmem_limit_bytes=32 * 1024 * 1024)

    outgoing = pl.pallas_call(
        functools.partial(pair_kernel, slot_depth, bricks_group),
        out_shape=jax.ShapeDtypeStruct((slots * SLOT_ROWS, LANES), jnp.float32),
        in_specs=[pl.BlockSpec(memory_space=pltpu.HBM)] * 7,
        out_specs=vmem(),
        scratch_shapes=[
            pltpu.SMEM((2, items), jnp.int32),
            pltpu.SMEM((items,), jnp.int32),
            pltpu.SMEM((items,), jnp.int32),
            pltpu.SMEM((bricks,), jnp.int32),
            pltpu.SMEM((items,), jnp.int32),
            pltpu.VMEM(block_data.shape, block_data.dtype),
            pltpu.VMEM((3, centres.shape[0], basis), jnp.float32),
            pltpu.VMEM(exponents.shape, jnp.float32),
            pltpu.VMEM((4, items, LANES), jnp.float32),
            pltpu.SemaphoreType.DMA((4,)),
            pltpu.SemaphoreType.DMA((3,)),
        ],
        compiler_params=params,
        name="pair_density",
    )(
        *(
            pltpu.with_memory_space_constraint(operand, pltpu.HBM)
            for operand in (
                item_pairs.T,
                dest_slot,
                brick_tag,
                levels,
                block_data,
                jnp.transpose(centres, (1, 0, 2)),
                exponents,
            )
        )
    )
    arrived = lax.all_to_all(
        outgoing.reshape(slots, 1, SLOT_ROWS * LANES),
        ("row", "col"),
        split_axis=0,
        concat_axis=0,
        tiled=True,
    ).reshape(outgoing.shape)
    rows, cols = lax.axis_size("row"), lax.axis_size("col")
    moves = moves_of(rows, owners)
    partial = pl.pallas_call(
        functools.partial(group_kernel, items, bricks_dev, moves),
        out_shape=[jax.ShapeDtypeStruct((bricks_dev * ROWS + table_rows, LANES), jnp.float32)]
        * (len(moves) + 1),
        in_specs=[vmem()],
        out_specs=[vmem()] * (len(moves) + 1),
        scratch_shapes=[
            pltpu.VMEM((owners + 1, bricks_dev * ROWS + table_rows, LANES), jnp.float32)
        ],
        compiler_params=params,
        name="group_sum",
    )(arrived)
    parts = [partial[0]] + [
        lax.ppermute(piece, ("row", "col", "basis"), pairs_of(move, rows, cols))
        for piece, move in zip(partial[1:], moves)
    ]
    cell_map = pl.pallas_call(
        map_kernel,
        out_shape=jax.ShapeDtypeStruct((bricks_dev, ROWS, LANES), jnp.int32),
        in_specs=[vmem()],
        out_specs=vmem(),
        compiler_params=params,
        cost_estimate=pl.CostEstimate(flops=4_000_000, bytes_accessed=200_000, transcendentals=0),
        name="cell_map",
    )(cell_pos)
    return pl.pallas_call(
        cell_kernel,
        out_shape=jax.ShapeDtypeStruct((bricks_dev, EDGE * FACE), jnp.float32),
        in_specs=[vmem()] * (len(parts) + 2),
        out_specs=pl.BlockSpec(memory_space=pltpu.HBM),
        scratch_shapes=[
            pltpu.VMEM((bricks_dev, EDGE * FACE), jnp.float32),
            pltpu.SemaphoreType.DMA((2,)),
        ],
        compiler_params=params,
        name="cells",
    )(*parts, cell_map, jnp.transpose(corner_refs, (0, 2, 1)))


def solution(mesh):
    split = ("row", "col", "basis")
    return jax.shard_map(
        body,
        mesh=mesh,
        in_specs=(
            P(split, None, None),
            P(split, None),
            P(split),
            P(split),
            P(),
            P(),
            P(),
            P(split, None),
            P(split, None, None),
        ),
        out_specs=P(split, None),
        check_vma=False,
    )
```
